32 devices in a mesh: img: 8 (over z, core), row: 4 (over y, x).
Axes of the slice: x: 2, y: 2, z: 4, core: 2. Of those that a mesh axis runs over, the one named last changes fastest.
Arguments:
- features: float32 [32, 1024, 256], P('img', 'row'), may hold values from -8 to 8
- partners: int32 [32, 2], replicated, may hold values from 0 to 31, as said below
- counts: int32 [32], replicated, may hold values from 256 to 1024, as said below
- shared_proj: bfloat16 [256, 256], replicated, may hold values from -0.375 to 0.375
- value_proj: bfloat16 [256, 256], replicated, may hold values from -0.375 to 0.375
- out_proj: bfloat16 [256, 256], replicated, may hold values from -0.375 to 0.375
- ffn_in: bfloat16 [512, 512], replicated, may hold values from -0.25 to 0.25
- ffn_in_bias: float32 [512], replicated, may hold values from -3 to 3
- norm_gain: float32 [512], replicated, may hold values from 0.1 to 1.9
- norm_bias: float32 [512], replicated, may hold values from -3 to 3
- ffn_out: bfloat16 [512, 256], replicated, may hold values from -0.25 to 0.25
- ffn_out_bias: float32 [256], replicated, may hold values from -3 to 3
Outputs:
- refined: float32 [32, 1024, 256], P('img', 'row')
The draws below stay inside these ranges and needn't reach their ends.
Inputs may be any that keep to these rules, and one draw needn't show every extreme that they name: Images form blocks of 4 consecutive ones around a cycle of blocks. Both partners of an image lie in a block at distance 1 or 2 from its own block in either direction around the cycle. Of the 8 partner entries of one block, at most 3 lie in any one of those four blocks, and in every block exactly 3 lie in one of them. Keypoint slots at positions counts[i] and beyond of image i are padding; counts may equal 1024.
All inputs are finite; a program needn't handle non-finite values.
Results may differ from the reference program's by a relative error of at most 0.004.
Values may be sent and summed in bfloat16 or wider, within the bound.
No kernel may reach another device: no remote copies, remote signals or barrier semaphores. Data moves between devices by JAX's collectives and lax.ppermute only.
A program may use at most 64 MiB of HBM per device.

```python
import jax
import jax.numpy as jnp
from jax import lax

D = 256
HEADS = 4
FFN = 512
KP = 1024
IMG_DEV = 4
CAP = 3
IMAGES = 32


def draw_partners(key, part):
    block_total = IMAGES // IMG_DEV
    edge_count = 2 * IMG_DEV

    def one_block(block_key, block_id):
        pick_key, rest_key, order_key, slot_key = jax.random.split(block_key, 4)
        full_offset = jax.random.randint(pick_key, (), 0, 4)
        remaining = (jnp.arange(3 * CAP, dtype=jnp.int32) // CAP + 1 + full_offset) % 4
        remaining = jax.random.permutation(rest_key, remaining)
        picks = jnp.concatenate([jnp.full((CAP,), full_offset, jnp.int32), remaining])[:edge_count]
        picks = jax.random.permutation(order_key, picks)
        offsets = jnp.array([1, -1, 2, -2], jnp.int32)[picks]
        target = (block_id + offsets) % block_total
        slot_idx = jax.random.randint(slot_key, (edge_count,), 0, IMG_DEV)
        return (target * IMG_DEV + slot_idx).reshape(IMG_DEV, 2)
    block_keys = jax.random.split(key, block_total)
    drawn = jax.vmap(one_block)(block_keys, jnp.arange(block_total, dtype=jnp.int32))
    return drawn.reshape(IMAGES, 2).astype(jnp.int32)


def draw_counts(key, part):
    drawn = jax.random.randint(key, (IMAGES,), KP // 4, KP + KP // 2)
    return jnp.minimum(drawn, KP).astype(jnp.int32)


def draw_features(key, part):
    draw_key = jax.random.fold_in(key, 0)
    return jnp.clip(jax.random.normal(draw_key, (IMAGES, KP, D)), -8.0, 8.0).astype(jnp.float32)


def normal_values(key, shape, scale, bound, held_as=jnp.bfloat16):
    values = scale * jax.random.normal(key, shape, jnp.float32)
    return jnp.clip(values, min=-bound, max=bound).astype(held_as)


def setup_inputs(seed: int = 0) -> dict:
    keys = jax.random.split(jax.random.key(seed), 13)
    return {
        "features": draw_features(jax.random.fold_in(keys[12], 71), 0),
        "partners": draw_partners(jax.random.fold_in(keys[12], 71), 0),
        "counts": draw_counts(jax.random.fold_in(keys[12], 71), 0),
        "shared_proj": normal_values(keys[3], (D, D), D ** -0.5, 0.375),
        "value_proj": normal_values(keys[4], (D, D), D ** -0.5, 0.375),
        "out_proj": normal_values(keys[5], (D, D), D ** -0.5, 0.375),
        "ffn_in": normal_values(keys[6], (FFN, FFN), FFN ** -0.5, 0.25),
        "ffn_in_bias": normal_values(keys[7], (FFN,), 0.5, 3.0, jnp.float32),
        "norm_gain": jnp.clip(1.0 + 0.18 * jax.random.normal(keys[8], (FFN,), jnp.float32), 0.1, 1.9),
        "norm_bias": normal_values(keys[9], (FFN,), 0.5, 3.0, jnp.float32),
        "ffn_out": normal_values(keys[10], (FFN, D), FFN ** -0.5, 0.25),
        "ffn_out_bias": normal_values(keys[11], (D,), 0.5, 3.0, jnp.float32),
    }


NEGATIVE = -1e+30

def masked_softmax(scores, allowed, axis_num):
    peak_value = lax.optimization_barrier(jnp.max(jnp.where(allowed, scores, NEGATIVE), axis=axis_num, keepdims=True))
    raised = jnp.where(allowed, jnp.exp(scores - peak_value), 0.0)
    return (raised / lax.optimization_barrier(jnp.sum(raised, axis=axis_num, keepdims=True))).astype(jnp.bfloat16)

def reference(features, partners, counts, shared_proj, value_proj, out_proj, ffn_in, ffn_in_bias, norm_gain, norm_bias, ffn_out, ffn_out_bias):
    head_dim = D // HEADS
    scale_factor = head_dim ** (-0.5)
    rounded = features.astype(jnp.bfloat16)
    flat_rows = rounded.reshape(IMAGES * KP, D)
    shared = jnp.dot(flat_rows, shared_proj, preferred_element_type=jnp.float32).astype(jnp.bfloat16).reshape(IMAGES, KP, HEADS, head_dim)
    values = jnp.dot(flat_rows, value_proj, preferred_element_type=jnp.float32).astype(jnp.bfloat16).reshape(IMAGES, KP, HEADS, head_dim)
    positions = jnp.arange(KP, dtype=jnp.int32)

    def one_edge(inboxes, edge_id):
        image_id = edge_id // 2
        partner = partners[image_id, edge_id % 2]
        query_side = lax.dynamic_index_in_dim(shared, image_id, 0, False).astype(jnp.float32)
        key_side = lax.dynamic_index_in_dim(shared, partner, 0, False).astype(jnp.float32)
        own_values = lax.dynamic_index_in_dim(values, image_id, 0, False).astype(jnp.float32)
        value_side = lax.dynamic_index_in_dim(values, partner, 0, False).astype(jnp.float32)
        scores = jnp.einsum('ahd,bhd->hab', query_side, key_side) * scale_factor
        row_weights = masked_softmax(scores, (positions < counts[partner])[None, None, :], 2)
        column_weights = masked_softmax(scores, (positions < counts[image_id])[None, :, None], 1)
        to_own = jnp.einsum('hab,bhd->ahd', row_weights.astype(jnp.float32), value_side).reshape(KP, D)
        to_partner = jnp.einsum('hab,ahd->bhd', column_weights.astype(jnp.float32), own_values).reshape(KP, D)
        inboxes = inboxes.at[image_id].add(to_own)
        inboxes = inboxes.at[partner].add(to_partner)
        return (inboxes, None)
    inbox, _ = lax.scan(one_edge, jnp.zeros((IMAGES, KP, D), jnp.float32), jnp.arange(IMAGES * 2, dtype=jnp.int32))
    degree = lax.optimization_barrier(jnp.sum((partners.reshape(1, -1) == jnp.arange(IMAGES, dtype=jnp.int32)[:, None]).astype(jnp.float32), axis=1))
    averaged = (inbox / (2.0 + degree)[:, None, None]).astype(jnp.bfloat16)
    projected = jnp.dot(averaged.reshape(IMAGES * KP, D), out_proj, preferred_element_type=jnp.float32).astype(jnp.bfloat16)
    joined = jnp.concatenate([flat_rows, projected], axis=1)
    hidden = jnp.dot(joined, ffn_in, preferred_element_type=jnp.float32) + ffn_in_bias
    center = lax.optimization_barrier(jnp.mean(hidden, axis=1, keepdims=True))
    spread = lax.optimization_barrier(jnp.mean((hidden - center) ** 2, axis=1, keepdims=True))
    normed = (hidden - center) * lax.rsqrt(spread + 1e-05) * norm_gain + norm_bias
    activated = jax.nn.gelu(normed, approximate=False).astype(jnp.bfloat16)
    update = jnp.dot(activated, ffn_out, preferred_element_type=jnp.float32) + ffn_out_bias
    return features + update.reshape(IMAGES, KP, D)
```

```python
import functools
import math

import jax
import jax.numpy as jnp
from jax import lax
from jax.experimental import pallas as pl
from jax.experimental.pallas import tpu as pltpu
from jax.sharding import PartitionSpec as P

HEADS = 4
PAIR = 128
LIMIT = 60.0
NEGATIVE = -1e30
VMEM = 40 * 2**20
NT = (((1,), (1,)), ((), ()))
F32 = jnp.float32
BF16 = jnp.bfloat16

UP, DN, SW, CROSS = range(4)


def permute(value, pairs):
    return lax.ppermute(value, "img", pairs)


def whole(memory=pltpu.VMEM):
    return pl.BlockSpec(memory_space=memory)


def kind_of(partner, me, per_dev, img_count):
    offset = lax.rem(lax.div(partner, per_dev) - me + img_count, img_count)
    odd = lax.rem(me, 2) == 1
    near = jnp.where(odd, offset == img_count - 1, offset == 1)
    kind = jnp.where(offset == img_count - 2, UP, jnp.where(offset == 2, DN, jnp.where(near, SW, CROSS)))
    return kind, lax.rem(partner, per_dev)


def pick_kernel(img_count, table, up, dn, sw, cross, out):
    edges, per_dev = out.shape[0], up.shape[0]
    me = table[0]
    for edge in range(edges):
        kind, image = kind_of(table[1 + edge], me, per_dev, img_count)
        for number, source in ((UP, up), (DN, dn), (SW, sw), (CROSS, cross)):

            @pl.when(kind == number)
            def _():
                out[edge] = source[image]


def attend_kernel(head_dim, limits, own, partner, shared_proj, value_proj, out,
                  own_shared, own_values, part_shared, part_values, own_norm, part_norm,
                  own_sum, weights, to_own, to_partner):
    devices, edges, row_count, _ = partner.shape
    keypoints = devices * row_count
    pairs = shared_proj.shape[1] // PAIR
    factor = head_dim ** (-0.5) * math.log2(math.e)
    chunk = 256
    lane_side = lax.broadcasted_iota(jnp.int32, (1, PAIR), 1) // head_dim
    sub_side = lax.broadcasted_iota(jnp.int32, (PAIR, 1), 0) // head_dim
    key_row = lax.broadcasted_iota(jnp.int32, (keypoints, 1), 0)
    key_lane = lax.broadcasted_iota(jnp.int32, (1, keypoints), 1)
    halves = (
        lax.broadcasted_iota(jnp.int32, (PAIR, PAIR), 0) // head_dim
        == lax.broadcasted_iota(jnp.int32, (PAIR, PAIR), 1) // head_dim
    ).astype(BF16)

    def project(rows, shared_ref, norm_ref, place):
        projected = jnp.dot(rows, shared_proj[...], preferred_element_type=F32).astype(BF16)
        for pair in range(pairs):
            tile = projected[:, pair * PAIR:(pair + 1) * PAIR]
            shared_ref[place + pair] = tile
            squares = jnp.dot(tile * tile, halves, preferred_element_type=F32)
            norm_ref[place + pair] = jnp.max(squares, axis=0, keepdims=True)

    own_rows = own[...].reshape(keypoints, own.shape[-1])
    project(own_rows, own_shared, own_norm, 0)
    turned = lax.dot_general(
        value_proj[...], own_rows, (((0,), (1,)), ((), ())), preferred_element_type=F32
    ).astype(BF16)
    for pair in range(pairs):
        own_values[pair] = turned[pair * PAIR:(pair + 1) * PAIR, :]
    for edge in range(edges):
        rows = partner[:, edge].reshape(keypoints, partner.shape[-1])
        project(rows, part_shared, part_norm, edge * pairs)
        projected = jnp.dot(rows, value_proj[...], preferred_element_type=F32).astype(BF16)
        for pair in range(pairs):
            part_values[edge * pairs + pair] = projected[:, pair * PAIR:(pair + 1) * PAIR]
    own_sum[...] = jnp.zeros_like(own_sum)
    one = jnp.ones((), BF16)
    zero = jnp.zeros((), BF16)

    def step(item, carry):
        edge, pair = item // pairs, item % pairs
        own_ok = key_lane < limits[0]
        partner_ok = key_row < limits[1 + edge]
        partner_ok_lane = key_lane < limits[1 + edge]

        def operands(side):
            keys = jnp.where(lane_side == side, part_shared[item], zero)
            values = jnp.where(partner_ok, jnp.where(lane_side == side, part_values[item], one), zero)
            flat = jnp.where(own_ok, jnp.where(sub_side == side, own_values[pair], one), zero)
            return keys, values, flat

        bound = jnp.max(own_norm[pair] * part_norm[item])
        small = bound < (LIMIT / head_dim ** (-0.5)) ** 2

        @pl.when(small)
        def _():
            for side in range(2):
                keys, values, flat = operands(side)
                for start in range(0, keypoints, chunk):
                    rows = slice(start, start + chunk)
                    scores = lax.dot_general(own_shared[pair, rows], keys, NT, preferred_element_type=F32)
                    raised = jnp.exp2(scores * factor).astype(BF16)
                    weights[side, rows] = raised
                    to_own[side, rows] = jnp.dot(raised, values, preferred_element_type=F32)
                to_partner[side] = jnp.dot(flat, weights[side], preferred_element_type=F32)

        @pl.when(jnp.logical_not(small))
        def _():
            for side in range(2):
                keys, values, flat = operands(side)

                def one_chunk(number, carry):
                    rows = pl.ds(pl.multiple_of(number * chunk, chunk), chunk)
                    scores = lax.dot_general(own_shared[pair, rows], keys, NT, preferred_element_type=F32)
                    peak = jnp.max(jnp.where(partner_ok_lane, scores, NEGATIVE), axis=1, keepdims=True)
                    raised = jnp.where(partner_ok_lane, jnp.exp2((scores - peak) * factor), 0.0)
                    to_own[side, rows] = jnp.dot(raised.astype(BF16), values, preferred_element_type=F32)
                    asked = jnp.where(lane_side == side, part_shared[item, rows], zero)
                    scores = lax.dot_general(asked, own_shared[pair], NT, preferred_element_type=F32)
                    peak = jnp.max(jnp.where(own_ok, scores, NEGATIVE), axis=1, keepdims=True)
                    raised = jnp.where(own_ok, jnp.exp2((scores - peak) * factor), 0.0)
                    to_partner[side, :, rows] = lax.dot_general(
                        flat, raised.astype(BF16), NT, preferred_element_type=F32
                    )
                    return carry

                lax.fori_loop(0, keypoints // chunk, one_chunk, 0)

        first = lane_side == 0
        total = jnp.where(first, to_own[1], to_own[0])
        own_sum[pair] += jnp.where(first, to_own[0], to_own[1]) / pltpu.roll(total, head_dim, 1)
        message = jnp.concatenate(
            [
                to_partner[0, :head_dim] / to_partner[0, head_dim:],
                to_partner[1, head_dim:] / to_partner[1, :head_dim],
            ],
            axis=0,
        )
        message = message.T.astype(BF16).reshape(devices, row_count, PAIR)
        columns = pl.ds(pl.multiple_of(pair * PAIR, PAIR), PAIR)
        for device in range(devices):
            out[device, 1 + edge, :, columns] = message[device]
        return carry

    lax.fori_loop(0, edges * pairs, step, 0)
    for pair in range(pairs):
        out[:, 0, :, pair * PAIR:(pair + 1) * PAIR] = (
            own_sum[pair].astype(BF16).reshape(devices, row_count, PAIR)
        )


def attend(limits, own, partner, shared_proj, value_proj, head_dim):
    devices, edges, row_count, width = partner.shape
    keypoints = devices * row_count
    columns = shared_proj.shape[1]
    pairs = columns // PAIR
    return pl.pallas_call(
        functools.partial(attend_kernel, head_dim),
        out_shape=jax.ShapeDtypeStruct((devices, 1 + edges, row_count, columns), BF16),
        in_specs=[whole(pltpu.SMEM)] + [whole()] * 4,
        out_specs=whole(),
        scratch_shapes=[
            pltpu.VMEM((pairs, keypoints, PAIR), BF16),
            pltpu.VMEM((pairs, PAIR, keypoints), BF16),
            pltpu.VMEM((edges * pairs, keypoints, PAIR), BF16),
            pltpu.VMEM((edges * pairs, keypoints, PAIR), BF16),
            pltpu.VMEM((pairs, 1, PAIR), F32),
            pltpu.VMEM((edges * pairs, 1, PAIR), F32),
            pltpu.VMEM((pairs, keypoints, PAIR), F32),
            pltpu.VMEM((2, keypoints, keypoints), BF16),
            pltpu.VMEM((2, keypoints, PAIR), F32),
            pltpu.VMEM((2, PAIR, keypoints), F32),
        ],
        compiler_params=pltpu.CompilerParams(vmem_limit_bytes=VMEM),
        cost_estimate=pl.CostEstimate(
            flops=edges * pairs * 2 * 3 * 2 * keypoints * keypoints * 256,
            bytes_accessed=4 * keypoints * width * (2 + 2 * edges),
            transcendentals=edges * pairs * 2 * keypoints * keypoints,
        ),
        name="attend",
    )(limits, own, partner, shared_proj, value_proj)


def add_messages(img_count, table, messages, totals, wanted):
    per_dev, slots = messages.shape[0], messages.shape[1] - 1
    me = table[0]
    for edge in range(per_dev * slots):
        kind, image = kind_of(table[1 + edge], me, per_dev, img_count)
        place = wanted(me, kind, image)

        @pl.when(place >= 0)
        def _():
            totals[place] += messages[edge // slots, 1 + edge % slots].astype(F32)


def early_kernel(img_count, table, messages, thin, near, totals):
    per_dev = messages.shape[0]
    totals[...] = jnp.zeros_like(totals)

    def wanted(me, kind, image):
        far = jnp.where(lax.rem(me, 2) == 1, DN, UP)
        return jnp.where(
            kind == far, image,
            jnp.where(kind == SW, per_dev + image, jnp.where(kind == CROSS, 2 * per_dev + image, -1)),
        )

    add_messages(img_count, table, messages, totals, wanted)
    thin[...] = totals[:per_dev].astype(BF16)
    near[...] = totals[per_dev:].astype(BF16)


def late_kernel(img_count, table, messages, received, thick, totals):
    per_dev = messages.shape[0]
    totals[...] = received[per_dev:].astype(F32)

    def wanted(me, kind, image):
        return jnp.where(kind == jnp.where(lax.rem(me, 2) == 1, UP, DN), image, -1)

    add_messages(img_count, table, messages, totals, wanted)
    thick[...] = totals[...].astype(BF16)


def refine_kernel(weight, features, messages, near, thin, thick, out_proj, ffn_in, ffn_in_bias,
                  norm_gain, norm_bias, ffn_out, ffn_out_bias, out):
    image = pl.program_id(0)
    width = features.shape[-1]
    inbox = (
        messages[0, 0].astype(F32) + near[0].astype(F32) + thin[0].astype(F32) + thick[0].astype(F32)
    )
    averaged = (inbox * weight[image]).astype(BF16)
    projected = jnp.dot(averaged, out_proj[...], preferred_element_type=F32).astype(BF16)
    source = features[0]
    hidden = (
        jnp.dot(source.astype(BF16), ffn_in[:width], preferred_element_type=F32)
        + jnp.dot(projected, ffn_in[width:], preferred_element_type=F32)
        + ffn_in_bias[...]
    )
    hidden = hidden - jnp.mean(hidden, axis=1, keepdims=True)
    spread = jnp.mean(hidden * hidden, axis=1, keepdims=True)
    normed = hidden * lax.rsqrt(spread + 1e-05) * norm_gain[...] + norm_bias[...]
    activated = (0.5 * normed * (1.0 + lax.erf(normed * (0.5**0.5)))).astype(BF16)
    out[0] = source + jnp.dot(activated, ffn_out[...], preferred_element_type=F32) + ffn_out_bias[...]


def per_device(features, partners, counts, shared_proj, value_proj, out_proj, ffn_in, ffn_in_bias,
               norm_gain, norm_bias, ffn_out, ffn_out_bias):
    img_count = lax.axis_size("img")
    row_devices = lax.axis_size("row")
    me = lax.axis_index("img")
    row_index = lax.axis_index("row")
    per_dev, row_count, width = features.shape
    head_dim = width // HEADS
    edge_count = 2 * per_dev
    everyone = range(img_count)
    forward = [(s, (s + 2) % img_count) for s in everyone]
    backward = [(s, (s - 2) % img_count) for s in everyone]
    swap = [(s, s ^ 1) for s in everyone]
    thin_pairs = [(s, (s + (2 if s % 2 else -2)) % img_count) for s in everyone]
    thick_pairs = [(s, (s + (-2 if s % 2 else 2)) % img_count) for s in everyone]

    repeats = row_devices // per_dev
    edges_here = 2 if repeats == 1 else 1
    groups = 1 if repeats == 1 else repeats // 2
    columns = width // groups

    rounded = features.astype(BF16)
    dn = permute(rounded, backward)
    up = permute(rounded, forward)
    sw = permute(rounded, swap)
    own = rounded if repeats == 1 else jnp.repeat(rounded, repeats, axis=0)
    own = lax.all_to_all(own, "row", split_axis=0, concat_axis=0, tiled=True)
    odd = me % 2 == 1
    cross = permute(jnp.where(odd, up, dn), swap)

    entries = lax.dynamic_slice_in_dim(partners, me * per_dev, per_dev, 0).reshape(-1)
    table = jnp.concatenate([me[None].astype(jnp.int32), entries])
    partner = pl.pallas_call(
        functools.partial(pick_kernel, img_count),
        out_shape=jax.ShapeDtypeStruct((edge_count, row_count, width), BF16),
        in_specs=[whole(pltpu.SMEM)] + [whole()] * 4,
        out_specs=whole(),
        compiler_params=pltpu.CompilerParams(vmem_limit_bytes=VMEM),
        name="pick",
    )(table, up, dn, sw, cross)
    if groups > 1:
        partner = jnp.repeat(partner, groups, axis=0)
    partner = lax.all_to_all(partner, "row", split_axis=0, concat_axis=0, tiled=True)
    partner = partner.reshape(row_devices, edges_here, row_count, width)

    first_edge = row_index * edges_here // groups
    limits = jnp.concatenate([
        lax.dynamic_slice_in_dim(counts, me * per_dev + first_edge // 2, 1, 0),
        counts[lax.dynamic_slice_in_dim(entries, first_edge, edges_here, 0)],
    ])
    if groups > 1:
        start = (row_index % groups) * columns
        shared_proj = lax.dynamic_slice_in_dim(shared_proj, start, columns, 1)
        value_proj = lax.dynamic_slice_in_dim(value_proj, start, columns, 1)
    messages = attend(limits, own, partner, shared_proj, value_proj, head_dim)
    messages = lax.all_to_all(messages, "row", split_axis=0, concat_axis=0, tiled=True)
    if groups > 1:
        split = messages.reshape(per_dev, 2, groups, 2, row_count, columns)
        split = split.transpose(0, 3, 1, 4, 2, 5).reshape(per_dev, 2, 2, row_count, width)
        summed = split[:, 0].astype(F32).sum(axis=1, keepdims=True).astype(BF16)
        messages = jnp.concatenate([summed, split[:, 1]], axis=1)

    block = jax.ShapeDtypeStruct((per_dev, row_count, width), BF16)
    thin, near = pl.pallas_call(
        functools.partial(early_kernel, img_count),
        out_shape=(block, jax.ShapeDtypeStruct((2 * per_dev, row_count, width), BF16)),
        in_specs=[whole(pltpu.SMEM), whole()],
        out_specs=(whole(), whole()),
        scratch_shapes=[pltpu.VMEM((3 * per_dev, row_count, width), F32)],
        compiler_params=pltpu.CompilerParams(vmem_limit_bytes=VMEM),
        name="early",
    )(table, messages)
    near = permute(near, swap)
    thin = permute(thin, thin_pairs)
    thick = pl.pallas_call(
        functools.partial(late_kernel, img_count),
        out_shape=block,
        in_specs=[whole(pltpu.SMEM), whole(), whole()],
        out_specs=whole(),
        scratch_shapes=[pltpu.VMEM((per_dev, row_count, width), F32)],
        compiler_params=pltpu.CompilerParams(vmem_limit_bytes=VMEM),
        name="late",
    )(table, messages, near)
    thick = permute(thick, thick_pairs)

    own_ids = me * per_dev + jnp.arange(per_dev, dtype=jnp.int32)
    degree = jnp.sum((partners.reshape(1, -1) == own_ids[:, None]).astype(F32), axis=1)
    weight = 1.0 / (2.0 + degree)
    per_image = pl.BlockSpec((1, row_count, width), lambda i: (i, 0, 0))
    return pl.pallas_call(
        refine_kernel,
        grid=(per_dev,),
        out_shape=jax.ShapeDtypeStruct(features.shape, F32),
        in_specs=[
            whole(pltpu.SMEM), per_image,
            pl.BlockSpec((1, 1, row_count, width), lambda i: (i, 0, 0, 0)),
            per_image, per_image, per_image,
        ] + [whole()] * 7,
        out_specs=per_image,
        compiler_params=pltpu.CompilerParams(vmem_limit_bytes=VMEM),
        name="refine",
    )(weight, features, messages, near, thin, thick, out_proj, ffn_in, ffn_in_bias[None],
      norm_gain[None], norm_bias[None], ffn_out, ffn_out_bias[None])


def solution(mesh):
    return jax.shard_map(
        per_device,
        mesh=mesh,
        in_specs=(P("img", "row", None), P(), P(), P(), P(), P(), P(), P(), P(), P(), P(), P()),
        out_specs=P("img", "row", None),
        check_vma=False,
    )
```

```python
import functools
import math

import jax
import jax.numpy as jnp
from jax import lax
from jax.experimental import pallas as pl
from jax.experimental.pallas import tpu as pltpu
from jax.sharding import PartitionSpec as P

HEADS = 4
CAP = 3
CHUNKS = 2
PAIR = 128
LIMIT = 60.0
NEGATIVE = -1e30
VMEM = 40 * 2**20
NT = (((1,), (1,)), ((), ()))
F32 = jnp.float32
BF16 = jnp.bfloat16

UP, DN, SW, CROSS = range(4)


def permute(value, pairs):
    return lax.ppermute(value, "img", pairs)


def exchange(value):
    return lax.all_to_all(value, "row", split_axis=0, concat_axis=0, tiled=True)


def whole(memory=pltpu.VMEM):
    return pl.BlockSpec(memory_space=memory)


def call(kernel, name, out_shape, arguments, scratch=(), flops=0, size=0, raised=0, **more):
    specs = [whole(pltpu.SMEM if a.ndim == 1 and a.dtype == jnp.int32 else pltpu.VMEM) for a in arguments]
    many = isinstance(out_shape, (tuple, list))
    return pl.pallas_call(
        kernel,
        out_shape=out_shape,
        in_specs=specs,
        out_specs=tuple(whole() for _ in out_shape) if many else whole(),
        scratch_shapes=list(scratch),
        compiler_params=pltpu.CompilerParams(vmem_limit_bytes=VMEM),
        cost_estimate=pl.CostEstimate(flops=flops, bytes_accessed=size, transcendentals=raised),
        name=name,
        **more,
    )(*arguments)


def kind_of(partner, block, per_dev, img_count):
    offset = lax.rem(lax.div(partner, per_dev) - block + img_count, img_count)
    odd = lax.rem(block, 2) == 1
    near = jnp.where(odd, offset == img_count - 1, offset == 1)
    return jnp.where(offset == img_count - 2, UP, jnp.where(offset == 2, DN, jnp.where(near, SW, CROSS)))


def work_of(row, row_devices, per_dev):
    repeats = row_devices // per_dev
    edges = 2 if repeats == 1 else 1
    groups = 1 if repeats == 1 else repeats // 2
    return edges, groups, lax.div(row * edges, groups)


def halves(head_dim, axis):
    return lax.broadcasted_iota(jnp.int32, (PAIR, 1) if axis == 0 else (1, PAIR), axis) // head_dim


def project_shared(rows, weight, shared_ref, norm_ref, place, head_dim):
    same_head = (halves(head_dim, 0) == halves(head_dim, 1)).astype(BF16)
    projected = jnp.dot(rows, weight, preferred_element_type=F32).astype(BF16)
    for pair in range(projected.shape[1] // PAIR):
        tile = projected[:, pair * PAIR:(pair + 1) * PAIR]
        shared_ref[place + pair] = tile
        squares = jnp.dot(tile * tile, same_head, preferred_element_type=F32)
        norm_ref[place + pair] = jnp.max(squares, axis=0, keepdims=True)


def prepare_kernel(head_dim, counts, own, shared_proj, value_proj, shared, flat, norm):
    devices, row_count, width = own.shape
    keypoints = devices * row_count
    per_dev = counts.shape[0] // lax.axis_size("img")
    first_edge = work_of(lax.axis_index("row"), devices, per_dev)[2]
    limit = counts[lax.axis_index("img") * per_dev + lax.div(first_edge, 2)]
    rows = own[...].reshape(keypoints, width)
    project_shared(rows, shared_proj[...], shared, norm, 0, head_dim)
    turned = lax.dot_general(
        value_proj[...], rows, (((0,), (1,)), ((), ())), preferred_element_type=F32
    ).astype(BF16)
    present = lax.broadcasted_iota(jnp.int32, (1, keypoints), 1) < limit
    for pair in range(shared_proj.shape[1] // PAIR):
        tile = turned[pair * PAIR:(pair + 1) * PAIR]
        for side in range(2):
            kept = jnp.where(halves(head_dim, 0) == side, tile, jnp.ones((), BF16))
            flat[2 * pair + side] = jnp.where(present, kept, jnp.zeros((), BF16))


def pick_kernel(chunk, partners, up, dn, sw, cross, _, out):
    edges, part, _ = out.shape
    per_dev = edges // 2
    img_count = lax.axis_size("img")
    me = lax.axis_index("img")
    for edge in range(edges):
        entry = partners[me * edges + edge]
        kind, image = kind_of(entry, me, per_dev, img_count), lax.rem(entry, per_dev)
        for number, source in ((UP, up), (DN, dn), (CROSS, cross)):

            @pl.when(kind == number)
            def _():
                out[edge] = source[image]

        @pl.when(kind == SW)
        def _():
            out[edge] = sw[image, chunk * part:(chunk + 1) * part]


def attend_kernel(head_dim, chunk, last, counts, partners, own_shared, own_flat, own_norm, partner,
                  shared_proj, value_proj, *refs):
    if last:
        (before, before_norm, carried, out, part_shared, part_values, part_norm, own_sum, weights,
         to_own, to_partner) = refs
    else:
        out, carry_out, part_norm, part_shared, part_values, weights, to_own, to_partner = refs
    devices, edges, part, width = partner.shape
    keys_here = devices * part
    keypoints = own_shared.shape[1]
    row_count = keypoints // devices
    pairs = shared_proj.shape[1] // PAIR
    factor = head_dim ** (-0.5) * math.log2(math.e)
    rows_once = 256
    img_count = lax.axis_size("img")
    me = lax.axis_index("img")
    per_dev = counts.shape[0] // img_count
    first_edge = work_of(lax.axis_index("row"), devices, per_dev)[2]
    own_limit = counts[me * per_dev + lax.div(first_edge, 2)]
    lane_side = halves(head_dim, 1)
    one = jnp.ones((), BF16)
    zero = jnp.zeros((), BF16)

    def position(axis, part_number):
        shape = (keys_here, 1) if axis == 0 else (1, keys_here)
        index = lax.broadcasted_iota(jnp.int32, shape, axis)
        return index // part * row_count + index % part + part_number * part

    for edge in range(edges):
        rows = partner[:, edge].reshape(keys_here, width)
        project_shared(rows, shared_proj[...], part_shared, part_norm, edge * pairs, head_dim)
        projected = jnp.dot(rows, value_proj[...], preferred_element_type=F32).astype(BF16)
        for pair in range(pairs):
            part_values[edge * pairs + pair] = projected[:, pair * PAIR:(pair + 1) * PAIR]
    if last:
        own_sum[...] = jnp.zeros_like(own_sum)

    def with_ones(side, values, limit, part_number):
        kept = jnp.where(lane_side == side, values, one)
        return jnp.where(position(0, part_number) < limit, kept, zero)

    def of_head(side, tile):
        return jnp.where(lane_side == side, tile, zero)

    def step(item, carry):
        edge, pair = item // pairs, item % pairs
        limit = counts[partners[me * 2 * per_dev + first_edge + edge]]
        largest = part_norm[item]
        if last:
            for other in range(before_norm.shape[0]):
                largest = jnp.maximum(largest, before_norm[other, item])
        small = jnp.max(own_norm[pair] * largest) < (LIMIT / head_dim ** (-0.5)) ** 2

        @pl.when(small)
        def _():
            for side in range(2):
                keys = of_head(side, part_shared[item])
                values = with_ones(side, part_values[item], limit, chunk)
                for start in range(0, keypoints, rows_once):
                    rows = slice(start, start + rows_once)
                    scores = lax.dot_general(own_shared[pair, rows], keys, NT, preferred_element_type=F32)
                    raised = jnp.exp2(scores * factor).astype(BF16)
                    weights[side, rows] = raised
                    to_own[side, rows] = jnp.dot(raised, values, preferred_element_type=F32)
                to_partner[side] = jnp.dot(
                    own_flat[2 * pair + side], weights[side], preferred_element_type=F32
                )
            numerator = jnp.where(lane_side == 0, to_own[0], to_own[1])
            total = jnp.where(lane_side == 0, to_own[1], to_own[0])
            if last:
                numerator += carried[item, 0]
                total += carried[item, 1]
                own_sum[pair] += numerator / pltpu.roll(total, head_dim, 1)
            else:
                carry_out[item, 0] = numerator
                carry_out[item, 1] = total

        @pl.when(jnp.logical_not(small))
        def _():
            present = lax.broadcasted_iota(jnp.int32, (1, keypoints), 1) < own_limit
            for side in range(2):

                def columns_once(number, carry):
                    rows = pl.ds(pl.multiple_of(number * PAIR, PAIR), PAIR)
                    asked = of_head(side, part_shared[item, rows])
                    scores = lax.dot_general(asked, own_shared[pair], NT, preferred_element_type=F32)
                    peak = jnp.max(jnp.where(present, scores, NEGATIVE), axis=1, keepdims=True)
                    raised = jnp.where(present, jnp.exp2((scores - peak) * factor), 0.0)
                    to_partner[side, :, rows] = lax.dot_general(
                        own_flat[2 * pair + side], raised.astype(BF16), NT, preferred_element_type=F32
                    )
                    return carry

                lax.fori_loop(0, keys_here // PAIR, columns_once, 0)
            if not last:
                return
            columns = pl.ds(pl.multiple_of(pair * PAIR, PAIR), PAIR)
            shared_parts, value_parts = [], []
            for other in range(before.shape[0]):
                rows = before[other, :, edge].reshape(keys_here, width)
                for weight, parts in ((shared_proj, shared_parts), (value_proj, value_parts)):
                    tile = jnp.dot(rows, weight[:, columns], preferred_element_type=F32)
                    parts.append(tile.astype(BF16))
            shared_parts.append(part_shared[item])
            value_parts.append(part_values[item])
            for side in range(2):

                def rows_step(number, carry):
                    rows = pl.ds(pl.multiple_of(number * rows_once, rows_once), rows_once)
                    peak = jnp.full((rows_once, 1), NEGATIVE, F32)
                    parts = []
                    for other, tile in enumerate(shared_parts):
                        scores = lax.dot_general(
                            own_shared[pair, rows], of_head(side, tile), NT, preferred_element_type=F32
                        )
                        scores = jnp.where(position(1, other) < limit, scores, NEGATIVE)
                        peak = jnp.maximum(peak, jnp.max(scores, axis=1, keepdims=True))
                        parts.append(scores)
                    total = jnp.zeros((rows_once, PAIR), F32)
                    for other, scores in enumerate(parts):
                        raised = jnp.exp2((scores - peak) * factor).astype(BF16)
                        values = with_ones(side, value_parts[other], limit, other)
                        total += jnp.dot(raised, values, preferred_element_type=F32)
                    to_own[side, rows] = total
                    return carry

                lax.fori_loop(0, keypoints // rows_once, rows_step, 0)
            total = jnp.where(lane_side == 0, to_own[1], to_own[0])
            own_sum[pair] += jnp.where(lane_side == 0, to_own[0], to_own[1]) / pltpu.roll(total, head_dim, 1)

        message = jnp.concatenate(
            [
                to_partner[0, :head_dim] / to_partner[0, head_dim:],
                to_partner[1, head_dim:] / to_partner[1, :head_dim],
            ],
            axis=0,
        )
        message = message.T.astype(BF16).reshape(devices, part, PAIR)
        columns = pl.ds(pl.multiple_of(pair * PAIR, PAIR), PAIR)
        for device in range(devices):
            out[device, pl.ds(pl.multiple_of(edge * part, part), part), columns] = message[device]
        return carry

    lax.fori_loop(0, edges * pairs, step, 0)
    if last:
        for pair in range(pairs):
            out[:, edges * part:, pair * PAIR:(pair + 1) * PAIR] = (
                own_sum[pair].astype(BF16).reshape(devices, row_count, PAIR)
            )


def attend(head_dim, chunk, counts, partners, own, partner, shared_proj, value_proj, earlier):
    own_shared, own_flat, own_norm = own
    devices, edges, part, width = partner.shape
    keypoints = own_shared.shape[1]
    keys_here = devices * part
    last = chunk == CHUNKS - 1
    columns = shared_proj.shape[1]
    pairs = columns // PAIR
    items = edges * pairs
    arguments = [counts, partners, own_shared, own_flat, own_norm, partner, shared_proj, value_proj]
    norm = jax.ShapeDtypeStruct((items, 1, PAIR), F32)
    carry = jax.ShapeDtypeStruct((items, 2, keypoints, PAIR), F32)
    scratch = [pltpu.VMEM((items, keys_here, PAIR), BF16)] * 2
    if last:
        arguments += earlier
        out_rows = edges * part + keypoints // devices
        outs = jax.ShapeDtypeStruct((devices, out_rows, columns), BF16)
        scratch += [pltpu.VMEM((items, 1, PAIR), F32), pltpu.VMEM((pairs, keypoints, PAIR), F32)]
    else:
        outs = (jax.ShapeDtypeStruct((devices, edges * part, columns), BF16), carry, norm)
    scratch += [
        pltpu.VMEM((2, keypoints, keys_here), BF16),
        pltpu.VMEM((2, keypoints, PAIR), F32),
        pltpu.VMEM((2, PAIR, keys_here), F32),
    ]
    return call(
        functools.partial(attend_kernel, head_dim, chunk, last), f"attend{chunk}", outs, arguments, scratch,
        flops=items * 2 * 3 * 2 * keypoints * keys_here * 256,
        size=2 * keypoints * width * (2 + 2 * edges),
        raised=items * 2 * keypoints * keys_here,
    )


def each_slot(partners, block, kind, per_dev, img_count, use):
    slot = jnp.zeros((), jnp.int32)
    for edge in range(2 * per_dev):
        entry = partners[block * 2 * per_dev + edge]
        hit = kind_of(entry, block, per_dev, img_count) == kind
        pl.when(hit)(functools.partial(use, edge, slot, lax.rem(entry, per_dev)))
        slot = slot + hit.astype(jnp.int32)


def route_kernel(partners, messages, *outs):
    per_dev = messages.shape[0]
    part = outs[0].shape[1]
    me, img_count = lax.axis_index("img"), lax.axis_size("img")
    for kind, out in enumerate(outs):

        def use(edge, slot, image):
            start = edge % 2 * part
            out[slot] = messages[edge // 2, start:start + part]

        each_slot(partners, me, kind, per_dev, img_count, use)


def refine_kernel(chunk, partners, everyone, features, messages, up, dn, sw, cross, out_proj, ffn_in,
                  ffn_in_bias, norm_gain, norm_bias, ffn_out, ffn_out_bias, *refs):
    out, inbox = refs[-2:]
    per_dev, part, width = inbox.shape
    me, img_count = lax.axis_index("img"), lax.axis_size("img")
    inbox[...] = messages[...].astype(F32)
    odd = lax.rem(me, 2) == 1
    sources = (me + 2, me - 2, me + jnp.where(odd, -1, 1), me + jnp.where(odd, 1, -1))
    for kind, (source, arrived) in enumerate(zip(sources, (up, dn, sw, cross))):

        def use(edge, slot, image):
            inbox[image] += arrived[slot].astype(F32)

        each_slot(partners, lax.rem(source + img_count, img_count), kind, per_dev, img_count, use)

    together = 2

    def some(number, carry):
        first = number * together
        averaged = []
        for image in range(together):
            asked = (everyone[...] == me * per_dev + first + image).astype(F32)
            degree = jnp.sum(asked, axis=1, keepdims=True)
            averaged.append((inbox[first + image] / (2.0 + degree)).astype(BF16))
        averaged = jnp.concatenate(averaged, axis=0)
        projected = jnp.dot(averaged, out_proj[...], preferred_element_type=F32).astype(BF16)
        source = features[pl.ds(first, together)].reshape(together * part, width)
        hidden = (
            jnp.dot(source.astype(BF16), ffn_in[:width], preferred_element_type=F32)
            + jnp.dot(projected, ffn_in[width:], preferred_element_type=F32)
            + ffn_in_bias[...]
        )
        hidden = hidden - jnp.mean(hidden, axis=1, keepdims=True)
        spread = jnp.mean(hidden * hidden, axis=1, keepdims=True)
        normed = hidden * lax.rsqrt(spread + 1e-05) * norm_gain[...] + norm_bias[...]
        activated = (0.5 * normed * (1.0 + lax.erf(normed * (0.5**0.5)))).astype(BF16)
        refined = source + jnp.dot(activated, ffn_out[...], preferred_element_type=F32) + ffn_out_bias[...]
        out[pl.ds(first, together)] = refined.reshape(together, part, width)
        return carry

    lax.fori_loop(0, per_dev // together, some, 0)


def refine(chunk, partners, features, messages, slots, parameters, done):
    per_dev, row_count, width = features.shape
    part = row_count // CHUNKS
    own_start = messages.shape[1] // part - CHUNKS
    rows = pl.BlockSpec((per_dev, part, width), lambda i: (0, chunk, 0))
    own = pl.BlockSpec((per_dev, part, width), lambda i: (0, own_start + chunk, 0))
    arguments = [partners, partners[None], features, messages, *slots, *parameters]
    specs = [whole(pltpu.SMEM), whole(), rows, own] + [whole()] * (len(slots) + len(parameters))
    aliases = {}
    if done is not None:
        aliases = {len(arguments): 0}
        arguments.append(done)
        specs.append(whole(pl.ANY))
    return pl.pallas_call(
        functools.partial(refine_kernel, chunk),
        grid=(1,),
        out_shape=jax.ShapeDtypeStruct(features.shape, F32),
        in_specs=specs,
        out_specs=rows,
        scratch_shapes=[pltpu.VMEM((per_dev, part, width), F32)],
        input_output_aliases=aliases,
        compiler_params=pltpu.CompilerParams(vmem_limit_bytes=VMEM),
        cost_estimate=pl.CostEstimate(flops=2 * 2**30, bytes_accessed=3 * 2**20, transcendentals=2**18),
        name=f"refine{chunk}",
    )(*arguments)


def per_device(features, partners, counts, shared_proj, value_proj, out_proj, ffn_in, ffn_in_bias,
               norm_gain, norm_bias, ffn_out, ffn_out_bias):
    img_count = lax.axis_size("img")
    row_devices = lax.axis_size("row")
    per_dev, row_count, width = features.shape
    head_dim = width // HEADS
    edge_count = 2 * per_dev
    part = row_count // CHUNKS
    keypoints = row_count * row_devices
    blocks = range(img_count)
    forward = [(s, (s + 2) % img_count) for s in blocks]
    backward = [(s, (s - 2) % img_count) for s in blocks]
    swap = [(s, s ^ 1) for s in blocks]
    across = [(s, (s + (1 if s % 2 else -1)) % img_count) for s in blocks]
    row = lax.axis_index("row")
    odd = lax.axis_index("img") % 2 == 1
    repeats = row_devices // per_dev
    edges_here, groups, _ = work_of(row, row_devices, per_dev)
    columns = width // groups
    partners = partners.reshape(-1)
    if groups > 1:
        start = (row % groups) * columns
        shared_proj = lax.dynamic_slice_in_dim(shared_proj, start, columns, 1)
        value_proj = lax.dynamic_slice_in_dim(value_proj, start, columns, 1)
    pairs = columns // PAIR

    far = []
    for chunk in range(CHUNKS):
        sent = features[:, chunk * part:(chunk + 1) * part].astype(BF16)
        far.append((permute(sent, forward), permute(sent, backward)))
    rounded = features.astype(BF16)
    sw = permute(rounded, swap)
    own = exchange(rounded if repeats == 1 else jnp.repeat(rounded, repeats, axis=0))
    own = call(
        functools.partial(prepare_kernel, head_dim), "prepare",
        (
            jax.ShapeDtypeStruct((pairs, keypoints, PAIR), BF16),
            jax.ShapeDtypeStruct((2 * pairs, PAIR, keypoints), BF16),
            jax.ShapeDtypeStruct((pairs, 1, PAIR), F32),
        ),
        [counts, own, shared_proj, value_proj], flops=2**31, size=2**21,
    )

    fetched, carried, sent_back, own_messages = [], [], [], None
    for chunk, (up, dn) in enumerate(far):
        cross = permute(jnp.where(odd, up, dn), swap)
        partner = call(
            functools.partial(pick_kernel, chunk), "pick",
            jax.ShapeDtypeStruct((edge_count, part, width), BF16),
            [partners, up, dn, sw, cross, own[2]], size=2**21,
        )
        if groups > 1:
            partner = jnp.repeat(partner, groups, axis=0)
        partner = exchange(partner).reshape(row_devices, edges_here, part, width)
        last = chunk == CHUNKS - 1
        earlier = []
        if last:
            befores, norms, sums = zip(*carried)
            earlier = [jnp.stack(befores), jnp.stack(norms), functools.reduce(jnp.add, sums)]
        result = attend(head_dim, chunk, counts, partners, own, partner, shared_proj, value_proj, earlier)
        if not last:
            carried.append((partner, result[2], result[1]))
            result = result[0]
        result = exchange(result)
        if groups > 1:
            split = result.reshape(per_dev, 2, groups, -1, columns)
            split = split.transpose(0, 1, 3, 2, 4).reshape(per_dev, 2, -1, width)
            back = split[:, :, :part].reshape(per_dev, 2 * part, width)
            summed = split[:, :, part:].astype(F32).sum(axis=1).astype(BF16)
            result = jnp.concatenate([back, summed], axis=1)
        slots = call(
            route_kernel, "route", (jax.ShapeDtypeStruct((CAP, part, width), BF16),) * 4,
            [partners, result], size=2**21,
        )
        sent_back.append([permute(s, p) for s, p in zip(slots, (backward, forward, swap, across))])

    parameters = (out_proj, ffn_in, ffn_in_bias[None], norm_gain[None], norm_bias[None], ffn_out,
                  ffn_out_bias[None])
    done = None
    for chunk, slots in enumerate(sent_back):
        done = refine(chunk, partners, features, result, slots, parameters, done)
    return done


def solution(mesh):
    return jax.shard_map(
        per_device,
        mesh=mesh,
        in_specs=(P("img", "row", None), P(), P(), P(), P(), P(), P(), P(), P(), P(), P(), P()),
        out_specs=P("img", "row", None),
        check_vma=False,
    )
```

```python
import functools
import math

import jax
import jax.numpy as jnp
from jax import lax
from jax.experimental import pallas as pl
from jax.experimental.pallas import tpu as pltpu
from jax.sharding import PartitionSpec as P

HEADS = 4
LEAST, MOST = 1e-25, 1e25
NEGATIVE = -1e30
VMEM = 56 * 2**20
NT = (((1,), (1,)), ((), ()))
F32 = jnp.float32
BF16 = jnp.bfloat16

COMPANION, THICK, THIN, CROSS = range(4)


def block_of(kind, me, img_count):
    odd = lax.rem(me, 2)
    ahead = 1 - 2 * odd
    step = {COMPANION: ahead, THICK: 2 * ahead, THIN: -2 * ahead, CROSS: -ahead}[kind]
    return lax.rem(me + step + img_count, img_count)


def whole(memory=pltpu.VMEM):
    return pl.BlockSpec(memory_space=memory)


def exchange(value):
    return lax.all_to_all(value, "row", split_axis=0, concat_axis=0, tiled=True)


def project_kernel(rows, weight, out):
    heads, _, width = out.shape
    for head in range(heads):
        part = weight[:, head * width:(head + 1) * width]
        out[head] = jnp.dot(rows[...], part, preferred_element_type=F32).astype(BF16)


def project(value, weight, row_devices):
    per_dev, row_count, width = value.shape
    rows = per_dev * row_count
    packed = pl.pallas_call(
        project_kernel,
        out_shape=jax.ShapeDtypeStruct((HEADS, rows, weight.shape[1] // HEADS), BF16),
        in_specs=[whole(), whole()],
        out_specs=whole(),
        compiler_params=pltpu.CompilerParams(vmem_limit_bytes=VMEM),
        cost_estimate=pl.CostEstimate(
            flops=2 * rows * weight.size, bytes_accessed=2 * rows * (width + weight.shape[1]), transcendentals=0
        ),
        name="project",
    )(value.reshape(rows, width), weight)
    if row_devices > HEADS:
        packed = jnp.repeat(packed, row_devices // HEADS, axis=0)
    return exchange(packed)


def attend_kernel(kinds, first, last, head_dim, counts, partners, own, *refs):
    blocks, refs = refs[:len(kinds)], refs[len(kinds):]
    if first:
        out, total, fine = refs
    else:
        carried, out, total, fine = refs
    devices, flat_rows, lanes = own.shape
    img_count = lax.axis_size("img")
    me = lax.axis_index("img")
    per_dev = counts.shape[0] // img_count
    row_count = flat_rows // per_dev
    keypoints = devices * row_count
    once = max(256, row_count)
    sources = once // row_count
    factor = head_dim ** (-0.5) * math.log2(math.e)
    lane_side = lax.broadcasted_iota(jnp.int32, (1, lanes), 1) // head_dim
    key_row = lax.broadcasted_iota(jnp.int32, (keypoints, 1), 0)
    key_lane = lax.broadcasted_iota(jnp.int32, (1, keypoints), 1)
    one, zero = jnp.ones((), BF16), jnp.zeros((), BF16)

    def rows_of(ref, image, start, count):
        rows = pl.ds(pl.multiple_of(image * row_count, row_count), row_count)
        return ref[start:start + count, rows, :].reshape(count * row_count, lanes)

    def begin():
        total[...] = jnp.zeros_like(total) if first else carried[...]

    def every_pair(body):
        for kind, block in zip(kinds, blocks):
            block_id = block_of(kind, me, img_count)

            def one_pair(number, carry):
                other, image = number // per_dev, number % per_dev
                theirs, mine = block_id * per_dev + other, me * per_dev + image
                times = jnp.zeros((), jnp.int32)
                for side in range(2):
                    times += (partners[2 * mine + side] == theirs).astype(jnp.int32)
                    times += (partners[2 * theirs + side] == mine).astype(jnp.int32)

                @pl.when(times > 0)
                def _():
                    tile = rows_of(block, other, 0, devices)
                    limit = counts[theirs]
                    side = image % 2
                    keys = jnp.where(lane_side == 0, tile, zero)
                    values = jnp.where(lane_side == 1, tile, pltpu.roll(tile, head_dim, 1))
                    values = jnp.where(lane_side == side, values, one)
                    values = jnp.where(key_row < limit, values, zero)
                    body(image, side, keys, values, limit, times.astype(F32))

                return carry

            lax.fori_loop(0, per_dev * per_dev, one_pair, 0)

    def add(image, side, start, got, times):
        message = got * times / pltpu.roll(got, head_dim, 1)
        rows = slice(start * row_count, start * row_count + once)
        total[image // 2, rows] += jnp.where(lane_side == side, message, 0.0)

    def fast(image, side, keys, values, limit, times):
        for start in range(0, devices, sources):
            queries = rows_of(own, image, start, sources)
            scores = lax.dot_general(queries, keys, NT, preferred_element_type=F32)
            raised = jnp.exp2(scores * factor).astype(BF16)
            got = jnp.dot(raised, values, preferred_element_type=F32)
            good = ((got > LEAST) & (got < MOST)) | (lane_side == side)
            good = jnp.where(good, 1.0, 0.0).reshape(once // 8, 8, lanes)
            fine[...] = jnp.minimum(fine[...], jnp.min(good, axis=0))
            add(image, side, start, got, times)

    def slow(image, side, keys, values, limit, times):
        for start in range(0, devices, sources):
            queries = rows_of(own, image, start, sources)
            scores = lax.dot_general(queries, keys, NT, preferred_element_type=F32)
            present = key_lane < limit
            peak = jnp.max(jnp.where(present, scores, NEGATIVE), axis=1, keepdims=True)
            raised = jnp.where(present, jnp.exp2((scores - peak) * factor), 0.0).astype(BF16)
            add(image, side, start, jnp.dot(raised, values, preferred_element_type=F32), times)

    begin()
    fine[...] = jnp.ones_like(fine)
    every_pair(fast)

    @pl.when(jnp.min(fine[...]) < 0.5)
    def _():
        begin()
        every_pair(slow)

    if last:
        for pair in range(per_dev // 2):
            out[:, pair * row_count:(pair + 1) * row_count] = (
                total[pair].astype(BF16).reshape(devices, row_count, lanes)
            )
    else:
        out[...] = total[...]


def attend(kinds, last, head_dim, counts, partners, own, blocks, carried):
    devices, flat_rows, lanes = own.shape
    per_dev = counts.shape[0] // lax.axis_size("img")
    keypoints = devices * flat_rows // per_dev
    sums = (per_dev // 2, keypoints, lanes)
    first = carried is None
    arguments = [counts, partners, own, *blocks] + ([] if first else [carried])
    if last:
        out_shape = jax.ShapeDtypeStruct((devices, flat_rows // 2, lanes), BF16)
    else:
        out_shape = jax.ShapeDtypeStruct(sums, F32)
    edges = 4 * len(kinds)
    return pl.pallas_call(
        functools.partial(attend_kernel, kinds, first, last, head_dim),
        out_shape=out_shape,
        in_specs=[whole(pltpu.SMEM)] * 2 + [whole()] * (len(arguments) - 2),
        out_specs=whole(),
        scratch_shapes=[pltpu.VMEM(sums, F32), pltpu.VMEM((8, lanes), F32)],
        compiler_params=pltpu.CompilerParams(vmem_limit_bytes=VMEM),
        cost_estimate=pl.CostEstimate(
            flops=edges * 2 * 2 * keypoints * keypoints * 256,
            bytes_accessed=2 * devices * flat_rows * lanes * (1 + len(kinds)) + 8 * keypoints * lanes,
            transcendentals=edges * keypoints * keypoints,
        ),
        name="attend_" + "_".join(str(kind) for kind in kinds),
    )(*arguments)


def refine_kernel(head_dim, everyone, features, messages, out_proj, ffn_in, ffn_in_bias, norm_gain,
                  norm_bias, ffn_out, ffn_out_bias, out):
    together, row_count, width = features.shape
    lanes = 2 * head_dim
    pair = pl.program_id(0)
    first_image = (lax.axis_index("img") * pl.num_programs(0) + pair) * together
    lane_side = lax.broadcasted_iota(jnp.int32, (1, lanes), 1) // head_dim
    tiles = [messages[head, 0].astype(F32) for head in range(HEADS)]
    turned = [pltpu.roll(tile, head_dim, 1) for tile in tiles]
    averaged = []
    for image in range(together):
        low, high = (tiles, turned) if image == 0 else (turned, tiles)
        inbox = jnp.concatenate(
            [jnp.where(lane_side == 0, low[head], high[head + 1]) for head in range(0, HEADS, 2)], axis=1
        )
        asked = (everyone[...] == first_image + image).astype(F32)
        degree = jnp.sum(asked, axis=1, keepdims=True)
        averaged.append((inbox / (2.0 + degree)).astype(BF16))
    averaged = jnp.concatenate(averaged, axis=0)
    projected = jnp.dot(averaged, out_proj[...], preferred_element_type=F32).astype(BF16)
    source = features[...].reshape(together * row_count, width)
    hidden = (
        jnp.dot(source.astype(BF16), ffn_in[:width], preferred_element_type=F32)
        + jnp.dot(projected, ffn_in[width:], preferred_element_type=F32)
        + ffn_in_bias[...]
    )
    hidden = hidden - jnp.mean(hidden, axis=1, keepdims=True)
    spread = jnp.mean(hidden * hidden, axis=1, keepdims=True)
    normed = hidden * lax.rsqrt(spread + 1e-05) * norm_gain[...] + norm_bias[...]
    activated = (0.5 * normed * (1.0 + lax.erf(normed * (0.5**0.5)))).astype(BF16)
    refined = source + jnp.dot(activated, ffn_out[...], preferred_element_type=F32) + ffn_out_bias[...]
    out[...] = refined.reshape(together, row_count, width)


def per_device(features, partners, counts, shared_proj, value_proj, out_proj, ffn_in, ffn_in_bias,
               norm_gain, norm_bias, ffn_out, ffn_out_bias):
    img_count = lax.axis_size("img")
    row_devices = lax.axis_size("row")
    per_dev, row_count, width = features.shape
    head_dim = width // HEADS
    blocks = range(img_count)
    swap = [(s, s ^ 1) for s in blocks]
    thick_pairs = [(s, (s + (2 if s % 2 else -2)) % img_count) for s in blocks]
    thin_pairs = [(s, (s + (-2 if s % 2 else 2)) % img_count) for s in blocks]

    rounded = features.astype(BF16)
    thick = lax.ppermute(rounded, "img", thick_pairs)
    thin = lax.ppermute(rounded, "img", thin_pairs)
    by_head = (width, HEADS, head_dim)
    weight = jnp.concatenate([shared_proj.reshape(by_head), value_proj.reshape(by_head)], axis=2)
    weight = weight.reshape(width, 2 * width)
    flat_partners = partners.reshape(-1)

    own = project(rounded, weight, row_devices)
    companion = lax.ppermute(own, "img", swap)
    thick = project(thick, weight, row_devices)
    cross = lax.ppermute(thick, "img", swap)
    thin = project(thin, weight, row_devices)

    sums = attend((COMPANION,), False, head_dim, counts, flat_partners, own, [companion], None)
    sums = attend((THICK,), False, head_dim, counts, flat_partners, own, [thick], sums)
    sums = attend((CROSS,), False, head_dim, counts, flat_partners, own, [cross], sums)
    messages = attend((THIN,), True, head_dim, counts, flat_partners, own, [thin], sums)
    messages = exchange(messages)[::row_devices // HEADS].reshape(HEADS, per_dev // 2, row_count, 2 * head_dim)

    pair = pl.BlockSpec((2, row_count, width), lambda i: (i, 0, 0))
    return pl.pallas_call(
        functools.partial(refine_kernel, head_dim),
        grid=(per_dev // 2,),
        out_shape=jax.ShapeDtypeStruct(features.shape, F32),
        in_specs=[
            whole(), pair, pl.BlockSpec((HEADS, 1, row_count, 2 * head_dim), lambda i: (0, i, 0, 0)),
        ] + [whole()] * 7,
        out_specs=pair,
        compiler_params=pltpu.CompilerParams(vmem_limit_bytes=VMEM),
        cost_estimate=pl.CostEstimate(
            flops=10 * per_dev * row_count * width * width * 2, bytes_accessed=2**22, transcendentals=2**20
        ),
        name="refine",
    )(flat_partners[None], features, messages, out_proj, ffn_in, ffn_in_bias[None], norm_gain[None],
      norm_bias[None], ffn_out, ffn_out_bias[None])


def solution(mesh):
    return jax.shard_map(
        per_device,
        mesh=mesh,
        in_specs=(P("img", "row", None), P(), P(), P(), P(), P(), P(), P(), P(), P(), P(), P()),
        out_specs=P("img", "row", None),
        check_vma=False,
    )
```

```python
import functools
import math

import jax
import jax.numpy as jnp
from jax import lax
from jax.experimental import pallas as pl
from jax.experimental.pallas import tpu as pltpu
from jax.sharding import PartitionSpec as P

HEADS = 4
LEAST, MOST = 1e-25, 1e25
NEGATIVE = -1e30
VMEM = 24 * 2**20
NT = (((1,), (1,)), ((), ()))
F32 = jnp.float32
BF16 = jnp.bfloat16

COMPANION, THICK, THIN, CROSS = range(4)


def block_of(kind, me, img_count):
    odd = lax.rem(me, 2)
    ahead = 1 - 2 * odd
    step = {COMPANION: ahead, THICK: 2 * ahead, THIN: -2 * ahead, CROSS: -ahead}[kind]
    return lax.rem(me + step + img_count, img_count)


def whole(memory=pltpu.VMEM):
    return pl.BlockSpec(memory_space=memory)


def exchange(value):
    return lax.all_to_all(value, "row", split_axis=0, concat_axis=0, tiled=True)


def project_kernel(head_dim, rows, shared_proj, value_proj, out):
    heads, _, lanes = out.shape
    scale = math.sqrt(head_dim ** (-0.5) * math.log2(math.e))
    low = lax.broadcasted_iota(jnp.int32, (1, lanes), 1) < head_dim
    for pair in range(heads // 2):
        columns = slice(pair * lanes, (pair + 1) * lanes)
        turned = pltpu.roll(value_proj[:, columns].astype(F32), head_dim, 1).astype(BF16)
        both = jnp.concatenate([shared_proj[:, columns], turned], axis=1)
        projected = jnp.dot(rows[...], both, preferred_element_type=F32)
        shared, values = projected[:, :lanes] * scale, projected[:, lanes:]
        out[2 * pair] = jnp.where(low, shared, values).astype(BF16)
        out[2 * pair + 1] = jnp.where(low, values, shared).astype(BF16)


def project(value, shared_proj, value_proj, row_devices, after=()):
    per_dev, row_count, width = value.shape
    rows = per_dev * row_count
    head_dim = width // HEADS

    def kernel(rows_ref, shared_ref, value_ref, *refs):
        project_kernel(head_dim, rows_ref, shared_ref, value_ref, refs[-1])

    packed = pl.pallas_call(
        kernel,
        out_shape=jax.ShapeDtypeStruct((HEADS, rows, 2 * head_dim), BF16),
        in_specs=[whole()] * 3 + [whole(pl.ANY)] * len(after),
        out_specs=whole(),
        compiler_params=pltpu.CompilerParams(vmem_limit_bytes=VMEM),
        cost_estimate=pl.CostEstimate(
            flops=4 * rows * width * width, bytes_accessed=6 * rows * width, transcendentals=0
        ),
        name="project",
    )(value.reshape(rows, width), shared_proj, value_proj, *after)
    if row_devices > HEADS:
        packed = jnp.repeat(packed, row_devices // HEADS, axis=0)
    return exchange(packed)


def attend_kernel(kind, first, last, head_dim, counts, partners, own, block, *refs):
    if first:
        out, total, limits, todo = refs
    else:
        carried, out, total, limits, todo = refs
    devices, flat_rows, lanes = own.shape
    img_count = lax.axis_size("img")
    me = lax.axis_index("img")
    per_dev = counts.shape[0] // img_count
    row_count = flat_rows // per_dev
    keypoints = devices * row_count
    once = max(256, row_count)
    sources = once // row_count
    block_id = block_of(kind, me, img_count)
    key_side = lax.rem(lax.div(lax.axis_index("row"), devices // HEADS), 2)
    lane_side = lax.broadcasted_iota(jnp.int32, (1, lanes), 1) // head_dim
    key_row = lax.broadcasted_iota(jnp.int32, (keypoints, 1), 0)
    key_lane = lax.broadcasted_iota(jnp.int32, (1, keypoints), 1)
    one, zero = jnp.ones((), BF16), jnp.zeros((), BF16)

    pairs = jnp.zeros((), jnp.int32)
    for other in range(per_dev):
        for image in range(per_dev):
            theirs, mine = block_id * per_dev + other, me * per_dev + image
            times = jnp.zeros((), jnp.int32)
            for side in range(2):
                times += (partners[2 * mine + side] == theirs).astype(jnp.int32)
                times += (partners[2 * theirs + side] == mine).astype(jnp.int32)
            todo[0, pairs] = other
            todo[1, pairs] = image
            todo[2, pairs] = times
            pairs = pairs + (times > 0).astype(jnp.int32)

    def rows_of(ref, image, start, count):
        rows = pl.ds(pl.multiple_of(image * row_count, row_count), row_count)
        return ref[start:start + count, rows, :].reshape(count * row_count, lanes)

    def begin():
        total[...] = jnp.zeros_like(total) if first else carried[...]

    def operands(number):
        other, image = todo[0, number], todo[1, number]
        limit = counts[block_id * per_dev + other]
        tile = rows_of(block, other, 0, devices)
        is_key, present = lane_side == key_side, key_row < limit
        keys = jnp.where(present, jnp.where(is_key, tile, zero), zero)
        values = jnp.where(present, jnp.where(is_key, one, tile), zero)
        return image, keys, values, limit, todo[2, number].astype(F32)

    def add(image, start, got, times):
        rows = slice(start * row_count, start * row_count + once)
        total[image, rows] += got * times / pltpu.roll(got, head_dim, 1)

    def fast(numbers):
        work = [operands(number) for number in numbers]
        least, most = limits[0], limits[1]
        for start in range(0, devices, sources):
            results = []
            for image, keys, values, _, times in work:
                queries = rows_of(own, image, start, sources)
                scores = lax.dot_general(queries, keys, NT, preferred_element_type=F32)
                raised = jnp.exp2(scores).astype(BF16)
                got = jnp.dot(raised, values, preferred_element_type=F32)
                by_row = got.reshape(once // 8, 8, lanes)
                least = jnp.minimum(least, jnp.min(by_row, axis=0))
                most = jnp.maximum(most, jnp.max(by_row, axis=0))
                results.append(got)
            for (image, _, _, _, times), got in zip(work, results):
                add(image, start, got, times)
        limits[0] = least
        limits[1] = most

    def slow(number, carry):
        image, keys, values, limit, times = operands(number)
        present = key_lane < limit
        for start in range(0, devices, sources):
            queries = rows_of(own, image, start, sources)
            scores = lax.dot_general(queries, keys, NT, preferred_element_type=F32)
            peak = jnp.max(jnp.where(present, scores, NEGATIVE), axis=1, keepdims=True)
            raised = jnp.where(present, jnp.exp2(scores - peak), 0.0).astype(BF16)
            add(image, start, jnp.dot(raised, values, preferred_element_type=F32), times)
        return carry

    def two(number, carry):
        fast((2 * number, 2 * number + 1))
        return carry

    begin()
    limits[...] = jnp.ones_like(limits)
    lax.fori_loop(0, pairs // 2, two, 0)

    @pl.when(pairs % 2 == 1)
    def _():
        fast((pairs - 1,))

    outside = (limits[0] < LEAST) | (limits[1] > MOST)
    outside = jnp.where((lane_side == key_side) & outside, 1.0, 0.0)

    @pl.when(jnp.max(outside) > 0.5)
    def _():
        begin()
        lax.fori_loop(0, pairs, slow, 0)

    if last:
        for pair in range(per_dev // 2):
            even, uneven = total[2 * pair], total[2 * pair + 1]
            even_low = jnp.where(key_side == 1, even, pltpu.roll(even, head_dim, 1))
            uneven_high = jnp.where(key_side == 0, uneven, pltpu.roll(uneven, head_dim, 1))
            both = jnp.where(lane_side == 0, even_low, uneven_high)
            out[:, pair * row_count:(pair + 1) * row_count] = (
                both.astype(BF16).reshape(devices, row_count, lanes)
            )
    else:
        out[...] = total[...]


def attend(kind, last, head_dim, counts, partners, own, block, carried):
    devices, flat_rows, lanes = own.shape
    per_dev = counts.shape[0] // lax.axis_size("img")
    keypoints = devices * flat_rows // per_dev
    sums = (per_dev, keypoints, lanes)
    first = carried is None
    arguments = [counts, partners, own, block] + ([] if first else [carried])
    if last:
        out_shape = jax.ShapeDtypeStruct((devices, flat_rows // 2, lanes), BF16)
    else:
        out_shape = jax.ShapeDtypeStruct(sums, F32)
    return pl.pallas_call(
        functools.partial(attend_kernel, kind, first, last, head_dim),
        out_shape=out_shape,
        in_specs=[whole(pltpu.SMEM)] * 2 + [whole()] * (len(arguments) - 2),
        out_specs=whole(),
        scratch_shapes=[
            pltpu.VMEM(sums, F32),
            pltpu.VMEM((2, 8, lanes), F32),
            pltpu.SMEM((3, per_dev * per_dev + 1), jnp.int32),
        ],
        compiler_params=pltpu.CompilerParams(vmem_limit_bytes=VMEM),
        cost_estimate=pl.CostEstimate(
            flops=4 * 2 * 2 * keypoints * keypoints * 256,
            bytes_accessed=4 * devices * flat_rows * lanes + 8 * keypoints * lanes,
            transcendentals=4 * keypoints * keypoints,
        ),
        name=f"attend{kind}",
    )(*arguments)


def refine_kernel(head_dim, everyone, features, messages, out_proj, ffn_in, ffn_in_bias, norm_gain,
                  norm_bias, ffn_out, ffn_out_bias, out):
    together, row_count, width = features.shape
    lanes = 2 * head_dim
    pair = pl.program_id(0)
    first_image = (lax.axis_index("img") * pl.num_programs(0) + pair) * together
    lane_side = lax.broadcasted_iota(jnp.int32, (1, lanes), 1) // head_dim
    tiles = [messages[head, 0].astype(F32) for head in range(HEADS)]
    turned = [pltpu.roll(tile, head_dim, 1) for tile in tiles]
    averaged = []
    for image in range(together):
        low, high = (tiles, turned) if image == 0 else (turned, tiles)
        inbox = jnp.concatenate(
            [jnp.where(lane_side == 0, low[head], high[head + 1]) for head in range(0, HEADS, 2)], axis=1
        )
        asked = (everyone[...] == first_image + image).astype(F32)
        degree = jnp.sum(asked, axis=1, keepdims=True)
        averaged.append((inbox / (2.0 + degree)).astype(BF16))
    averaged = jnp.concatenate(averaged, axis=0)
    projected = jnp.dot(averaged, out_proj[...], preferred_element_type=F32).astype(BF16)
    source = features[...].reshape(together * row_count, width)
    hidden = (
        jnp.dot(source.astype(BF16), ffn_in[:width], preferred_element_type=F32)
        + jnp.dot(projected, ffn_in[width:], preferred_element_type=F32)
        + ffn_in_bias[...]
    )
    hidden = hidden - jnp.mean(hidden, axis=1, keepdims=True)
    spread = jnp.mean(hidden * hidden, axis=1, keepdims=True)
    normed = hidden * lax.rsqrt(spread + 1e-05) * norm_gain[...] + norm_bias[...]
    activated = (0.5 * normed * (1.0 + lax.erf(normed * (0.5**0.5)))).astype(BF16)
    refined = source + jnp.dot(activated, ffn_out[...], preferred_element_type=F32) + ffn_out_bias[...]
    out[...] = refined.reshape(together, row_count, width)


def per_device(features, partners, counts, shared_proj, value_proj, out_proj, ffn_in, ffn_in_bias,
               norm_gain, norm_bias, ffn_out, ffn_out_bias):
    img_count = lax.axis_size("img")
    row_devices = lax.axis_size("row")
    per_dev, row_count, width = features.shape
    head_dim = width // HEADS
    blocks = range(img_count)
    swap = [(s, s ^ 1) for s in blocks]
    thick_pairs = [(s, (s + (2 if s % 2 else -2)) % img_count) for s in blocks]
    thin_pairs = [(s, (s + (-2 if s % 2 else 2)) % img_count) for s in blocks]

    rounded = features.astype(BF16)
    thick = lax.ppermute(rounded, "img", thick_pairs)
    thin = lax.ppermute(rounded, "img", thin_pairs)
    flat_partners = partners.reshape(-1)

    weights = (shared_proj, value_proj, row_devices)
    own = project(rounded, *weights)
    companion = lax.ppermute(own, "img", swap)
    thick = project(thick, *weights)
    cross = lax.ppermute(thick, "img", swap)
    sums = attend(COMPANION, False, head_dim, counts, flat_partners, own, companion, None)
    thin = project(thin, *weights, after=(sums,))
    sums = attend(THICK, False, head_dim, counts, flat_partners, own, thick, sums)
    sums = attend(CROSS, False, head_dim, counts, flat_partners, own, cross, sums)
    messages = attend(THIN, True, head_dim, counts, flat_partners, own, thin, sums)
    messages = exchange(messages)[::row_devices // HEADS].reshape(HEADS, per_dev // 2, row_count, 2 * head_dim)

    pair = pl.BlockSpec((2, row_count, width), lambda i: (i, 0, 0))
    return pl.pallas_call(
        functools.partial(refine_kernel, head_dim),
        grid=(per_dev // 2,),
        out_shape=jax.ShapeDtypeStruct(features.shape, F32),
        in_specs=[
            whole(), pair, pl.BlockSpec((HEADS, 1, row_count, 2 * head_dim), lambda i: (0, i, 0, 0)),
        ] + [whole()] * 7,
        out_specs=pair,
        compiler_params=pltpu.CompilerParams(vmem_limit_bytes=VMEM),
        cost_estimate=pl.CostEstimate(
            flops=10 * per_dev * row_count * width * width * 2, bytes_accessed=2**22, transcendentals=2**20
        ),
        name="refine",
    )(flat_partners[None], features, messages, out_proj, ffn_in, ffn_in_bias[None], norm_gain[None],
      norm_bias[None], ffn_out, ffn_out_bias[None])


def solution(mesh):
    return jax.shard_map(
        per_device,
        mesh=mesh,
        in_specs=(P("img", "row", None), P(), P(), P(), P(), P(), P(), P(), P(), P(), P(), P()),
        out_specs=P("img", "row", None),
        check_vma=False,
    )
```

```python
import functools
import math

import jax
import jax.numpy as jnp
from jax import lax
from jax.experimental import pallas as pl
from jax.experimental.pallas import tpu as pltpu
from jax.sharding import PartitionSpec as P

HEADS = 4
LEAST, MOST = 1e-25, 1e25
NEGATIVE = -1e30
VMEM = 60 * 2**20
NT = (((1,), (1,)), ((), ()))
F32 = jnp.float32
BF16 = jnp.bfloat16

COMPANION, THICK, THIN, CROSS = range(4)


def block_of(kind, me, img_count):
    odd = lax.rem(me, 2)
    ahead = 1 - 2 * odd
    step = {COMPANION: ahead, THICK: 2 * ahead, THIN: -2 * ahead, CROSS: -ahead}[kind]
    return lax.rem(me + step + img_count, img_count)


def whole(memory=pltpu.VMEM):
    return pl.BlockSpec(memory_space=memory)


def exchange(value):
    return lax.all_to_all(value, "row", split_axis=0, concat_axis=0, tiled=True)


def project_kernel(head_dim, rows, shared_proj, value_proj, out):
    heads, _, lanes = out.shape
    low = lax.broadcasted_iota(jnp.int32, (1, lanes), 1) < head_dim
    for pair in range(heads // 2):
        columns = slice(pair * lanes, (pair + 1) * lanes)
        turned = pltpu.roll(value_proj[:, columns].astype(F32), head_dim, 1).astype(BF16)
        both = jnp.concatenate([shared_proj[:, columns], turned], axis=1)
        projected = jnp.dot(rows[...], both, preferred_element_type=F32)
        shared, values = projected[:, :lanes], projected[:, lanes:]
        out[2 * pair] = jnp.where(low, shared, values).astype(BF16)
        out[2 * pair + 1] = jnp.where(low, values, shared).astype(BF16)


def project(value, shared_proj, value_proj, row_devices, after=(), weigh=1):
    per_dev, row_count, width = value.shape
    rows = per_dev * row_count
    head_dim = width // HEADS

    def kernel(rows_ref, shared_ref, value_ref, *refs):
        project_kernel(head_dim, rows_ref, shared_ref, value_ref, refs[-1])

    packed = pl.pallas_call(
        kernel,
        out_shape=jax.ShapeDtypeStruct((HEADS, rows, 2 * head_dim), BF16),
        in_specs=[whole()] * 3 + [whole(pl.ANY)] * len(after),
        out_specs=whole(),
        compiler_params=pltpu.CompilerParams(vmem_limit_bytes=VMEM),
        cost_estimate=pl.CostEstimate(
            flops=weigh * 4 * rows * width * width, bytes_accessed=6 * rows * width, transcendentals=0
        ),
        name="project",
    )(value.reshape(rows, width), shared_proj, value_proj, *after)
    if row_devices > HEADS:
        packed = jnp.repeat(packed, row_devices // HEADS, axis=0)
    return exchange(packed)


def tie(value, after):
    def kernel(value_ref, after_ref, out_ref):
        pass

    return pl.pallas_call(
        kernel,
        out_shape=jax.ShapeDtypeStruct(value.shape, value.dtype),
        in_specs=[whole(pltpu.HBM)] * 2,
        out_specs=whole(pltpu.HBM),
        input_output_aliases={0: 0},
        name="tie",
    )(value, after)


def attend_kernel(kinds, first, last, head_dim, counts, partners, own_hbm, *refs):
    blocks_hbm, refs = refs[:len(kinds)], refs[len(kinds):]
    if first:
        out_hbm, own, blocks, total, limits, todo, arrived, out, left = refs
    else:
        carried_hbm, out_hbm, own, blocks, total, limits, todo, arrived, out, left, carried, carried_here = refs
    devices, flat_rows, lanes = own.shape
    img_count = lax.axis_size("img")
    me = lax.axis_index("img")
    per_dev = counts.shape[0] // img_count
    row_count = flat_rows // per_dev
    keypoints = devices * row_count
    once = max(256, row_count)
    sources = once // row_count
    factor = head_dim ** (-0.5) * math.log2(math.e)

    copies = []
    for number, (source, target) in enumerate(
        [(own_hbm, own)] + [(block, blocks.at[place]) for place, block in enumerate(blocks_hbm)]
    ):
        for device in range(devices):
            copies.append(
                pltpu.make_async_copy(source.at[device], target.at[device], arrived.at[number, device])
            )
    for copy in copies:
        copy.start()
    if not first:
        carry_copy = pltpu.make_async_copy(carried_hbm, carried, carried_here)
        carry_copy.start()

    key_side = lax.rem(lax.div(lax.axis_index("row"), devices // HEADS), 2)
    lane_side = lax.broadcasted_iota(jnp.int32, (1, lanes), 1) // head_dim
    key_row = lax.broadcasted_iota(jnp.int32, (keypoints, 1), 0)
    key_lane = lax.broadcasted_iota(jnp.int32, (1, keypoints), 1)
    one, zero = jnp.ones((), BF16), jnp.zeros((), BF16)
    total[...] = jnp.zeros_like(total)
    limits[...] = jnp.ones_like(limits)

    pairs = jnp.zeros((), jnp.int32)
    for place, kind in enumerate(kinds):
        block_id = block_of(kind, me, img_count)
        for other in range(per_dev):
            for image in range(per_dev):
                theirs, mine = block_id * per_dev + other, me * per_dev + image
                times = jnp.zeros((), jnp.int32)
                for side in range(2):
                    times += (partners[2 * mine + side] == theirs).astype(jnp.int32)
                    times += (partners[2 * theirs + side] == mine).astype(jnp.int32)
                todo[0, pairs] = place * per_dev + other
                todo[1, pairs] = image
                todo[2, pairs] = times
                todo[3, pairs] = counts[theirs]
                pairs = pairs + (times > 0).astype(jnp.int32)
    for copy in copies:
        copy.wait()

    def image_rows(image):
        return pl.ds(pl.multiple_of(image * row_count, row_count), row_count)

    def operands(number):
        other, image, limit = todo[0, number], todo[1, number], todo[3, number]
        place, other = lax.div(other, per_dev), lax.rem(other, per_dev)
        tile = blocks[place, :, image_rows(other), :].reshape(keypoints, lanes)
        is_key, present = lane_side == key_side, key_row < limit
        keys = jnp.where(present, jnp.where(is_key, tile, zero), zero)
        values = jnp.where(present, jnp.where(is_key, one, tile), zero)
        return image, keys, values, limit, todo[2, number].astype(F32)

    def score(image, start, keys):
        queries = own[start:start + sources, image_rows(image), :].reshape(once, lanes)
        return lax.dot_general(queries, keys, NT, preferred_element_type=F32)

    def add(image, start, got, times):
        rows = slice(start * row_count, start * row_count + once)
        total[image, rows] += got * times / pltpu.roll(got, head_dim, 1)

    def fast(numbers):
        work = [operands(number) for number in numbers]
        least, most = limits[0], limits[1]
        for start in range(0, devices, sources):
            results = []
            for image, keys, values, _, times in work:
                raised = jnp.exp2(score(image, start, keys) * factor).astype(BF16)
                got = jnp.dot(raised, values, preferred_element_type=F32)
                by_row = got.reshape(once // 8, 8, lanes)
                least = jnp.minimum(least, jnp.min(by_row, axis=0))
                most = jnp.maximum(most, jnp.max(by_row, axis=0))
                results.append(got)
            for (image, _, _, _, times), got in zip(work, results):
                add(image, start, got, times)
        limits[0] = least
        limits[1] = most

    def slow(number, carry):
        image, keys, values, limit, times = operands(number)
        present = key_lane < limit
        for start in range(0, devices, sources):
            scores = score(image, start, keys)
            peak = jnp.max(jnp.where(present, scores, NEGATIVE), axis=1, keepdims=True)
            raised = jnp.where(present, jnp.exp2((scores - peak) * factor), 0.0).astype(BF16)
            add(image, start, jnp.dot(raised, values, preferred_element_type=F32), times)
        return carry

    def two(number, carry):
        fast((2 * number, 2 * number + 1))
        return carry

    lax.fori_loop(0, pairs // 2, two, 0)

    @pl.when(pairs % 2 == 1)
    def _():
        fast((pairs - 1,))

    outside = (limits[0] < LEAST) | (limits[1] > MOST)
    outside = jnp.where((lane_side == key_side) & outside, 1.0, 0.0)

    @pl.when(jnp.max(outside) > 0.5)
    def _():
        total[...] = jnp.zeros_like(total)
        lax.fori_loop(0, pairs, slow, 0)

    if not first:
        carry_copy.wait()
    gone = []
    for pair in range(per_dev // 2):
        even, uneven = total[2 * pair], total[2 * pair + 1]
        even_low = jnp.where(key_side == 1, even, pltpu.roll(even, head_dim, 1))
        uneven_high = jnp.where(key_side == 0, uneven, pltpu.roll(uneven, head_dim, 1))
        both = jnp.where(lane_side == 0, even_low, uneven_high)
        if not first:
            both += carried[pair]
        if last:
            place = (slice(None), slice(pair * row_count, (pair + 1) * row_count))
            out[place] = both.astype(BF16).reshape(devices, row_count, lanes)
        else:
            place = (pair,)
            out[pair] = both
        gone.append(pltpu.make_async_copy(out.at[place], out_hbm.at[place], left.at[pair]))
        gone[-1].start()
    for copy in gone:
        copy.wait()


def attend(kinds, last, head_dim, counts, partners, own, blocks, carried):
    devices, flat_rows, lanes = own.shape
    per_dev = counts.shape[0] // lax.axis_size("img")
    keypoints = devices * flat_rows // per_dev
    packed = (per_dev // 2, keypoints, lanes)
    first = carried is None
    arguments = [counts, partners, own, *blocks] + ([] if first else [carried])
    if last:
        out_shape = jax.ShapeDtypeStruct((devices, flat_rows // 2, lanes), BF16)
    else:
        out_shape = jax.ShapeDtypeStruct(packed, F32)
    scratch = [
        pltpu.VMEM(own.shape, BF16),
        pltpu.VMEM((len(kinds), *own.shape), BF16),
        pltpu.VMEM((per_dev, keypoints, lanes), F32),
        pltpu.VMEM((2, 8, lanes), F32),
        pltpu.SMEM((4, len(kinds) * per_dev * per_dev + 1), jnp.int32),
        pltpu.SemaphoreType.DMA((1 + len(kinds), devices)),
        pltpu.VMEM(out_shape.shape, out_shape.dtype),
        pltpu.SemaphoreType.DMA((per_dev // 2,)),
    ]
    if not first:
        scratch += [pltpu.VMEM(packed, F32), pltpu.SemaphoreType.DMA]
    return pl.pallas_call(
        functools.partial(attend_kernel, kinds, first, last, head_dim),
        out_shape=out_shape,
        in_specs=[whole(pltpu.SMEM)] * 2 + [whole(pltpu.HBM)] * (len(arguments) - 2),
        out_specs=whole(pltpu.HBM),
        scratch_shapes=scratch,
        compiler_params=pltpu.CompilerParams(vmem_limit_bytes=VMEM),
        cost_estimate=pl.CostEstimate(
            flops=0 if first else len(kinds) * 4 * 2 * 2 * keypoints * keypoints * 512,
            bytes_accessed=0 if first else 4 * devices * flat_rows * lanes + 8 * keypoints * lanes,
            transcendentals=0 if first else len(kinds) * 4 * keypoints * keypoints,
        ),
        name="attend_" + "_".join(str(kind) for kind in kinds),
    )(*arguments)


def refine_kernel(head_dim, everyone, features, messages, out_proj, ffn_in, ffn_in_bias, norm_gain,
                  norm_bias, ffn_out, ffn_out_bias, out):
    together, row_count, width = features.shape
    lanes = 2 * head_dim
    pair = pl.program_id(0)
    first_image = (lax.axis_index("img") * pl.num_programs(0) + pair) * together
    lane_side = lax.broadcasted_iota(jnp.int32, (1, lanes), 1) // head_dim
    tiles = [messages[head, 0].astype(F32) for head in range(HEADS)]
    turned = [pltpu.roll(tile, head_dim, 1) for tile in tiles]
    averaged = []
    for image in range(together):
        low, high = (tiles, turned) if image == 0 else (turned, tiles)
        inbox = jnp.concatenate(
            [jnp.where(lane_side == 0, low[head], high[head + 1]) for head in range(0, HEADS, 2)], axis=1
        )
        asked = (everyone[...] == first_image + image).astype(F32)
        degree = jnp.sum(asked, axis=1, keepdims=True)
        averaged.append((inbox / (2.0 + degree)).astype(BF16))
    averaged = jnp.concatenate(averaged, axis=0)
    projected = jnp.dot(averaged, out_proj[...], preferred_element_type=F32).astype(BF16)
    source = features[...].reshape(together * row_count, width)
    hidden = (
        jnp.dot(source.astype(BF16), ffn_in[:width], preferred_element_type=F32)
        + jnp.dot(projected, ffn_in[width:], preferred_element_type=F32)
        + ffn_in_bias[...]
    )
    hidden = hidden - jnp.mean(hidden, axis=1, keepdims=True)
    spread = jnp.mean(hidden * hidden, axis=1, keepdims=True)
    normed = hidden * lax.rsqrt(spread + 1e-05) * norm_gain[...] + norm_bias[...]
    activated = (0.5 * normed * (1.0 + lax.erf(normed * (0.5**0.5)))).astype(BF16)
    refined = source + jnp.dot(activated, ffn_out[...], preferred_element_type=F32) + ffn_out_bias[...]
    out[...] = refined.reshape(together, row_count, width)


def per_device(features, partners, counts, shared_proj, value_proj, out_proj, ffn_in, ffn_in_bias,
               norm_gain, norm_bias, ffn_out, ffn_out_bias):
    img_count = lax.axis_size("img")
    row_devices = lax.axis_size("row")
    per_dev, row_count, width = features.shape
    head_dim = width // HEADS
    blocks = range(img_count)
    swap = [(s, s ^ 1) for s in blocks]
    thick_pairs = [(s, (s + (2 if s % 2 else -2)) % img_count) for s in blocks]
    thin_pairs = [(s, (s + (-2 if s % 2 else 2)) % img_count) for s in blocks]

    rounded = features.astype(BF16)
    thick = lax.ppermute(rounded, "img", thick_pairs)
    thin = lax.ppermute(rounded, "img", thin_pairs)
    flat_partners = partners.reshape(-1)

    weights = (shared_proj, value_proj, row_devices)
    own = project(rounded, *weights)
    companion = lax.ppermute(own, "img", swap)
    thick = project(thick, *weights, weigh=50)
    work = functools.partial(attend, head_dim=head_dim, counts=counts, partners=flat_partners, own=own)
    sums = work((COMPANION,), False, blocks=[companion], carried=None)
    thick = tie(thick, sums)
    cross = lax.ppermute(thick, "img", swap)
    thin = project(thin, *weights, after=(sums,), weigh=50)
    sums = work((THICK, CROSS), False, blocks=[thick, cross], carried=sums)
    messages = work((THIN,), True, blocks=[thin], carried=sums)
    messages = exchange(messages)[::row_devices // HEADS].reshape(HEADS, per_dev // 2, row_count, 2 * head_dim)

    pair = pl.BlockSpec((2, row_count, width), lambda i: (i, 0, 0))
    return pl.pallas_call(
        functools.partial(refine_kernel, head_dim),
        grid=(per_dev // 2,),
        out_shape=jax.ShapeDtypeStruct(features.shape, F32),
        in_specs=[
            whole(), pair, pl.BlockSpec((HEADS, 1, row_count, 2 * head_dim), lambda i: (0, i, 0, 0)),
        ] + [whole()] * 7,
        out_specs=pair,
        compiler_params=pltpu.CompilerParams(vmem_limit_bytes=VMEM // 3),
        cost_estimate=pl.CostEstimate(
            flops=10 * per_dev * row_count * width * width * 2, bytes_accessed=2**22, transcendentals=2**20
        ),
        name="refine",
    )(flat_partners[None], features, messages, out_proj, ffn_in, ffn_in_bias[None], norm_gain[None],
      norm_bias[None], ffn_out, ffn_out_bias[None])


def solution(mesh):
    return jax.shard_map(
        per_device,
        mesh=mesh,
        in_specs=(P("img", "row", None), P(), P(), P(), P(), P(), P(), P(), P(), P(), P(), P()),
        out_specs=P("img", "row", None),
        check_vma=False,
    )
```

```python
import functools
import math

import jax
import jax.numpy as jnp
from jax import lax
from jax.experimental import pallas as pl
from jax.experimental.pallas import tpu as pltpu
from jax.sharding import PartitionSpec as P

HEADS = 4
LEAST, MOST = 1e-25, 1e25
NEGATIVE = -1e30
VMEM = 60 * 2**20
NT = (((1,), (1,)), ((), ()))
F32 = jnp.float32
BF16 = jnp.bfloat16

COMPANION, THICK, THIN, CROSS = range(4)


def block_of(kind, me, img_count):
    odd = lax.rem(me, 2)
    ahead = 1 - 2 * odd
    step = {COMPANION: ahead, THICK: 2 * ahead, THIN: -2 * ahead, CROSS: -ahead}[kind]
    return lax.rem(me + step + img_count, img_count)


def whole(memory=pltpu.VMEM):
    return pl.BlockSpec(memory_space=memory)


def exchange(value):
    return lax.all_to_all(value, "row", split_axis=0, concat_axis=0, tiled=True)


def project_kernel(head_dim, rounds, rows, shared_proj, value_proj, *outs):
    out = outs[-1]
    heads, _, lanes = out.shape
    low = lax.broadcasted_iota(jnp.int32, (1, lanes), 1) < head_dim
    source = rows[...].astype(BF16)
    if rounds:
        outs[0][...] = source
    for pair in range(heads // 2):
        columns = slice(pair * lanes, (pair + 1) * lanes)
        turned = pltpu.roll(value_proj[:, columns].astype(F32), head_dim, 1).astype(BF16)
        both = jnp.concatenate([shared_proj[:, columns], turned], axis=1)
        projected = jnp.dot(source, both, preferred_element_type=F32)
        shared, values = projected[:, :lanes], projected[:, lanes:]
        out[2 * pair] = jnp.where(low, shared, values).astype(BF16)
        out[2 * pair + 1] = jnp.where(low, values, shared).astype(BF16)


def project(value, shared_proj, value_proj, row_devices, after=(), weigh=1):
    per_dev, row_count, width = value.shape
    rows = per_dev * row_count
    head_dim = width // HEADS
    rounds = value.dtype == F32

    def kernel(rows_ref, shared_ref, value_ref, *refs):
        project_kernel(head_dim, rounds, rows_ref, shared_ref, value_ref, *refs[len(after):])

    part = pl.BlockSpec((row_count, width), lambda i: (i, 0))
    out_shapes = [jax.ShapeDtypeStruct((HEADS, rows, 2 * head_dim), BF16)]
    out_specs = [pl.BlockSpec((HEADS, row_count, 2 * head_dim), lambda i: (0, i, 0))]
    if rounds:
        out_shapes.insert(0, jax.ShapeDtypeStruct((rows, width), BF16))
        out_specs.insert(0, part)
    *rounded, packed = pl.pallas_call(
        kernel,
        grid=(per_dev,),
        out_shape=out_shapes,
        in_specs=[part] + [whole()] * 2 + [whole(pl.ANY)] * len(after),
        out_specs=out_specs,
        compiler_params=pltpu.CompilerParams(vmem_limit_bytes=VMEM),
        cost_estimate=pl.CostEstimate(
            flops=weigh * 4 * rows * width * width, bytes_accessed=6 * rows * width, transcendentals=0
        ),
        name="project",
    )(value.reshape(rows, width), shared_proj, value_proj, *after)
    if row_devices > HEADS:
        packed = jnp.repeat(packed, row_devices // HEADS, axis=0)
    packed = exchange(packed)
    return (rounded[0].reshape(value.shape), packed) if rounds else packed


def tie(value, after):
    def kernel(value_ref, after_ref, out_ref):
        pass

    return pl.pallas_call(
        kernel,
        out_shape=jax.ShapeDtypeStruct(value.shape, value.dtype),
        in_specs=[whole(pltpu.HBM)] * 2,
        out_specs=whole(pltpu.HBM),
        input_output_aliases={0: 0},
        name="tie",
    )(value, after)


def attend_kernel(kinds, first, last, head_dim, counts, partners, own_hbm, *refs):
    blocks_hbm, refs = refs[:len(kinds)], refs[len(kinds):]
    if first:
        out_hbm, own, blocks, keys, values, turned, total, limits, todo, arrived, out, left = refs
    else:
        carried_hbm, out_hbm, own, blocks, keys, values, turned, total, limits, todo, arrived, out, left, carried, carried_here = refs
    devices, flat_rows, lanes = own.shape
    img_count = lax.axis_size("img")
    me = lax.axis_index("img")
    per_dev = counts.shape[0] // img_count
    row_count = flat_rows // per_dev
    keypoints = devices * row_count
    once = max(256, row_count)
    sources = once // row_count
    factor = head_dim ** (-0.5) * math.log2(math.e)

    copies = []
    for number, (source, target) in enumerate(
        [(own_hbm, own)] + [(block, blocks.at[place]) for place, block in enumerate(blocks_hbm)]
    ):
        for device in range(devices):
            copies.append(
                pltpu.make_async_copy(source.at[device], target.at[device], arrived.at[number, device])
            )
    for copy in copies:
        copy.start()
    if not first:
        carry_copy = pltpu.make_async_copy(carried_hbm, carried, carried_here)
        carry_copy.start()

    key_side = lax.rem(lax.div(lax.axis_index("row"), devices // HEADS), 2)
    lane_side = lax.broadcasted_iota(jnp.int32, (1, lanes), 1) // head_dim
    key_row = lax.broadcasted_iota(jnp.int32, (keypoints, 1), 0)
    key_lane = lax.broadcasted_iota(jnp.int32, (1, keypoints), 1)
    one, zero = jnp.ones((), BF16), jnp.zeros((), BF16)
    total[...] = jnp.zeros_like(total)
    limits[...] = jnp.ones_like(limits)

    pairs = jnp.zeros((), jnp.int32)
    for place, kind in enumerate(kinds):
        block_id = block_of(kind, me, img_count)
        for other in range(per_dev):
            for image in range(per_dev):
                theirs, mine = block_id * per_dev + other, me * per_dev + image
                times = jnp.zeros((), jnp.int32)
                for side in range(2):
                    times += (partners[2 * mine + side] == theirs).astype(jnp.int32)
                    times += (partners[2 * theirs + side] == mine).astype(jnp.int32)
                todo[0, pairs] = place * per_dev + other
                todo[1, pairs] = image
                todo[2, pairs] = times
                todo[3, pairs] = counts[theirs]
                pairs = pairs + (times > 0).astype(jnp.int32)
    for copy in copies:
        copy.wait()

    def image_rows(image):
        return pl.ds(pl.multiple_of(image * row_count, row_count), row_count)

    value_rows = pl.ds(pl.multiple_of((1 - key_side) * head_dim, head_dim), head_dim)
    for place, kind in enumerate(kinds):
        block_id = block_of(kind, me, img_count)
        for other in range(per_dev):
            spot = place * per_dev + other
            limit = counts[block_id * per_dev + other]
            tile = blocks[place, :, other * row_count:(other + 1) * row_count].reshape(keypoints, lanes)
            keys[spot] = jnp.where(key_row < limit, jnp.where(lane_side == key_side, tile, zero), zero)
            turned[...] = tile.T
            values[spot, :head_dim] = jnp.where(key_lane < limit, turned[value_rows], zero)
            values[spot, head_dim:] = jnp.broadcast_to(
                jnp.where(key_lane < limit, one, zero), (values.shape[1] - head_dim, keypoints)
            )

    def score(spot, image, start):
        queries = own[start:start + sources, image_rows(image), :].reshape(once, lanes)
        return lax.dot_general(keys[spot], queries, NT, preferred_element_type=F32)

    def add(image, start, got, times):
        columns = slice(start * row_count, start * row_count + once)
        share = times / got[head_dim:head_dim + 8]
        messages = got[:head_dim].reshape(head_dim // 8, 8, once) * share
        total[image, :, columns] += messages.reshape(head_dim, once)

    def fast(numbers):
        work = [(todo[0, number], todo[1, number], todo[2, number].astype(F32)) for number in numbers]
        least, most = limits[0], limits[1]
        for start in range(0, devices, sources):
            results = []
            for spot, image, _ in work:
                raised = jnp.exp2(score(spot, image, start) * factor).astype(BF16)
                got = jnp.dot(values[spot], raised, preferred_element_type=F32)
                least = jnp.minimum(least, got[head_dim:head_dim + 8])
                most = jnp.maximum(most, got[head_dim:head_dim + 8])
                results.append(got)
            for (_, image, times), got in zip(work, results):
                add(image, start, got, times)
        limits[0] = least
        limits[1] = most

    def slow(number, carry):
        spot, image, times = todo[0, number], todo[1, number], todo[2, number].astype(F32)
        present = key_row < todo[3, number]
        for start in range(0, devices, sources):
            scores = score(spot, image, start)
            peak = jnp.max(jnp.where(present, scores, NEGATIVE), axis=0, keepdims=True)
            raised = jnp.where(present, jnp.exp2((scores - peak) * factor), 0.0).astype(BF16)
            add(image, start, jnp.dot(values[spot], raised, preferred_element_type=F32), times)
        return carry

    def two(number, carry):
        fast((2 * number, 2 * number + 1))
        return carry

    lax.fori_loop(0, pairs // 2, two, 0)

    @pl.when(pairs % 2 == 1)
    def _():
        fast((pairs - 1,))

    outside = (limits[0] < LEAST) | (limits[1] > MOST)

    @pl.when(jnp.max(jnp.where(outside, 1.0, 0.0)) > 0.5)
    def _():
        total[...] = jnp.zeros_like(total)
        lax.fori_loop(0, pairs, slow, 0)

    if not first:
        carry_copy.wait()
    gone = []
    for pair in range(per_dev // 2):
        both = total[2 * pair:2 * pair + 2].reshape(lanes, keypoints).T
        if not first:
            both += carried[pair]
        if last:
            place = (slice(None), slice(pair * row_count, (pair + 1) * row_count))
            out[place] = both.astype(BF16).reshape(devices, row_count, lanes)
        else:
            place = (pair,)
            out[pair] = both
        gone.append(pltpu.make_async_copy(out.at[place], out_hbm.at[place], left.at[pair]))
        gone[-1].start()
    for copy in gone:
        copy.wait()


def attend(kinds, last, head_dim, counts, partners, own, blocks, carried):
    devices, flat_rows, lanes = own.shape
    per_dev = counts.shape[0] // lax.axis_size("img")
    keypoints = devices * flat_rows // per_dev
    packed = (per_dev // 2, keypoints, lanes)
    first = carried is None
    arguments = [counts, partners, own, *blocks] + ([] if first else [carried])
    if last:
        out_shape = jax.ShapeDtypeStruct((devices, flat_rows // 2, lanes), BF16)
    else:
        out_shape = jax.ShapeDtypeStruct(packed, F32)
    scratch = [
        pltpu.VMEM(own.shape, BF16),
        pltpu.VMEM((len(kinds), *own.shape), BF16),
        pltpu.VMEM((len(kinds) * per_dev, keypoints, lanes), BF16),
        pltpu.VMEM((len(kinds) * per_dev, head_dim + 16, keypoints), BF16),
        pltpu.VMEM((lanes, keypoints), BF16),
        pltpu.VMEM((per_dev, head_dim, keypoints), F32),
        pltpu.VMEM((2, 8, max(256, flat_rows // per_dev)), F32),
        pltpu.SMEM((4, len(kinds) * per_dev * per_dev + 1), jnp.int32),
        pltpu.SemaphoreType.DMA((1 + len(kinds), devices)),
        pltpu.VMEM(out_shape.shape, out_shape.dtype),
        pltpu.SemaphoreType.DMA((per_dev // 2,)),
    ]
    if not first:
        scratch += [pltpu.VMEM(packed, F32), pltpu.SemaphoreType.DMA]
    return pl.pallas_call(
        functools.partial(attend_kernel, kinds, first, last, head_dim),
        out_shape=out_shape,
        in_specs=[whole(pltpu.SMEM)] * 2 + [whole(pltpu.HBM)] * (len(arguments) - 2),
        out_specs=whole(pltpu.HBM),
        scratch_shapes=scratch,
        compiler_params=pltpu.CompilerParams(vmem_limit_bytes=VMEM),
        cost_estimate=pl.CostEstimate(
            flops=0 if first else len(kinds) * 4 * 2 * 2 * keypoints * keypoints * 512,
            bytes_accessed=0 if first else 4 * devices * flat_rows * lanes + 8 * keypoints * lanes,
            transcendentals=0 if first else len(kinds) * 4 * keypoints * keypoints,
        ),
        name="attend_" + "_".join(str(kind) for kind in kinds),
    )(*arguments)


def refine_kernel(head_dim, everyone, features, messages, out_proj, ffn_in, ffn_in_bias, norm_gain,
                  norm_bias, ffn_out, ffn_out_bias, out):
    together, row_count, width = features.shape
    lanes = 2 * head_dim
    pair = pl.program_id(0)
    first_image = (lax.axis_index("img") * pl.num_programs(0) + pair) * together
    lane_side = lax.broadcasted_iota(jnp.int32, (1, lanes), 1) // head_dim
    tiles = [messages[head, 0].astype(F32) for head in range(HEADS)]
    turned = [pltpu.roll(tile, head_dim, 1) for tile in tiles]
    averaged = []
    for image in range(together):
        low, high = (tiles, turned) if image == 0 else (turned, tiles)
        inbox = jnp.concatenate(
            [jnp.where(lane_side == 0, low[head], high[head + 1]) for head in range(0, HEADS, 2)], axis=1
        )
        asked = (everyone[...] == first_image + image).astype(F32)
        degree = jnp.sum(asked, axis=1, keepdims=True)
        averaged.append((inbox / (2.0 + degree)).astype(BF16))
    averaged = jnp.concatenate(averaged, axis=0)
    projected = jnp.dot(averaged, out_proj[...], preferred_element_type=F32).astype(BF16)
    source = features[...].reshape(together * row_count, width)
    hidden = (
        jnp.dot(source.astype(BF16), ffn_in[:width], preferred_element_type=F32)
        + jnp.dot(projected, ffn_in[width:], preferred_element_type=F32)
        + ffn_in_bias[...]
    )
    hidden = hidden - jnp.mean(hidden, axis=1, keepdims=True)
    spread = jnp.mean(hidden * hidden, axis=1, keepdims=True)
    normed = hidden * lax.rsqrt(spread + 1e-05) * norm_gain[...] + norm_bias[...]
    activated = (0.5 * normed * (1.0 + lax.erf(normed * (0.5**0.5)))).astype(BF16)
    refined = source + jnp.dot(activated, ffn_out[...], preferred_element_type=F32) + ffn_out_bias[...]
    out[...] = refined.reshape(together, row_count, width)


def per_device(features, partners, counts, shared_proj, value_proj, out_proj, ffn_in, ffn_in_bias,
               norm_gain, norm_bias, ffn_out, ffn_out_bias):
    img_count = lax.axis_size("img")
    row_devices = lax.axis_size("row")
    per_dev, row_count, width = features.shape
    head_dim = width // HEADS
    blocks = range(img_count)
    swap = [(s, s ^ 1) for s in blocks]
    thick_pairs = [(s, (s + (2 if s % 2 else -2)) % img_count) for s in blocks]
    thin_pairs = [(s, (s + (-2 if s % 2 else 2)) % img_count) for s in blocks]

    weights = (shared_proj, value_proj, row_devices)
    rounded, own = project(features, *weights)
    thick = lax.ppermute(rounded, "img", thick_pairs)
    thin = lax.ppermute(rounded, "img", thin_pairs)
    flat_partners = partners.reshape(-1)

    companion = lax.ppermute(own, "img", swap)
    thick = project(thick, *weights, weigh=50)
    work = functools.partial(attend, head_dim=head_dim, counts=counts, partners=flat_partners, own=own)
    sums = work((COMPANION,), False, blocks=[companion], carried=None)
    thick = tie(thick, sums)
    cross = lax.ppermute(thick, "img", swap)
    thin = project(thin, *weights, after=(sums,), weigh=50)
    sums = work((THICK, CROSS), False, blocks=[thick, cross], carried=sums)
    messages = work((THIN,), True, blocks=[thin], carried=sums)
    messages = exchange(messages)[::row_devices // HEADS].reshape(HEADS, per_dev // 2, row_count, 2 * head_dim)

    pair = pl.BlockSpec((2, row_count, width), lambda i: (i, 0, 0))
    return pl.pallas_call(
        functools.partial(refine_kernel, head_dim),
        grid=(per_dev // 2,),
        out_shape=jax.ShapeDtypeStruct(features.shape, F32),
        in_specs=[
            whole(), pair, pl.BlockSpec((HEADS, 1, row_count, 2 * head_dim), lambda i: (0, i, 0, 0)),
        ] + [whole()] * 7,
        out_specs=pair,
        compiler_params=pltpu.CompilerParams(vmem_limit_bytes=VMEM // 3),
        cost_estimate=pl.CostEstimate(
            flops=10 * per_dev * row_count * width * width * 2, bytes_accessed=2**22, transcendentals=2**20
        ),
        name="refine",
    )(flat_partners[None], features, messages, out_proj, ffn_in, ffn_in_bias[None], norm_gain[None],
      norm_bias[None], ffn_out, ffn_out_bias[None])


def solution(mesh):
    return jax.shard_map(
        per_device,
        mesh=mesh,
        in_specs=(P("img", "row", None), P(), P(), P(), P(), P(), P(), P(), P(), P(), P(), P()),
        out_specs=P("img", "row", None),
        check_vma=False,
    )
```

```python
import functools
import math

import jax
import jax.numpy as jnp
from jax import lax
from jax.experimental import pallas as pl
from jax.experimental.pallas import tpu as pltpu
from jax.sharding import PartitionSpec as P

HEADS = 4
LEAST, MOST = 1e-25, 1e25
NEGATIVE = -1e30
VMEM = 60 * 2**20
NT = (((1,), (1,)), ((), ()))
F32 = jnp.float32
BF16 = jnp.bfloat16

COMPANION, THICK, THIN, CROSS = range(4)


def block_of(kind, me, img_count):
    odd = lax.rem(me, 2)
    ahead = 1 - 2 * odd
    step = {COMPANION: ahead, THICK: 2 * ahead, THIN: -2 * ahead, CROSS: -ahead}[kind]
    return lax.rem(me + step + img_count, img_count)


def whole(memory=pltpu.VMEM):
    return pl.BlockSpec(memory_space=memory)


def exchange(value):
    return lax.all_to_all(value, "row", split_axis=0, concat_axis=0, tiled=True)


def project_kernel(head_dim, per_dev, rounds, source, shared_hbm, value_hbm, *refs):
    rows, shared_proj, value_proj, packed, came, went, *rounded = refs[-7 if rounds else -6:]
    outs = refs[:-7 if rounds else -6]
    out_hbm = outs[-1]
    heads, flat_rows, lanes = packed.shape
    row_count = flat_rows // per_dev
    arrivals = [
        pltpu.make_async_copy(shared_hbm, shared_proj, came.at[per_dev]),
        pltpu.make_async_copy(value_hbm, value_proj, came.at[per_dev + 1]),
    ]
    pieces = [slice(image * row_count, (image + 1) * row_count) for image in range(per_dev)]
    loads = [
        pltpu.make_async_copy(source.at[piece], rows.at[piece], came.at[image])
        for image, piece in enumerate(pieces)
    ]
    for copy in arrivals + loads:
        copy.start()
    for copy in arrivals:
        copy.wait()
    low = lax.broadcasted_iota(jnp.int32, (1, lanes), 1) < head_dim
    both = []
    for pair in range(heads // 2):
        columns = slice(pair * lanes, (pair + 1) * lanes)
        turned = pltpu.roll(value_proj[:, columns].astype(F32), head_dim, 1).astype(BF16)
        both.append(jnp.concatenate([shared_proj[:, columns], turned], axis=1))
    leaving = []
    for image, piece in enumerate(pieces):
        loads[image].wait()
        value = rows[piece].astype(BF16)
        if rounds:
            rounded[0][piece] = value
            leaving.append(pltpu.make_async_copy(rounded[0].at[piece], outs[0].at[piece], went.at[1, image]))
            leaving[-1].start()
        for pair in range(heads // 2):
            projected = jnp.dot(value, both[pair], preferred_element_type=F32)
            shared, values = projected[:, :lanes], projected[:, lanes:]
            packed[2 * pair, piece] = jnp.where(low, shared, values).astype(BF16)
            packed[2 * pair + 1, piece] = jnp.where(low, values, shared).astype(BF16)
        leaving.append(pltpu.make_async_copy(packed.at[:, piece], out_hbm.at[:, piece], went.at[0, image]))
        leaving[-1].start()
    for copy in leaving:
        copy.wait()


def project(value, shared_proj, value_proj, row_devices, after=(), weigh=1):
    per_dev, row_count, width = value.shape
    rows = per_dev * row_count
    head_dim = width // HEADS
    rounds = value.dtype == F32

    def kernel(rows_ref, shared_ref, value_ref, *refs):
        project_kernel(head_dim, per_dev, rounds, rows_ref, shared_ref, value_ref, *refs[len(after):])

    packed_shape = (HEADS, rows, 2 * head_dim)
    out_shapes = [jax.ShapeDtypeStruct(packed_shape, BF16)]
    scratch = [
        pltpu.VMEM((rows, width), value.dtype),
        pltpu.VMEM(shared_proj.shape, BF16),
        pltpu.VMEM(value_proj.shape, BF16),
        pltpu.VMEM(packed_shape, BF16),
        pltpu.SemaphoreType.DMA((per_dev + 2,)),
        pltpu.SemaphoreType.DMA((2, per_dev)),
    ]
    if rounds:
        out_shapes.insert(0, jax.ShapeDtypeStruct((rows, width), BF16))
        scratch.append(pltpu.VMEM((rows, width), BF16))
    *rounded, packed = pl.pallas_call(
        kernel,
        out_shape=out_shapes,
        in_specs=[whole(pl.ANY)] * (3 + len(after)),
        out_specs=[whole(pl.ANY)] * len(out_shapes),
        scratch_shapes=scratch,
        compiler_params=pltpu.CompilerParams(vmem_limit_bytes=VMEM),
        cost_estimate=pl.CostEstimate(
            flops=weigh * 4 * rows * width * width, bytes_accessed=6 * rows * width, transcendentals=0
        ),
        name="project",
    )(value.reshape(rows, width), shared_proj, value_proj, *after)
    if row_devices > HEADS:
        packed = jnp.repeat(packed, row_devices // HEADS, axis=0)
    packed = exchange(packed)
    return (rounded[0].reshape(value.shape), packed) if rounds else packed


def tie(value, after):
    def kernel(value_ref, after_ref, out_ref):
        pass

    return pl.pallas_call(
        kernel,
        out_shape=jax.ShapeDtypeStruct(value.shape, value.dtype),
        in_specs=[whole(pltpu.HBM)] * 2,
        out_specs=whole(pltpu.HBM),
        input_output_aliases={0: 0},
        name="tie",
    )(value, after)


def attend_kernel(kinds, first, last, head_dim, counts, partners, own_hbm, *refs):
    blocks_hbm, refs = refs[:len(kinds)], refs[len(kinds):]
    if first:
        out_hbm, own, blocks, total, limits, todo, arrived, out, left = refs
    else:
        carried_hbm, out_hbm, own, blocks, total, limits, todo, arrived, out, left, carried, carried_here = refs
    devices, flat_rows, lanes = own.shape
    img_count = lax.axis_size("img")
    me = lax.axis_index("img")
    per_dev = counts.shape[0] // img_count
    row_count = flat_rows // per_dev
    keypoints = devices * row_count
    once = max(min(512, keypoints), row_count)
    sources = once // row_count
    factor = head_dim ** (-0.5) * math.log2(math.e)

    copies = []
    for number, (source, target) in enumerate(
        [(own_hbm, own)] + [(block, blocks.at[place]) for place, block in enumerate(blocks_hbm)]
    ):
        for device in range(devices):
            copies.append(
                pltpu.make_async_copy(source.at[device], target.at[device], arrived.at[number, device])
            )
    for copy in copies:
        copy.start()
    if not first:
        carry_copy = pltpu.make_async_copy(carried_hbm, carried, carried_here)
        carry_copy.start()

    key_side = lax.rem(lax.div(lax.axis_index("row"), devices // HEADS), 2)
    lane_side = lax.broadcasted_iota(jnp.int32, (1, lanes), 1) // head_dim
    key_row = lax.broadcasted_iota(jnp.int32, (keypoints, 1), 0)
    key_lane = lax.broadcasted_iota(jnp.int32, (1, keypoints), 1)
    one, zero = jnp.ones((), BF16), jnp.zeros((), BF16)
    total[...] = jnp.zeros_like(total)
    limits[...] = jnp.ones_like(limits)

    pairs = jnp.zeros((), jnp.int32)
    for place, kind in enumerate(kinds):
        block_id = block_of(kind, me, img_count)
        for other in range(per_dev):
            for image in range(per_dev):
                theirs, mine = block_id * per_dev + other, me * per_dev + image
                times = jnp.zeros((), jnp.int32)
                for side in range(2):
                    times += (partners[2 * mine + side] == theirs).astype(jnp.int32)
                    times += (partners[2 * theirs + side] == mine).astype(jnp.int32)
                todo[0, pairs] = place * per_dev + other
                todo[1, pairs] = image
                todo[2, pairs] = times
                todo[3, pairs] = counts[theirs]
                pairs = pairs + (times > 0).astype(jnp.int32)
    for copy in copies:
        copy.wait()

    def image_rows(image):
        return pl.ds(pl.multiple_of(image * row_count, row_count), row_count)

    def operands(number):
        other, image, limit = todo[0, number], todo[1, number], todo[3, number]
        place, other = lax.div(other, per_dev), lax.rem(other, per_dev)
        tile = blocks[place, :, image_rows(other), :].reshape(keypoints, lanes)
        is_key, present = lane_side == key_side, key_row < limit
        keys = jnp.where(present, jnp.where(is_key, tile, zero), zero)
        values = jnp.where(present, jnp.where(is_key, one, tile), zero)
        return image, keys, values, limit, todo[2, number].astype(F32)

    def score(image, start, keys):
        queries = own[start:start + sources, image_rows(image), :].reshape(once, lanes)
        return lax.dot_general(queries, keys, NT, preferred_element_type=F32)

    def add(image, start, got, times):
        rows = slice(start * row_count, start * row_count + once)
        below = pltpu.roll(got, head_dim, 1)
        share = pl.reciprocal(below, approx=True)
        share = share * (2.0 - below * share)
        total[image, rows] += got * (share * times)

    def fast(numbers):
        work = [operands(number) for number in numbers]
        least, most = limits[0], limits[1]
        for start in range(0, devices, sources):
            results = []
            for image, keys, values, _, times in work:
                raised = jnp.exp2(score(image, start, keys) * factor).astype(BF16)
                got = jnp.dot(raised, values, preferred_element_type=F32)
                by_row = got.reshape(once // 8, 8, lanes)
                least = jnp.minimum(least, jnp.min(by_row, axis=0))
                most = jnp.maximum(most, jnp.max(by_row, axis=0))
                results.append(got)
            for (image, _, _, _, times), got in zip(work, results):
                add(image, start, got, times)
        limits[0] = least
        limits[1] = most

    def slow(number, carry):
        image, keys, values, limit, times = operands(number)
        present = key_lane < limit
        for start in range(0, devices, sources):
            scores = score(image, start, keys)
            peak = jnp.max(jnp.where(present, scores, NEGATIVE), axis=1, keepdims=True)
            raised = jnp.where(present, jnp.exp2((scores - peak) * factor), 0.0).astype(BF16)
            add(image, start, jnp.dot(raised, values, preferred_element_type=F32), times)
        return carry

    def two(number, carry):
        fast((2 * number, 2 * number + 1))
        return carry

    lax.fori_loop(0, pairs // 2, two, 0)

    @pl.when(pairs % 2 == 1)
    def _():
        fast((pairs - 1,))

    outside = (limits[0] < LEAST) | (limits[1] > MOST)
    outside = jnp.where((lane_side == key_side) & outside, 1.0, 0.0)

    @pl.when(jnp.max(outside) > 0.5)
    def _():
        total[...] = jnp.zeros_like(total)
        lax.fori_loop(0, pairs, slow, 0)

    if not first:
        carry_copy.wait()
    gone = []
    for pair in range(per_dev // 2):
        even, uneven = total[2 * pair], total[2 * pair + 1]
        even_low = jnp.where(key_side == 1, even, pltpu.roll(even, head_dim, 1))
        uneven_high = jnp.where(key_side == 0, uneven, pltpu.roll(uneven, head_dim, 1))
        both = jnp.where(lane_side == 0, even_low, uneven_high)
        if not first:
            both += carried[pair]
        if last:
            place = (slice(None), slice(pair * row_count, (pair + 1) * row_count))
            out[place] = both.astype(BF16).reshape(devices, row_count, lanes)
        else:
            place = (pair,)
            out[pair] = both
        gone.append(pltpu.make_async_copy(out.at[place], out_hbm.at[place], left.at[pair]))
        gone[-1].start()
    for copy in gone:
        copy.wait()


def attend(kinds, last, head_dim, counts, partners, own, blocks, carried):
    devices, flat_rows, lanes = own.shape
    per_dev = counts.shape[0] // lax.axis_size("img")
    keypoints = devices * flat_rows // per_dev
    packed = (per_dev // 2, keypoints, lanes)
    first = carried is None
    arguments = [counts, partners, own, *blocks] + ([] if first else [carried])
    if last:
        out_shape = jax.ShapeDtypeStruct((devices, flat_rows // 2, lanes), BF16)
    else:
        out_shape = jax.ShapeDtypeStruct(packed, F32)
    scratch = [
        pltpu.VMEM(own.shape, BF16),
        pltpu.VMEM((len(kinds), *own.shape), BF16),
        pltpu.VMEM((per_dev, keypoints, lanes), F32),
        pltpu.VMEM((2, 8, lanes), F32),
        pltpu.SMEM((4, len(kinds) * per_dev * per_dev + 1), jnp.int32),
        pltpu.SemaphoreType.DMA((1 + len(kinds), devices)),
        pltpu.VMEM(out_shape.shape, out_shape.dtype),
        pltpu.SemaphoreType.DMA((per_dev // 2,)),
    ]
    if not first:
        scratch += [pltpu.VMEM(packed, F32), pltpu.SemaphoreType.DMA]
    return pl.pallas_call(
        functools.partial(attend_kernel, kinds, first, last, head_dim),
        out_shape=out_shape,
        in_specs=[whole(pltpu.SMEM)] * 2 + [whole(pltpu.HBM)] * (len(arguments) - 2),
        out_specs=whole(pltpu.HBM),
        scratch_shapes=scratch,
        compiler_params=pltpu.CompilerParams(vmem_limit_bytes=VMEM),
        cost_estimate=pl.CostEstimate(
            flops=0 if first else len(kinds) * 4 * 2 * 2 * keypoints * keypoints * 512,
            bytes_accessed=0 if first else 4 * devices * flat_rows * lanes + 8 * keypoints * lanes,
            transcendentals=0 if first else len(kinds) * 4 * keypoints * keypoints,
        ),
        name="attend_" + "_".join(str(kind) for kind in kinds),
    )(*arguments)


def refine_kernel(head_dim, everyone, features, messages, out_proj, ffn_in, ffn_in_bias, norm_gain,
                  norm_bias, ffn_out, ffn_out_bias, out):
    together, row_count, width = features.shape
    lanes = 2 * head_dim
    pair = pl.program_id(0)
    first_image = (lax.axis_index("img") * pl.num_programs(0) + pair) * together
    lane_side = lax.broadcasted_iota(jnp.int32, (1, lanes), 1) // head_dim
    tiles = [messages[head, 0].astype(F32) for head in range(HEADS)]
    turned = [pltpu.roll(tile, head_dim, 1) for tile in tiles]
    averaged = []
    for image in range(together):
        low, high = (tiles, turned) if image == 0 else (turned, tiles)
        inbox = jnp.concatenate(
            [jnp.where(lane_side == 0, low[head], high[head + 1]) for head in range(0, HEADS, 2)], axis=1
        )
        asked = (everyone[...] == first_image + image).astype(F32)
        degree = jnp.sum(asked, axis=1, keepdims=True)
        averaged.append((inbox / (2.0 + degree)).astype(BF16))
    averaged = jnp.concatenate(averaged, axis=0)
    projected = jnp.dot(averaged, out_proj[...], preferred_element_type=F32).astype(BF16)
    source = features[...].reshape(together * row_count, width)
    hidden = (
        jnp.dot(source.astype(BF16), ffn_in[:width], preferred_element_type=F32)
        + jnp.dot(projected, ffn_in[width:], preferred_element_type=F32)
        + ffn_in_bias[...]
    )
    hidden = hidden - jnp.mean(hidden, axis=1, keepdims=True)
    spread = jnp.mean(hidden * hidden, axis=1, keepdims=True)
    normed = hidden * lax.rsqrt(spread + 1e-05) * norm_gain[...] + norm_bias[...]
    activated = (0.5 * normed * (1.0 + lax.erf(normed * (0.5**0.5)))).astype(BF16)
    refined = source + jnp.dot(activated, ffn_out[...], preferred_element_type=F32) + ffn_out_bias[...]
    out[...] = refined.reshape(together, row_count, width)


def per_device(features, partners, counts, shared_proj, value_proj, out_proj, ffn_in, ffn_in_bias,
               norm_gain, norm_bias, ffn_out, ffn_out_bias):
    img_count = lax.axis_size("img")
    row_devices = lax.axis_size("row")
    per_dev, row_count, width = features.shape
    head_dim = width // HEADS
    blocks = range(img_count)
    swap = [(s, s ^ 1) for s in blocks]
    thick_pairs = [(s, (s + (2 if s % 2 else -2)) % img_count) for s in blocks]
    thin_pairs = [(s, (s + (-2 if s % 2 else 2)) % img_count) for s in blocks]

    weights = (shared_proj, value_proj, row_devices)
    rounded, own = project(features, *weights)
    thick = lax.ppermute(rounded, "img", thick_pairs)
    thin = lax.ppermute(rounded, "img", thin_pairs)
    flat_partners = partners.reshape(-1)

    companion = lax.ppermute(own, "img", swap)
    thick = project(thick, *weights, weigh=50)
    work = functools.partial(attend, head_dim=head_dim, counts=counts, partners=flat_partners, own=own)
    sums = work((COMPANION,), False, blocks=[companion], carried=None)
    thick = tie(thick, sums)
    cross = lax.ppermute(thick, "img", swap)
    thin = project(thin, *weights, after=(sums,), weigh=50)
    sums = work((THICK, CROSS), False, blocks=[thick, cross], carried=sums)
    messages = work((THIN,), True, blocks=[thin], carried=sums)
    messages = exchange(messages)[::row_devices // HEADS].reshape(HEADS, per_dev // 2, row_count, 2 * head_dim)

    pair = pl.BlockSpec((2, row_count, width), lambda i: (i, 0, 0))
    return pl.pallas_call(
        functools.partial(refine_kernel, head_dim),
        grid=(per_dev // 2,),
        out_shape=jax.ShapeDtypeStruct(features.shape, F32),
        in_specs=[
            whole(), pair, pl.BlockSpec((HEADS, 1, row_count, 2 * head_dim), lambda i: (0, i, 0, 0)),
        ] + [whole()] * 7,
        out_specs=pair,
        compiler_params=pltpu.CompilerParams(vmem_limit_bytes=VMEM // 3),
        cost_estimate=pl.CostEstimate(
            flops=10 * per_dev * row_count * width * width * 2, bytes_accessed=2**22, transcendentals=2**20
        ),
        name="refine",
    )(flat_partners[None], features, messages, out_proj, ffn_in, ffn_in_bias[None], norm_gain[None],
      norm_bias[None], ffn_out, ffn_out_bias[None])


def solution(mesh):
    return jax.shard_map(
        per_device,
        mesh=mesh,
        in_specs=(P("img", "row", None), P(), P(), P(), P(), P(), P(), P(), P(), P(), P(), P()),
        out_specs=P("img", "row", None),
        check_vma=False,
    )
```

```python
import functools
import math

import jax
import jax.numpy as jnp
from jax import lax
from jax.experimental import pallas as pl
from jax.experimental.pallas import tpu as pltpu
from jax.sharding import PartitionSpec as P

HEADS = 4
LEAST, MOST = 1e-25, 1e25
NEGATIVE = -1e30
VMEM = 60 * 2**20
NT = (((1,), (1,)), ((), ()))
F32 = jnp.float32
BF16 = jnp.bfloat16

COMPANION, THICK, THIN, CROSS = range(4)


def block_of(kind, me, img_count):
    odd = lax.rem(me, 2)
    ahead = 1 - 2 * odd
    step = {COMPANION: ahead, THICK: 2 * ahead, THIN: -2 * ahead, CROSS: -ahead}[kind]
    return lax.rem(me + step + img_count, img_count)


def whole(memory=pltpu.VMEM):
    return pl.BlockSpec(memory_space=memory)


def exchange(value):
    return lax.all_to_all(value, "row", split_axis=0, concat_axis=0, tiled=True)


CALLS = ((COMPANION,), (THICK, CROSS), (THIN,))


def plan_slots(per_dev):
    return max(len(kinds) for kinds in CALLS) * per_dev * per_dev + 1


def plan(counts, partners, todo):
    img_count = lax.axis_size("img")
    me = lax.axis_index("img")
    per_dev = counts.shape[0] // img_count
    slots = plan_slots(per_dev)
    for call, kinds in enumerate(CALLS):
        pairs = jnp.zeros((), jnp.int32)
        start = 4 * call * slots
        for place, kind in enumerate(kinds):
            block_id = block_of(kind, me, img_count)
            for other in range(per_dev):
                for image in range(per_dev):
                    theirs, mine = block_id * per_dev + other, me * per_dev + image
                    times = jnp.zeros((), jnp.int32)
                    for side in range(2):
                        times += (partners[2 * mine + side] == theirs).astype(jnp.int32)
                        times += (partners[2 * theirs + side] == mine).astype(jnp.int32)
                    todo[start + pairs] = place * per_dev + other
                    todo[start + slots + pairs] = image
                    todo[start + 2 * slots + pairs] = times
                    todo[start + 3 * slots + pairs] = counts[theirs]
                    pairs = pairs + (times > 0).astype(jnp.int32)
        todo[4 * len(CALLS) * slots + call] = pairs


def project_kernel(head_dim, per_dev, rounds, plans, source, shared_hbm, value_hbm, *refs):
    rows, shared_proj, value_proj, packed, came, went, *rounded = refs[-7 if rounds else -6:]
    outs = refs[:-7 if rounds else -6]
    out_hbm = outs[-1]
    if plans:
        counts, partners, todo, out_hbm = outs
    heads, flat_rows, lanes = packed.shape
    row_count = flat_rows // per_dev
    arrivals = [
        pltpu.make_async_copy(shared_hbm, shared_proj, came.at[per_dev]),
        pltpu.make_async_copy(value_hbm, value_proj, came.at[per_dev + 1]),
    ]
    pieces = [slice(image * row_count, (image + 1) * row_count) for image in range(per_dev)]
    loads = [
        pltpu.make_async_copy(source.at[piece], rows.at[piece], came.at[image])
        for image, piece in enumerate(pieces)
    ]
    for copy in arrivals + loads:
        copy.start()
    if plans:
        plan(counts, partners, todo)
    for copy in arrivals:
        copy.wait()
    low = lax.broadcasted_iota(jnp.int32, (1, lanes), 1) < head_dim
    both = []
    for pair in range(heads // 2):
        columns = slice(pair * lanes, (pair + 1) * lanes)
        turned = pltpu.roll(value_proj[:, columns].astype(F32), head_dim, 1).astype(BF16)
        both.append(jnp.concatenate([shared_proj[:, columns], turned], axis=1))
    leaving = []
    for image, piece in enumerate(pieces):
        loads[image].wait()
        value = rows[piece].astype(BF16)
        if rounds:
            rounded[0][piece] = value
            leaving.append(pltpu.make_async_copy(rounded[0].at[piece], outs[0].at[piece], went.at[1, image]))
            leaving[-1].start()
        for pair in range(heads // 2):
            projected = jnp.dot(value, both[pair], preferred_element_type=F32)
            shared, values = projected[:, :lanes], projected[:, lanes:]
            packed[2 * pair, piece] = jnp.where(low, shared, values).astype(BF16)
            packed[2 * pair + 1, piece] = jnp.where(low, values, shared).astype(BF16)
        leaving.append(pltpu.make_async_copy(packed.at[:, piece], out_hbm.at[:, piece], went.at[0, image]))
        leaving[-1].start()
    for copy in leaving:
        copy.wait()


def project(value, shared_proj, value_proj, row_devices, after=(), planned=(), weigh=1):
    per_dev, row_count, width = value.shape
    rows = per_dev * row_count
    head_dim = width // HEADS
    rounds = value.dtype == F32

    def kernel(rows_ref, shared_ref, value_ref, *refs):
        refs = refs[len(after):]
        project_kernel(head_dim, per_dev, rounds, bool(planned), rows_ref, shared_ref, value_ref, *refs)

    packed_shape = (HEADS, rows, 2 * head_dim)
    out_shapes = [jax.ShapeDtypeStruct(packed_shape, BF16)]
    scratch = [
        pltpu.VMEM((rows, width), value.dtype),
        pltpu.VMEM(shared_proj.shape, BF16),
        pltpu.VMEM(value_proj.shape, BF16),
        pltpu.VMEM(packed_shape, BF16),
        pltpu.SemaphoreType.DMA((per_dev + 2,)),
        pltpu.SemaphoreType.DMA((2, per_dev)),
    ]
    if rounds:
        out_shapes.insert(0, jax.ShapeDtypeStruct((rows, width), BF16))
        scratch.append(pltpu.VMEM((rows, width), BF16))
    out_specs = [whole(pl.ANY)] * len(out_shapes)
    if planned:
        length = 4 * len(CALLS) * plan_slots(per_dev) + len(CALLS)
        out_shapes.insert(0, jax.ShapeDtypeStruct((length,), jnp.int32))
        out_specs.insert(0, whole(pltpu.SMEM))
    *more, packed = pl.pallas_call(
        kernel,
        out_shape=out_shapes,
        in_specs=[whole(pl.ANY)] * (3 + len(after)) + [whole(pltpu.SMEM)] * len(planned),
        out_specs=out_specs,
        scratch_shapes=scratch,
        compiler_params=pltpu.CompilerParams(vmem_limit_bytes=VMEM),
        cost_estimate=pl.CostEstimate(
            flops=weigh * 4 * rows * width * width, bytes_accessed=6 * rows * width, transcendentals=0
        ),
        name="project",
    )(value.reshape(rows, width), shared_proj, value_proj, *after, *planned)
    if row_devices > HEADS:
        packed = jnp.repeat(packed, row_devices // HEADS, axis=0)
    packed = exchange(packed)
    return (*more, packed) if more else packed


def tie(value, after):
    def kernel(value_ref, after_ref, out_ref):
        pass

    return pl.pallas_call(
        kernel,
        out_shape=jax.ShapeDtypeStruct(value.shape, value.dtype),
        in_specs=[whole(pltpu.HBM)] * 2,
        out_specs=whole(pltpu.HBM),
        input_output_aliases={0: 0},
        name="tie",
    )(value, after)


def attend_kernel(call, first, last, head_dim, todo, own_hbm, *refs):
    kinds = CALLS[call]
    blocks_hbm, refs = refs[:len(kinds)], refs[len(kinds):]
    if first:
        out_hbm, own, blocks, total, limits, arrived, left = refs
    elif last:
        carried_hbm, out_hbm, own, blocks, total, limits, arrived, left, out = refs
    else:
        carried_hbm, out_hbm, own, blocks, total, limits, arrived, left = refs
    devices, flat_rows, lanes = own.shape
    halved, keypoints, _ = total.shape
    per_dev = 2 * halved
    row_count = flat_rows // per_dev
    slots = plan_slots(per_dev)
    once = max(min(512, keypoints), row_count)
    sources = once // row_count
    factor = head_dim ** (-0.5) * math.log2(math.e)

    def begin():
        if first:
            total[...] = jnp.zeros_like(total)
            return []
        copy = pltpu.make_async_copy(carried_hbm, total, left.at[halved])
        copy.start()
        return [copy]

    copies = []
    for number, (source, target) in enumerate(
        [(own_hbm, own)] + [(block, blocks.at[place]) for place, block in enumerate(blocks_hbm)]
    ):
        for device in range(devices):
            copies.append(
                pltpu.make_async_copy(source.at[device], target.at[device], arrived.at[number, device])
            )
            copies[-1].start()
    copies += begin()

    key_side = lax.rem(lax.div(lax.axis_index("row"), devices // HEADS), 2)
    lane_side = lax.broadcasted_iota(jnp.int32, (1, lanes), 1) // head_dim
    key_row = lax.broadcasted_iota(jnp.int32, (keypoints, 1), 0)
    key_lane = lax.broadcasted_iota(jnp.int32, (1, keypoints), 1)
    one, zero = jnp.ones((), BF16), jnp.zeros((), BF16)
    limits[...] = jnp.ones_like(limits)
    pairs = todo[4 * len(CALLS) * slots + call]
    for copy in copies:
        copy.wait()

    def image_rows(image):
        return pl.ds(pl.multiple_of(image * row_count, row_count), row_count)

    def operands(number):
        spot, image, times, limit = [todo[(4 * call + field) * slots + number] for field in range(4)]
        place, other = lax.div(spot, per_dev), lax.rem(spot, per_dev)
        tile = blocks[place, :, image_rows(other), :].reshape(keypoints, lanes)
        is_key, present = lane_side == key_side, key_row < limit
        keys = jnp.where(present, jnp.where(is_key, tile, zero), zero)
        values = jnp.where(present, jnp.where(is_key, one, tile), zero)
        return image, keys, values, limit, times.astype(F32)

    def score(image, start, keys):
        queries = own[start:start + sources, image_rows(image), :].reshape(once, lanes)
        return lax.dot_general(queries, keys, NT, preferred_element_type=F32)

    def add(image, start, got, times):
        rows = slice(start * row_count, start * row_count + once)
        side = lax.rem(image, 2)
        turned = pltpu.roll(got, head_dim, 1)
        stays = side != key_side
        above, below = jnp.where(stays, got, turned), jnp.where(stays, turned, got)
        share = pl.reciprocal(below, approx=True)
        share = share * (2.0 - below * share)
        total[lax.div(image, 2), rows] += jnp.where(lane_side == side, above * (share * times), 0.0)

    def fast(numbers):
        work = [operands(number) for number in numbers]
        least, most = limits[0], limits[1]
        for start in range(0, devices, sources):
            results = []
            for image, keys, values, _, times in work:
                raised = jnp.exp2(score(image, start, keys) * factor).astype(BF16)
                got = jnp.dot(raised, values, preferred_element_type=F32)
                by_row = got.reshape(once // 8, 8, lanes)
                least = jnp.minimum(least, jnp.min(by_row, axis=0))
                most = jnp.maximum(most, jnp.max(by_row, axis=0))
                results.append(got)
            for (image, _, _, _, times), got in zip(work, results):
                add(image, start, got, times)
        limits[0] = least
        limits[1] = most

    def slow(number, carry):
        image, keys, values, limit, times = operands(number)
        present = key_lane < limit
        for start in range(0, devices, sources):
            scores = score(image, start, keys)
            peak = jnp.max(jnp.where(present, scores, NEGATIVE), axis=1, keepdims=True)
            raised = jnp.where(present, jnp.exp2((scores - peak) * factor), 0.0).astype(BF16)
            add(image, start, jnp.dot(raised, values, preferred_element_type=F32), times)
        return carry

    def two(number, carry):
        fast((2 * number, 2 * number + 1))
        return carry

    lax.fori_loop(0, pairs // 2, two, 0)

    @pl.when(pairs % 2 == 1)
    def _():
        fast((pairs - 1,))

    outside = (limits[0] < LEAST) | (limits[1] > MOST)
    outside = jnp.where((lane_side == key_side) & outside, 1.0, 0.0)

    @pl.when(jnp.max(outside) > 0.5)
    def _():
        for copy in begin():
            copy.wait()
        lax.fori_loop(0, pairs, slow, 0)

    gone = []
    for pair in range(halved):
        source, place = total.at[pair], (pair,)
        if last:
            place = (slice(None), slice(pair * row_count, (pair + 1) * row_count))
            out[place] = total[pair].astype(BF16).reshape(devices, row_count, lanes)
            source = out.at[place]
        gone.append(pltpu.make_async_copy(source, out_hbm.at[place], left.at[pair]))
        gone[-1].start()
    for copy in gone:
        copy.wait()


def attend(call, per_dev, head_dim, todo, own, blocks, carried):
    devices, flat_rows, lanes = own.shape
    first, last = call == 0, call == len(CALLS) - 1
    halved = per_dev // 2
    row_count = flat_rows // (2 * halved)
    packed = (halved, devices * row_count, lanes)
    arguments = [todo, own, *blocks] + ([] if first else [carried])
    if last:
        out_shape = jax.ShapeDtypeStruct((devices, flat_rows // 2, lanes), BF16)
    else:
        out_shape = jax.ShapeDtypeStruct(packed, F32)
    scratch = [
        pltpu.VMEM(own.shape, BF16),
        pltpu.VMEM((len(blocks), *own.shape), BF16),
        pltpu.VMEM(packed, F32),
        pltpu.VMEM((2, 8, lanes), F32),
        pltpu.SemaphoreType.DMA((1 + len(blocks), devices)),
        pltpu.SemaphoreType.DMA((halved + 1,)),
    ]
    if last:
        scratch.append(pltpu.VMEM(out_shape.shape, BF16))
    area = (devices * row_count) ** 2
    return pl.pallas_call(
        functools.partial(attend_kernel, call, first, last, head_dim),
        out_shape=out_shape,
        in_specs=[whole(pltpu.SMEM)] + [whole(pltpu.HBM)] * (len(arguments) - 1),
        out_specs=whole(pltpu.HBM),
        scratch_shapes=scratch,
        compiler_params=pltpu.CompilerParams(vmem_limit_bytes=VMEM),
        cost_estimate=pl.CostEstimate(
            flops=0 if first else len(blocks) * 4 * 2 * 2 * area * 512,
            bytes_accessed=0 if first else 4 * devices * flat_rows * lanes,
            transcendentals=0 if first else len(blocks) * 4 * area,
        ),
        name=f"attend{call}",
    )(*arguments)


def refine_kernel(head_dim, everyone, features, messages, out_proj, ffn_in, ffn_in_bias, norm_gain,
                  norm_bias, ffn_out, ffn_out_bias, out):
    together, row_count, width = features.shape
    lanes = 2 * head_dim
    pair = pl.program_id(0)
    first_image = (lax.axis_index("img") * pl.num_programs(0) + pair) * together
    lane_side = lax.broadcasted_iota(jnp.int32, (1, lanes), 1) // head_dim
    tiles = [messages[head, 0].astype(F32) for head in range(HEADS)]
    turned = [pltpu.roll(tile, head_dim, 1) for tile in tiles]
    averaged = []
    for image in range(together):
        low, high = (tiles, turned) if image == 0 else (turned, tiles)
        inbox = jnp.concatenate(
            [jnp.where(lane_side == 0, low[head], high[head + 1]) for head in range(0, HEADS, 2)], axis=1
        )
        asked = (everyone[...] == first_image + image).astype(F32)
        degree = jnp.sum(asked, axis=1, keepdims=True)
        averaged.append((inbox / (2.0 + degree)).astype(BF16))
    averaged = jnp.concatenate(averaged, axis=0)
    projected = jnp.dot(averaged, out_proj[...], preferred_element_type=F32).astype(BF16)
    source = features[...].reshape(together * row_count, width)
    hidden = (
        jnp.dot(source.astype(BF16), ffn_in[:width], preferred_element_type=F32)
        + jnp.dot(projected, ffn_in[width:], preferred_element_type=F32)
        + ffn_in_bias[...]
    )
    hidden = hidden - jnp.mean(hidden, axis=1, keepdims=True)
    spread = jnp.mean(hidden * hidden, axis=1, keepdims=True)
    normed = hidden * lax.rsqrt(spread + 1e-05) * norm_gain[...] + norm_bias[...]
    activated = (0.5 * normed * (1.0 + lax.erf(normed * (0.5**0.5)))).astype(BF16)
    refined = source + jnp.dot(activated, ffn_out[...], preferred_element_type=F32) + ffn_out_bias[...]
    out[...] = refined.reshape(together, row_count, width)


def per_device(features, partners, counts, shared_proj, value_proj, out_proj, ffn_in, ffn_in_bias,
               norm_gain, norm_bias, ffn_out, ffn_out_bias):
    img_count = lax.axis_size("img")
    row_devices = lax.axis_size("row")
    per_dev, row_count, width = features.shape
    head_dim = width // HEADS
    blocks = range(img_count)
    swap = [(s, s ^ 1) for s in blocks]
    thick_pairs = [(s, (s + (2 if s % 2 else -2)) % img_count) for s in blocks]
    thin_pairs = [(s, (s + (-2 if s % 2 else 2)) % img_count) for s in blocks]

    weights = (shared_proj, value_proj, row_devices)
    rounded, own = project(features, *weights)
    rounded = rounded.reshape(features.shape)
    thick = lax.ppermute(rounded, "img", thick_pairs)
    thin = lax.ppermute(rounded, "img", thin_pairs)
    flat_partners = partners.reshape(-1)

    companion = lax.ppermute(own, "img", swap)
    todo, thick = project(thick, *weights, planned=(counts, flat_partners), weigh=50)
    sums = attend(0, per_dev, head_dim, todo, own, [companion], None)
    thick = tie(thick, sums)
    cross = lax.ppermute(thick, "img", swap)
    thin = project(thin, *weights, after=(sums,), weigh=50)
    sums = attend(1, per_dev, head_dim, todo, own, [thick, cross], sums)
    messages = attend(2, per_dev, head_dim, todo, own, [thin], sums)
    messages = exchange(messages)[::row_devices // HEADS].reshape(HEADS, per_dev // 2, row_count, 2 * head_dim)

    pair = pl.BlockSpec((2, row_count, width), lambda i: (i, 0, 0))
    return pl.pallas_call(
        functools.partial(refine_kernel, head_dim),
        grid=(per_dev // 2,),
        out_shape=jax.ShapeDtypeStruct(features.shape, F32),
        in_specs=[
            whole(), pair, pl.BlockSpec((HEADS, 1, row_count, 2 * head_dim), lambda i: (0, i, 0, 0)),
        ] + [whole()] * 7,
        out_specs=pair,
        compiler_params=pltpu.CompilerParams(vmem_limit_bytes=VMEM // 3),
        cost_estimate=pl.CostEstimate(
            flops=10 * per_dev * row_count * width * width * 2, bytes_accessed=2**22, transcendentals=2**20
        ),
        name="refine",
    )(flat_partners[None], features, messages, out_proj, ffn_in, ffn_in_bias[None], norm_gain[None],
      norm_bias[None], ffn_out, ffn_out_bias[None])


def solution(mesh):
    return jax.shard_map(
        per_device,
        mesh=mesh,
        in_specs=(P("img", "row", None), P(), P(), P(), P(), P(), P(), P(), P(), P(), P(), P()),
        out_specs=P("img", "row", None),
        check_vma=False,
    )
```

```python
import functools
import math

import jax
import jax.numpy as jnp
from jax import lax
from jax.experimental import pallas as pl
from jax.experimental.pallas import tpu as pltpu
from jax.sharding import PartitionSpec as P

HEADS = 4
LEAST, MOST = 1e-25, 1e25
NEGATIVE = -1e30
VMEM = 60 * 2**20
NT = (((1,), (1,)), ((), ()))
F32 = jnp.float32
BF16 = jnp.bfloat16

COMPANION, THICK, THIN, CROSS = range(4)


def block_of(kind, me, img_count):
    odd = lax.rem(me, 2)
    ahead = 1 - 2 * odd
    step = {COMPANION: ahead, THICK: 2 * ahead, THIN: -2 * ahead, CROSS: -ahead}[kind]
    return lax.rem(me + step + img_count, img_count)


def whole(memory=pltpu.VMEM):
    return pl.BlockSpec(memory_space=memory)


def exchange(value):
    return lax.all_to_all(value, "row", split_axis=0, concat_axis=0, tiled=True)


CALLS = ((COMPANION,), (THICK, CROSS), (THIN,))


def plan_slots(per_dev):
    return max(len(kinds) for kinds in CALLS) * per_dev * per_dev + 1


def plan(counts, partners, todo):
    img_count = lax.axis_size("img")
    me = lax.axis_index("img")
    per_dev = counts.shape[0] // img_count
    slots = plan_slots(per_dev)
    for call, kinds in enumerate(CALLS):
        pairs = jnp.zeros((), jnp.int32)
        start = 4 * call * slots
        for place, kind in enumerate(kinds):
            block_id = block_of(kind, me, img_count)
            for other in range(per_dev):
                for image in range(per_dev):
                    theirs, mine = block_id * per_dev + other, me * per_dev + image
                    times = jnp.zeros((), jnp.int32)
                    for side in range(2):
                        times += (partners[2 * mine + side] == theirs).astype(jnp.int32)
                        times += (partners[2 * theirs + side] == mine).astype(jnp.int32)
                    todo[start + pairs] = place * per_dev + other
                    todo[start + slots + pairs] = image
                    todo[start + 2 * slots + pairs] = times
                    todo[start + 3 * slots + pairs] = counts[theirs]
                    pairs = pairs + (times > 0).astype(jnp.int32)
        todo[4 * len(CALLS) * slots + call] = pairs


def joined_weights(shared_proj, value_proj, lanes):
    both = []
    for start in range(0, shared_proj.shape[1], lanes):
        columns = slice(start, start + lanes)
        turned = pltpu.roll(value_proj[:, columns].astype(F32), lanes // 2, 1).astype(BF16)
        both.append(jnp.concatenate([shared_proj[:, columns], turned], axis=1))
    return both


def pack(head_dim, value, both, out, piece):
    lanes = 2 * head_dim
    low = lax.broadcasted_iota(jnp.int32, (1, lanes), 1) < head_dim
    for pair, weight in enumerate(both):
        projected = jnp.dot(value, weight, preferred_element_type=F32)
        shared, values = projected[:, :lanes], projected[:, lanes:]
        out[2 * pair, piece] = jnp.where(low, shared, values).astype(BF16)
        out[2 * pair + 1, piece] = jnp.where(low, values, shared).astype(BF16)


def project_kernel(head_dim, rows, shared_proj, value_proj, after, out):
    both = joined_weights(shared_proj, value_proj, 2 * head_dim)
    pack(head_dim, rows[...], both, out, slice(None))


def open_kernel(head_dim, per_dev, source, shared_hbm, value_hbm, rounded_hbm, out_hbm, rows, shared_proj,
                value_proj, packed, came, went, rounded):
    heads, flat_rows, lanes = packed.shape
    row_count = flat_rows // per_dev
    arrivals = [
        pltpu.make_async_copy(shared_hbm, shared_proj, came.at[per_dev]),
        pltpu.make_async_copy(value_hbm, value_proj, came.at[per_dev + 1]),
    ]
    pieces = [slice(image * row_count, (image + 1) * row_count) for image in range(per_dev)]
    loads = [
        pltpu.make_async_copy(source.at[piece], rows.at[piece], came.at[image])
        for image, piece in enumerate(pieces)
    ]
    for copy in arrivals + loads:
        copy.start()
    for copy in arrivals:
        copy.wait()
    both = joined_weights(shared_proj, value_proj, lanes)
    leaving = []
    for image, piece in enumerate(pieces):
        loads[image].wait()
        value = rows[piece].astype(BF16)
        rounded[piece] = value
        leaving.append(pltpu.make_async_copy(rounded.at[piece], rounded_hbm.at[piece], went.at[1, image]))
        leaving[-1].start()
        pack(head_dim, value, both, packed, piece)
        leaving.append(pltpu.make_async_copy(packed.at[:, piece], out_hbm.at[:, piece], went.at[0, image]))
        leaving[-1].start()
    for copy in leaving:
        copy.wait()


def spread(packed, row_devices):
    if row_devices > HEADS:
        packed = jnp.repeat(packed, row_devices // HEADS, axis=0)
    return exchange(packed)


def project_cost(rows, width, weigh):
    return pl.CostEstimate(
        flops=weigh * 4 * rows * width * width, bytes_accessed=6 * rows * width, transcendentals=0
    )


def begin(features, shared_proj, value_proj):
    per_dev, row_count, width = features.shape
    rows = per_dev * row_count
    head_dim = width // HEADS
    packed_shape = (HEADS, rows, 2 * head_dim)
    rounded, packed = pl.pallas_call(
        functools.partial(open_kernel, head_dim, per_dev),
        out_shape=(jax.ShapeDtypeStruct((rows, width), BF16), jax.ShapeDtypeStruct(packed_shape, BF16)),
        in_specs=[whole(pl.ANY)] * 3,
        out_specs=(whole(pl.ANY),) * 2,
        scratch_shapes=[
            pltpu.VMEM((rows, width), F32),
            pltpu.VMEM(shared_proj.shape, BF16),
            pltpu.VMEM(value_proj.shape, BF16),
            pltpu.VMEM(packed_shape, BF16),
            pltpu.SemaphoreType.DMA((per_dev + 2,)),
            pltpu.SemaphoreType.DMA((2, per_dev)),
            pltpu.VMEM((rows, width), BF16),
        ],
        compiler_params=pltpu.CompilerParams(vmem_limit_bytes=VMEM),
        cost_estimate=project_cost(rows, width, 1),
        name="begin",
    )(features.reshape(rows, width), shared_proj, value_proj)
    return rounded.reshape(features.shape), packed


def project(value, shared_proj, value_proj, after):
    per_dev, row_count, width = value.shape
    rows = per_dev * row_count
    head_dim = width // HEADS
    waits = pltpu.SMEM if after.dtype == jnp.int32 else pl.ANY
    return pl.pallas_call(
        functools.partial(project_kernel, head_dim),
        out_shape=jax.ShapeDtypeStruct((HEADS, rows, 2 * head_dim), BF16),
        in_specs=[whole()] * 3 + [whole(waits)],
        out_specs=whole(),
        compiler_params=pltpu.CompilerParams(vmem_limit_bytes=VMEM // 4),
        cost_estimate=project_cost(rows, width, 50),
        name="project",
    )(value.reshape(rows, width), shared_proj, value_proj, after)


def make_plan(counts, partners, per_dev):
    length = 4 * len(CALLS) * plan_slots(per_dev) + len(CALLS)
    return pl.pallas_call(
        plan,
        out_shape=jax.ShapeDtypeStruct((length,), jnp.int32),
        in_specs=[whole(pltpu.SMEM)] * 2,
        out_specs=whole(pltpu.SMEM),
        name="plan",
    )(counts, partners)


def tie(value, after):
    def kernel(value_ref, after_ref, out_ref):
        pass

    return pl.pallas_call(
        kernel,
        out_shape=jax.ShapeDtypeStruct(value.shape, value.dtype),
        in_specs=[whole(pltpu.HBM)] * 2,
        out_specs=whole(pltpu.HBM),
        input_output_aliases={0: 0},
        name="tie",
    )(value, after)


def attend_kernel(call, first, last, head_dim, todo, own_hbm, *refs):
    kinds = CALLS[call]
    blocks_hbm, refs = refs[:len(kinds)], refs[len(kinds):]
    if first:
        out_hbm, own, blocks, total, limits, seen, arrived, left = refs
    elif last:
        carried_hbm, out_hbm, own, blocks, total, limits, seen, arrived, left, out = refs
    else:
        carried_hbm, out_hbm, own, blocks, total, limits, seen, arrived, left = refs
    devices, flat_rows, lanes = own.shape
    halved, keypoints, _ = total.shape
    per_dev = 2 * halved
    row_count = flat_rows // per_dev
    slots = plan_slots(per_dev)
    once = max(min(512, keypoints), row_count)
    sources = once // row_count
    factor = head_dim ** (-0.5) * math.log2(math.e)

    def image_rows(image):
        return pl.ds(pl.multiple_of(image * row_count, row_count), row_count)

    def start_totals():
        if first:
            total[...] = jnp.zeros_like(total)
            return []
        copy = pltpu.make_async_copy(carried_hbm, total, left.at[halved])
        copy.start()
        return [copy]

    def block_copy(source, place, other, spot):
        rows = image_rows(other)
        return pltpu.make_async_copy(source.at[:, rows], blocks.at[place, :, rows], arrived.at[devices + spot])

    copies = []
    for device in range(devices):
        copies.append(pltpu.make_async_copy(own_hbm.at[device], own.at[device], arrived.at[device]))
        copies[-1].start()
    for place, source in enumerate(blocks_hbm):
        for other in range(per_dev):
            block_copy(source, place, other, place * per_dev + other).start()
            if place + other == 0:
                copies += start_totals()
    seen[0] = 0

    def need(spots):
        def one(spot, carry):
            block_copy(blocks_hbm[0], 0, 0, spot).wait()
            return carry

        lax.fori_loop(seen[0], spots, one, 0)
        seen[0] = jnp.maximum(seen[0], spots)

    key_side = lax.rem(lax.div(lax.axis_index("row"), devices // HEADS), 2)
    lane_side = lax.broadcasted_iota(jnp.int32, (1, lanes), 1) // head_dim
    key_row = lax.broadcasted_iota(jnp.int32, (keypoints, 1), 0)
    key_lane = lax.broadcasted_iota(jnp.int32, (1, keypoints), 1)
    one, zero = jnp.ones((), BF16), jnp.zeros((), BF16)
    limits[...] = jnp.ones_like(limits)
    pairs = todo[4 * len(CALLS) * slots + call]
    for copy in copies:
        copy.wait()

    def operands(number):
        spot, image, times, limit = [todo[(4 * call + field) * slots + number] for field in range(4)]
        place, other = lax.div(spot, per_dev), lax.rem(spot, per_dev)
        tile = blocks[place, :, image_rows(other), :].reshape(keypoints, lanes)
        is_key, present = lane_side == key_side, key_row < limit
        keys = jnp.where(present, jnp.where(is_key, tile, zero), zero)
        values = jnp.where(present, jnp.where(is_key, one, tile), zero)
        return image, keys, values, limit, times.astype(F32)

    def score(image, start, keys):
        queries = own[start:start + sources, image_rows(image), :].reshape(once, lanes)
        return lax.dot_general(queries, keys, NT, preferred_element_type=F32)

    def add(image, start, got, times):
        rows = slice(start * row_count, start * row_count + once)
        side = lax.rem(image, 2)
        turned = pltpu.roll(got, head_dim, 1)
        stays = side != key_side
        above, below = jnp.where(stays, got, turned), jnp.where(stays, turned, got)
        share = pl.reciprocal(below, approx=True)
        share = share * (2.0 - below * share)
        total[lax.div(image, 2), rows] += jnp.where(lane_side == side, above * (share * times), 0.0)

    def fast(numbers):
        need(todo[4 * call * slots + numbers[-1]] + 1)
        work = [operands(number) for number in numbers]
        least, most = limits[0], limits[1]
        for start in range(0, devices, sources):
            results = []
            for image, keys, values, _, times in work:
                raised = jnp.exp2(score(image, start, keys) * factor).astype(BF16)
                got = jnp.dot(raised, values, preferred_element_type=F32)
                by_row = got.reshape(once // 8, 8, lanes)
                least = jnp.minimum(least, jnp.min(by_row, axis=0))
                most = jnp.maximum(most, jnp.max(by_row, axis=0))
                results.append(got)
            for (image, _, _, _, times), got in zip(work, results):
                add(image, start, got, times)
        limits[0] = least
        limits[1] = most

    def slow(number, carry):
        image, keys, values, limit, times = operands(number)
        present = key_lane < limit
        for start in range(0, devices, sources):
            scores = score(image, start, keys)
            peak = jnp.max(jnp.where(present, scores, NEGATIVE), axis=1, keepdims=True)
            raised = jnp.where(present, jnp.exp2((scores - peak) * factor), 0.0).astype(BF16)
            add(image, start, jnp.dot(raised, values, preferred_element_type=F32), times)
        return carry

    def four(number, carry):
        fast([4 * number + pair for pair in range(4)])
        return carry

    lax.fori_loop(0, pairs // 4, four, 0)
    done = pairs // 4 * 4

    @pl.when(pairs % 4 >= 2)
    def _():
        fast([done, done + 1])

    @pl.when(pairs % 2 == 1)
    def _():
        fast([pairs - 1])

    need(len(kinds) * per_dev)
    outside = (limits[0] < LEAST) | (limits[1] > MOST)
    outside = jnp.where((lane_side == key_side) & outside, 1.0, 0.0)

    @pl.when(jnp.max(outside) > 0.5)
    def _():
        for copy in start_totals():
            copy.wait()
        lax.fori_loop(0, pairs, slow, 0)

    gone = []
    for pair in range(halved):
        source, place = total.at[pair], (pair,)
        if last:
            place = (slice(None), slice(pair * row_count, (pair + 1) * row_count))
            out[place] = total[pair].astype(BF16).reshape(devices, row_count, lanes)
            source = out.at[place]
        gone.append(pltpu.make_async_copy(source, out_hbm.at[place], left.at[pair]))
        gone[-1].start()
    for copy in gone:
        copy.wait()


def attend(call, per_dev, head_dim, todo, own, blocks, carried):
    devices, flat_rows, lanes = own.shape
    first, last = call == 0, call == len(CALLS) - 1
    halved = per_dev // 2
    row_count = flat_rows // (2 * halved)
    packed = (halved, devices * row_count, lanes)
    arguments = [todo, own, *blocks] + ([] if first else [carried])
    if last:
        out_shape = jax.ShapeDtypeStruct((devices, flat_rows // 2, lanes), BF16)
    else:
        out_shape = jax.ShapeDtypeStruct(packed, F32)
    scratch = [
        pltpu.VMEM(own.shape, BF16),
        pltpu.VMEM((len(blocks), *own.shape), BF16),
        pltpu.VMEM(packed, F32),
        pltpu.VMEM((2, 8, lanes), F32),
        pltpu.SMEM((1,), jnp.int32),
        pltpu.SemaphoreType.DMA((devices + len(blocks) * per_dev,)),
        pltpu.SemaphoreType.DMA((halved + 1,)),
    ]
    if last:
        scratch.append(pltpu.VMEM(out_shape.shape, BF16))
    area = (devices * row_count) ** 2
    return pl.pallas_call(
        functools.partial(attend_kernel, call, first, last, head_dim),
        out_shape=out_shape,
        in_specs=[whole(pltpu.SMEM)] + [whole(pltpu.HBM)] * (len(arguments) - 1),
        out_specs=whole(pltpu.HBM),
        scratch_shapes=scratch,
        compiler_params=pltpu.CompilerParams(vmem_limit_bytes=VMEM),
        cost_estimate=pl.CostEstimate(
            flops=0 if first else len(blocks) * 4 * 2 * 2 * area * 512,
            bytes_accessed=0 if first else 4 * devices * flat_rows * lanes,
            transcendentals=0 if first else len(blocks) * 4 * area,
        ),
        name=f"attend{call}",
    )(*arguments)


def refine_kernel(head_dim, everyone, features, messages, out_proj, ffn_in, ffn_in_bias, norm_gain,
                  norm_bias, ffn_out, ffn_out_bias, out):
    together, row_count, width = features.shape
    lanes = 2 * head_dim
    pair = pl.program_id(0)
    first_image = (lax.axis_index("img") * pl.num_programs(0) + pair) * together
    lane_side = lax.broadcasted_iota(jnp.int32, (1, lanes), 1) // head_dim
    tiles = [messages[head, 0].astype(F32) for head in range(HEADS)]
    turned = [pltpu.roll(tile, head_dim, 1) for tile in tiles]
    averaged = []
    for image in range(together):
        low, high = (tiles, turned) if image == 0 else (turned, tiles)
        inbox = jnp.concatenate(
            [jnp.where(lane_side == 0, low[head], high[head + 1]) for head in range(0, HEADS, 2)], axis=1
        )
        asked = (everyone[...] == first_image + image).astype(F32)
        degree = jnp.sum(asked, axis=1, keepdims=True)
        averaged.append((inbox / (2.0 + degree)).astype(BF16))
    averaged = jnp.concatenate(averaged, axis=0)
    projected = jnp.dot(averaged, out_proj[...], preferred_element_type=F32).astype(BF16)
    source = features[...].reshape(together * row_count, width)
    hidden = (
        jnp.dot(source.astype(BF16), ffn_in[:width], preferred_element_type=F32)
        + jnp.dot(projected, ffn_in[width:], preferred_element_type=F32)
        + ffn_in_bias[...]
    )
    hidden = hidden - jnp.mean(hidden, axis=1, keepdims=True)
    spread = jnp.mean(hidden * hidden, axis=1, keepdims=True)
    normed = hidden * lax.rsqrt(spread + 1e-05) * norm_gain[...] + norm_bias[...]
    activated = (0.5 * normed * (1.0 + lax.erf(normed * (0.5**0.5)))).astype(BF16)
    refined = source + jnp.dot(activated, ffn_out[...], preferred_element_type=F32) + ffn_out_bias[...]
    out[...] = refined.reshape(together, row_count, width)


def per_device(features, partners, counts, shared_proj, value_proj, out_proj, ffn_in, ffn_in_bias,
               norm_gain, norm_bias, ffn_out, ffn_out_bias):
    img_count = lax.axis_size("img")
    row_devices = lax.axis_size("row")
    per_dev, row_count, width = features.shape
    head_dim = width // HEADS
    blocks = range(img_count)
    swap = [(s, s ^ 1) for s in blocks]
    thick_pairs = [(s, (s + (2 if s % 2 else -2)) % img_count) for s in blocks]
    thin_pairs = [(s, (s + (-2 if s % 2 else 2)) % img_count) for s in blocks]

    rounded, own = begin(features, shared_proj, value_proj)
    own = spread(own, row_devices)
    thick = lax.ppermute(rounded, "img", thick_pairs)
    thin = lax.ppermute(rounded, "img", thin_pairs)
    flat_partners = partners.reshape(-1)

    companion = lax.ppermute(own, "img", swap)
    todo = make_plan(counts, flat_partners, per_dev)
    thick = spread(project(thick, shared_proj, value_proj, todo), row_devices)
    sums = attend(0, per_dev, head_dim, todo, own, [companion], None)
    thick = tie(thick, sums)
    cross = lax.ppermute(thick, "img", swap)
    thin = spread(project(thin, shared_proj, value_proj, sums), row_devices)
    sums = attend(1, per_dev, head_dim, todo, own, [thick, cross], sums)
    messages = attend(2, per_dev, head_dim, todo, own, [thin], sums)
    messages = exchange(messages)[::row_devices // HEADS].reshape(HEADS, per_dev // 2, row_count, 2 * head_dim)

    pair = pl.BlockSpec((2, row_count, width), lambda i: (i, 0, 0))
    return pl.pallas_call(
        functools.partial(refine_kernel, head_dim),
        grid=(per_dev // 2,),
        out_shape=jax.ShapeDtypeStruct(features.shape, F32),
        in_specs=[
            whole(), pair, pl.BlockSpec((HEADS, 1, row_count, 2 * head_dim), lambda i: (0, i, 0, 0)),
        ] + [whole()] * 7,
        out_specs=pair,
        compiler_params=pltpu.CompilerParams(vmem_limit_bytes=VMEM // 3),
        cost_estimate=pl.CostEstimate(
            flops=10 * per_dev * row_count * width * width * 2, bytes_accessed=2**22, transcendentals=2**20
        ),
        name="refine",
    )(flat_partners[None], features, messages, out_proj, ffn_in, ffn_in_bias[None], norm_gain[None],
      norm_bias[None], ffn_out, ffn_out_bias[None])


def solution(mesh):
    return jax.shard_map(
        per_device,
        mesh=mesh,
        in_specs=(P("img", "row", None), P(), P(), P(), P(), P(), P(), P(), P(), P(), P(), P()),
        out_specs=P("img", "row", None),
        check_vma=False,
    )
```

```python
import functools
import math

import jax
import jax.numpy as jnp
from jax import lax
from jax.experimental import pallas as pl
from jax.experimental.pallas import tpu as pltpu
from jax.sharding import PartitionSpec as P

HEADS = 4
LEAST, MOST = 1e-25, 1e25
NEGATIVE = -1e30
VMEM = 60 * 2**20
NT = (((1,), (1,)), ((), ()))
F32 = jnp.float32
BF16 = jnp.bfloat16

COMPANION, THICK, THIN, CROSS = range(4)


def block_of(kind, me, img_count):
    odd = lax.rem(me, 2)
    ahead = 1 - 2 * odd
    step = {COMPANION: ahead, THICK: 2 * ahead, THIN: -2 * ahead, CROSS: -ahead}[kind]
    return lax.rem(me + step + img_count, img_count)


def whole(memory=pltpu.VMEM):
    return pl.BlockSpec(memory_space=memory)


def exchange(value):
    return lax.all_to_all(value, "row", split_axis=0, concat_axis=0, tiled=True)


CALLS = ((COMPANION,), (THICK, CROSS), (THIN,))


def plan_slots(per_dev):
    return max(len(kinds) for kinds in CALLS) * per_dev * per_dev + 1


def plan(counts, partners, todo):
    img_count = lax.axis_size("img")
    me = lax.axis_index("img")
    per_dev = counts.shape[0] // img_count
    slots = plan_slots(per_dev)
    for call, kinds in enumerate(CALLS):
        pairs = jnp.zeros((), jnp.int32)
        start = 4 * call * slots
        for place, kind in enumerate(kinds):
            block_id = block_of(kind, me, img_count)
            for other in range(per_dev):
                for image in range(per_dev):
                    theirs, mine = block_id * per_dev + other, me * per_dev + image
                    times = jnp.zeros((), jnp.int32)
                    for side in range(2):
                        times += (partners[2 * mine + side] == theirs).astype(jnp.int32)
                        times += (partners[2 * theirs + side] == mine).astype(jnp.int32)
                    todo[start + pairs] = place * per_dev + other
                    todo[start + slots + pairs] = image
                    todo[start + 2 * slots + pairs] = times
                    todo[start + 3 * slots + pairs] = counts[theirs]
                    pairs = pairs + (times > 0).astype(jnp.int32)
        todo[4 * len(CALLS) * slots + call] = pairs


def joined_weights(shared_proj, value_proj, lanes):
    both = []
    for start in range(0, shared_proj.shape[1], lanes):
        columns = slice(start, start + lanes)
        turned = pltpu.roll(value_proj[:, columns].astype(F32), lanes // 2, 1).astype(BF16)
        both.append(jnp.concatenate([shared_proj[:, columns], turned], axis=1))
    return both


def pack(head_dim, value, both, out, piece):
    lanes = 2 * head_dim
    low = lax.broadcasted_iota(jnp.int32, (1, lanes), 1) < head_dim
    for pair, weight in enumerate(both):
        projected = jnp.dot(value, weight, preferred_element_type=F32)
        shared, values = projected[:, :lanes], projected[:, lanes:]
        out[2 * pair, piece] = jnp.where(low, shared, values).astype(BF16)
        out[2 * pair + 1, piece] = jnp.where(low, values, shared).astype(BF16)


def project_kernel(head_dim, rows, shared_proj, value_proj, after, out):
    both = joined_weights(shared_proj, value_proj, 2 * head_dim)
    pack(head_dim, rows[...], both, out, slice(None))


def open_kernel(head_dim, per_dev, source, shared_hbm, value_hbm, rounded_hbm, out_hbm, rows, shared_proj,
                value_proj, packed, came, went, rounded):
    heads, flat_rows, lanes = packed.shape
    row_count = flat_rows // per_dev
    arrivals = [
        pltpu.make_async_copy(shared_hbm, shared_proj, came.at[per_dev]),
        pltpu.make_async_copy(value_hbm, value_proj, came.at[per_dev + 1]),
    ]
    pieces = [slice(image * row_count, (image + 1) * row_count) for image in range(per_dev)]
    loads = [
        pltpu.make_async_copy(source.at[piece], rows.at[piece], came.at[image])
        for image, piece in enumerate(pieces)
    ]
    for copy in arrivals + loads:
        copy.start()
    for copy in arrivals:
        copy.wait()
    both = joined_weights(shared_proj, value_proj, lanes)
    leaving = []
    for image, piece in enumerate(pieces):
        loads[image].wait()
        value = rows[piece].astype(BF16)
        rounded[piece] = value
        leaving.append(pltpu.make_async_copy(rounded.at[piece], rounded_hbm.at[piece], went.at[1, image]))
        leaving[-1].start()
        pack(head_dim, value, both, packed, piece)
        leaving.append(pltpu.make_async_copy(packed.at[:, piece], out_hbm.at[:, piece], went.at[0, image]))
        leaving[-1].start()
    for copy in leaving:
        copy.wait()


def spread(packed, row_devices):
    if row_devices > HEADS:
        packed = jnp.repeat(packed, row_devices // HEADS, axis=0)
    return exchange(packed)


def project_cost(rows, width, weigh):
    return pl.CostEstimate(
        flops=weigh * 4 * rows * width * width, bytes_accessed=6 * rows * width, transcendentals=0
    )


def begin(features, shared_proj, value_proj):
    per_dev, row_count, width = features.shape
    rows = per_dev * row_count
    head_dim = width // HEADS
    packed_shape = (HEADS, rows, 2 * head_dim)
    rounded, packed = pl.pallas_call(
        functools.partial(open_kernel, head_dim, per_dev),
        out_shape=(jax.ShapeDtypeStruct((rows, width), BF16), jax.ShapeDtypeStruct(packed_shape, BF16)),
        in_specs=[whole(pl.ANY)] * 3,
        out_specs=(whole(pl.ANY),) * 2,
        scratch_shapes=[
            pltpu.VMEM((rows, width), F32),
            pltpu.VMEM(shared_proj.shape, BF16),
            pltpu.VMEM(value_proj.shape, BF16),
            pltpu.VMEM(packed_shape, BF16),
            pltpu.SemaphoreType.DMA((per_dev + 2,)),
            pltpu.SemaphoreType.DMA((2, per_dev)),
            pltpu.VMEM((rows, width), BF16),
        ],
        compiler_params=pltpu.CompilerParams(vmem_limit_bytes=VMEM),
        cost_estimate=project_cost(rows, width, 1),
        name="begin",
    )(features.reshape(rows, width), shared_proj, value_proj)
    return rounded.reshape(features.shape), packed


def project(value, shared_proj, value_proj, after):
    per_dev, row_count, width = value.shape
    rows = per_dev * row_count
    head_dim = width // HEADS
    waits = pltpu.SMEM if after.dtype == jnp.int32 else pl.ANY
    return pl.pallas_call(
        functools.partial(project_kernel, head_dim),
        out_shape=jax.ShapeDtypeStruct((HEADS, rows, 2 * head_dim), BF16),
        in_specs=[whole()] * 3 + [whole(waits)],
        out_specs=whole(),
        compiler_params=pltpu.CompilerParams(vmem_limit_bytes=VMEM // 4),
        cost_estimate=project_cost(rows, width, 50),
        name="project",
    )(value.reshape(rows, width), shared_proj, value_proj, after)


def make_plan(counts, partners, per_dev):
    length = 4 * len(CALLS) * plan_slots(per_dev) + len(CALLS)
    return pl.pallas_call(
        plan,
        out_shape=jax.ShapeDtypeStruct((length,), jnp.int32),
        in_specs=[whole(pltpu.SMEM)] * 2,
        out_specs=whole(pltpu.SMEM),
        name="plan",
    )(counts, partners)


def tie(value, after):
    def kernel(value_ref, after_ref, out_ref):
        pass

    return pl.pallas_call(
        kernel,
        out_shape=jax.ShapeDtypeStruct(value.shape, value.dtype),
        in_specs=[whole(pltpu.HBM)] * 2,
        out_specs=whole(pltpu.HBM),
        input_output_aliases={0: 0},
        name="tie",
    )(value, after)


def attend_kernel(call, first, last, head_dim, todo, own_hbm, *refs):
    kinds = CALLS[call]
    blocks_hbm, refs = refs[:len(kinds)], refs[len(kinds):]
    if not first:
        carried_hbm, refs = refs[0], refs[1:]
    outs_hbm, refs = refs[:HEADS if last else 1], refs[HEADS if last else 1:]
    own, blocks, total, limits, seen, arrived, left, *out = refs
    out = out[0] if last else None
    devices, flat_rows, lanes = own.shape
    halved, keypoints, _ = total.shape
    per_dev = 2 * halved
    row_count = flat_rows // per_dev
    slots = plan_slots(per_dev)
    once = max(min(512, keypoints), row_count)
    sources = once // row_count
    factor = head_dim ** (-0.5) * math.log2(math.e)

    def image_rows(image):
        return pl.ds(pl.multiple_of(image * row_count, row_count), row_count)

    def start_totals():
        if first:
            total[...] = jnp.zeros_like(total)
            return []
        copy = pltpu.make_async_copy(carried_hbm, total, left.at[halved * HEADS])
        copy.start()
        return [copy]

    def block_copy(source, place, other, spot):
        rows = image_rows(other)
        return pltpu.make_async_copy(source.at[:, rows], blocks.at[place, :, rows], arrived.at[devices + spot])

    copies = []
    for device in range(devices):
        copies.append(pltpu.make_async_copy(own_hbm.at[device], own.at[device], arrived.at[device]))
        copies[-1].start()
    for place, source in enumerate(blocks_hbm):
        for other in range(per_dev):
            block_copy(source, place, other, place * per_dev + other).start()
            if place + other == 0:
                copies += start_totals()
    seen[0] = 0

    def need(spots):
        def one(spot, carry):
            block_copy(blocks_hbm[0], 0, 0, spot).wait()
            return carry

        lax.fori_loop(seen[0], spots, one, 0)
        seen[0] = jnp.maximum(seen[0], spots)

    key_side = lax.rem(lax.div(lax.axis_index("row"), devices // HEADS), 2)
    lane_side = lax.broadcasted_iota(jnp.int32, (1, lanes), 1) // head_dim
    key_row = lax.broadcasted_iota(jnp.int32, (keypoints, 1), 0)
    key_lane = lax.broadcasted_iota(jnp.int32, (1, keypoints), 1)
    one, zero = jnp.ones((), BF16), jnp.zeros((), BF16)
    limits[...] = jnp.ones_like(limits)
    pairs = todo[4 * len(CALLS) * slots + call]
    for copy in copies:
        copy.wait()

    def operands(number):
        spot, image, times, limit = [todo[(4 * call + field) * slots + number] for field in range(4)]
        place, other = lax.div(spot, per_dev), lax.rem(spot, per_dev)
        tile = blocks[place, :, image_rows(other), :].reshape(keypoints, lanes)
        is_key, present = lane_side == key_side, key_row < limit
        keys = jnp.where(present, jnp.where(is_key, tile, zero), zero)
        values = jnp.where(present, jnp.where(is_key, one, tile), zero)
        return image, keys, values, limit, times.astype(F32)

    def score(image, start, keys):
        queries = own[start:start + sources, image_rows(image), :].reshape(once, lanes)
        return lax.dot_general(queries, keys, NT, preferred_element_type=F32)

    def add(image, start, got, times):
        rows = slice(start * row_count, start * row_count + once)
        side = lax.rem(image, 2)
        turned = pltpu.roll(got, head_dim, 1)
        stays = side != key_side
        above, below = jnp.where(stays, got, turned), jnp.where(stays, turned, got)
        share = pl.reciprocal(below, approx=True)
        share = share * (2.0 - below * share)
        total[lax.div(image, 2), rows] += jnp.where(lane_side == side, above * (share * times), 0.0)

    def fast(numbers):
        need(todo[4 * call * slots + numbers[-1]] + 1)
        work = [operands(number) for number in numbers]
        least, most = limits[0], limits[1]
        for start in range(0, devices, sources):
            results = []
            for image, keys, values, _, times in work:
                raised = jnp.exp2(score(image, start, keys) * factor).astype(BF16)
                got = jnp.dot(raised, values, preferred_element_type=F32)
                by_row = got.reshape(once // 8, 8, lanes)
                least = jnp.minimum(least, jnp.min(by_row, axis=0))
                most = jnp.maximum(most, jnp.max(by_row, axis=0))
                results.append(got)
            for (image, _, _, _, times), got in zip(work, results):
                add(image, start, got, times)
        limits[0] = least
        limits[1] = most

    def slow(number, carry):
        image, keys, values, limit, times = operands(number)
        present = key_lane < limit
        for start in range(0, devices, sources):
            scores = score(image, start, keys)
            peak = jnp.max(jnp.where(present, scores, NEGATIVE), axis=1, keepdims=True)
            raised = jnp.where(present, jnp.exp2((scores - peak) * factor), 0.0).astype(BF16)
            add(image, start, jnp.dot(raised, values, preferred_element_type=F32), times)
        return carry

    def two(number, carry):
        fast([2 * number, 2 * number + 1])
        return carry

    lax.fori_loop(0, pairs // 2, two, 0)

    @pl.when(pairs % 2 == 1)
    def _():
        fast([pairs - 1])

    need(len(kinds) * per_dev)
    outside = (limits[0] < LEAST) | (limits[1] > MOST)
    outside = jnp.where((lane_side == key_side) & outside, 1.0, 0.0)

    @pl.when(jnp.max(outside) > 0.5)
    def _():
        for copy in start_totals():
            copy.wait()
        lax.fori_loop(0, pairs, slow, 0)

    gone = []
    if last:
        shift = devices // HEADS
        for number, target in enumerate(outs_hbm):
            rows = image_rows(lax.axis_index("row") ^ (number * shift))
            for pair in range(halved):
                out[number, pair] = total[pair, rows].astype(BF16)
            gone.append(pltpu.make_async_copy(out.at[number], target, left.at[number]))
            gone[-1].start()
    else:
        for pair in range(halved):
            for number in range(HEADS):
                rows = slice(number * keypoints // HEADS, (number + 1) * keypoints // HEADS)
                place = left.at[pair * HEADS + number]
                gone.append(pltpu.make_async_copy(total.at[pair, rows], outs_hbm[0].at[pair, rows], place))
                gone[-1].start()
    for copy in gone:
        copy.wait()


def attend(call, per_dev, head_dim, todo, own, blocks, carried):
    devices, flat_rows, lanes = own.shape
    first, last = call == 0, call == len(CALLS) - 1
    halved = per_dev // 2
    row_count = flat_rows // (2 * halved)
    packed = (halved, devices * row_count, lanes)
    arguments = [todo, own, *blocks] + ([] if first else [carried])
    if last:
        out_shape = (jax.ShapeDtypeStruct((halved, row_count, lanes), BF16),) * HEADS
    else:
        out_shape = (jax.ShapeDtypeStruct(packed, F32),)
    scratch = [
        pltpu.VMEM(own.shape, BF16),
        pltpu.VMEM((len(blocks), *own.shape), BF16),
        pltpu.VMEM(packed, F32),
        pltpu.VMEM((2, 8, lanes), F32),
        pltpu.SMEM((1,), jnp.int32),
        pltpu.SemaphoreType.DMA((devices + len(blocks) * per_dev,)),
        pltpu.SemaphoreType.DMA((halved * HEADS + 1,)),
    ]
    if last:
        scratch.append(pltpu.VMEM((HEADS, halved, row_count, lanes), BF16))
    area = (devices * row_count) ** 2
    return pl.pallas_call(
        functools.partial(attend_kernel, call, first, last, head_dim),
        out_shape=out_shape,
        in_specs=[whole(pltpu.SMEM)] + [whole(pltpu.HBM)] * (len(arguments) - 1),
        out_specs=(whole(pltpu.HBM),) * len(out_shape),
        scratch_shapes=scratch,
        compiler_params=pltpu.CompilerParams(vmem_limit_bytes=VMEM),
        cost_estimate=pl.CostEstimate(
            flops=0 if first else len(blocks) * 4 * 2 * 2 * area * 512,
            bytes_accessed=0 if first else 4 * devices * flat_rows * lanes,
            transcendentals=0 if first else len(blocks) * 4 * area,
        ),
        name=f"attend{call}",
    )(*arguments)


def refine_kernel(head_dim, shift, everyone, features, *refs):
    messages, refs = refs[:HEADS], refs[HEADS:]
    out_proj, ffn_in, ffn_in_bias, norm_gain, norm_bias, ffn_out, ffn_out_bias, out, by_head = refs
    together, row_count, width = features.shape
    lanes = 2 * head_dim
    pair = pl.program_id(0)
    first_image = (lax.axis_index("img") * pl.num_programs(0) + pair) * together
    lane_side = lax.broadcasted_iota(jnp.int32, (1, lanes), 1) // head_dim
    for number, message in enumerate(messages):
        by_head[lax.div(lax.axis_index("row"), shift) ^ number] = message[0].astype(F32)
    tiles = [by_head[head] for head in range(HEADS)]
    turned = [pltpu.roll(tile, head_dim, 1) for tile in tiles]
    averaged = []
    for image in range(together):
        low, high = (tiles, turned) if image == 0 else (turned, tiles)
        inbox = jnp.concatenate(
            [jnp.where(lane_side == 0, low[head], high[head + 1]) for head in range(0, HEADS, 2)], axis=1
        )
        asked = (everyone[...] == first_image + image).astype(F32)
        degree = jnp.sum(asked, axis=1, keepdims=True)
        averaged.append((inbox / (2.0 + degree)).astype(BF16))
    averaged = jnp.concatenate(averaged, axis=0)
    projected = jnp.dot(averaged, out_proj[...], preferred_element_type=F32).astype(BF16)
    source = features[...].reshape(together * row_count, width)
    hidden = (
        jnp.dot(source.astype(BF16), ffn_in[:width], preferred_element_type=F32)
        + jnp.dot(projected, ffn_in[width:], preferred_element_type=F32)
        + ffn_in_bias[...]
    )
    hidden = hidden - jnp.mean(hidden, axis=1, keepdims=True)
    spread = jnp.mean(hidden * hidden, axis=1, keepdims=True)
    normed = hidden * lax.rsqrt(spread + 1e-05) * norm_gain[...] + norm_bias[...]
    activated = (0.5 * normed * (1.0 + lax.erf(normed * (0.5**0.5)))).astype(BF16)
    refined = source + jnp.dot(activated, ffn_out[...], preferred_element_type=F32) + ffn_out_bias[...]
    out[...] = refined.reshape(together, row_count, width)


def per_device(features, partners, counts, shared_proj, value_proj, out_proj, ffn_in, ffn_in_bias,
               norm_gain, norm_bias, ffn_out, ffn_out_bias):
    img_count = lax.axis_size("img")
    row_devices = lax.axis_size("row")
    per_dev, row_count, width = features.shape
    head_dim = width // HEADS
    blocks = range(img_count)
    swap = [(s, s ^ 1) for s in blocks]
    thick_pairs = [(s, (s + (2 if s % 2 else -2)) % img_count) for s in blocks]
    thin_pairs = [(s, (s + (-2 if s % 2 else 2)) % img_count) for s in blocks]

    rounded, own = begin(features, shared_proj, value_proj)
    own = spread(own, row_devices)
    thick = lax.ppermute(rounded, "img", thick_pairs)
    thin = lax.ppermute(rounded, "img", thin_pairs)
    flat_partners = partners.reshape(-1)

    companion = lax.ppermute(own, "img", swap)
    todo = make_plan(counts, flat_partners, per_dev)
    thick = spread(project(thick, shared_proj, value_proj, todo), row_devices)
    (sums,) = attend(0, per_dev, head_dim, todo, own, [companion], None)
    thick = tie(thick, sums)
    cross = lax.ppermute(thick, "img", swap)
    thin = spread(project(thin, shared_proj, value_proj, sums), row_devices)
    (sums,) = attend(1, per_dev, head_dim, todo, own, [thick, cross], sums)
    messages = attend(2, per_dev, head_dim, todo, own, [thin], sums)
    shift = row_devices // HEADS
    messages = [
        lax.ppermute(message, "row", [(s, s ^ (number * shift)) for s in range(row_devices)]) if number else message
        for number, message in enumerate(messages)
    ]

    pair = pl.BlockSpec((2, row_count, width), lambda i: (i, 0, 0))
    return pl.pallas_call(
        functools.partial(refine_kernel, head_dim, shift),
        grid=(per_dev // 2,),
        out_shape=jax.ShapeDtypeStruct(features.shape, F32),
        in_specs=[
            whole(), pair, *[pl.BlockSpec((1, row_count, 2 * head_dim), lambda i: (i, 0, 0))] * HEADS,
        ] + [whole()] * 7,
        out_specs=pair,
        scratch_shapes=[pltpu.VMEM((HEADS, row_count, 2 * head_dim), F32)],
        compiler_params=pltpu.CompilerParams(vmem_limit_bytes=VMEM // 3),
        cost_estimate=pl.CostEstimate(
            flops=10 * per_dev * row_count * width * width * 2, bytes_accessed=2**22, transcendentals=2**20
        ),
        name="refine",
    )(flat_partners[None], features, *messages, out_proj, ffn_in, ffn_in_bias[None], norm_gain[None],
      norm_bias[None], ffn_out, ffn_out_bias[None])


def solution(mesh):
    return jax.shard_map(
        per_device,
        mesh=mesh,
        in_specs=(P("img", "row", None), P(), P(), P(), P(), P(), P(), P(), P(), P(), P(), P()),
        out_specs=P("img", "row", None),
        check_vma=False,
    )
```

```python
import functools
import math

import jax
import jax.numpy as jnp
from jax import lax
from jax.experimental import pallas as pl
from jax.experimental.pallas import tpu as pltpu
from jax.sharding import PartitionSpec as P

HEADS = 4
LEAST, MOST = 1e-25, 1e25
NEGATIVE = -1e30
VMEM = 60 * 2**20
NT = (((1,), (1,)), ((), ()))
F32 = jnp.float32
BF16 = jnp.bfloat16

COMPANION, THICK, THIN, CROSS = range(4)


def block_of(kind, me, img_count):
    odd = lax.rem(me, 2)
    ahead = 1 - 2 * odd
    step = {COMPANION: ahead, THICK: 2 * ahead, THIN: -2 * ahead, CROSS: -ahead}[kind]
    return lax.rem(me + step + img_count, img_count)


def whole(memory=pltpu.VMEM):
    return pl.BlockSpec(memory_space=memory)


def exchange(value):
    return lax.all_to_all(value, "row", split_axis=0, concat_axis=0, tiled=True)


CALLS = ((COMPANION,), (THICK, CROSS), (THIN,))


def plan_slots(per_dev):
    return max(len(kinds) for kinds in CALLS) * per_dev * per_dev + 1


def plan(counts, partners, todo):
    img_count = lax.axis_size("img")
    me = lax.axis_index("img")
    per_dev = counts.shape[0] // img_count
    slots = plan_slots(per_dev)
    for call, kinds in enumerate(CALLS):
        pairs = jnp.zeros((), jnp.int32)
        start = 4 * call * slots
        for place, kind in enumerate(kinds):
            block_id = block_of(kind, me, img_count)
            for other in range(per_dev):
                for image in range(per_dev):
                    theirs, mine = block_id * per_dev + other, me * per_dev + image
                    times = jnp.zeros((), jnp.int32)
                    for side in range(2):
                        times += (partners[2 * mine + side] == theirs).astype(jnp.int32)
                        times += (partners[2 * theirs + side] == mine).astype(jnp.int32)
                    todo[start + pairs] = place * per_dev + other
                    todo[start + slots + pairs] = image
                    todo[start + 2 * slots + pairs] = times
                    todo[start + 3 * slots + pairs] = counts[theirs]
                    pairs = pairs + (times > 0).astype(jnp.int32)
        todo[4 * len(CALLS) * slots + call] = pairs


def joined_weights(shared_proj, value_proj, lanes):
    both = []
    for start in range(0, shared_proj.shape[1], lanes):
        columns = slice(start, start + lanes)
        turned = pltpu.roll(value_proj[:, columns].astype(F32), lanes // 2, 1).astype(BF16)
        both.append(jnp.concatenate([shared_proj[:, columns], turned], axis=1))
    return both


def pack(head_dim, value, both, out, piece):
    lanes = 2 * head_dim
    low = lax.broadcasted_iota(jnp.int32, (1, lanes), 1) < head_dim
    for pair, weight in enumerate(both):
        projected = jnp.dot(value, weight, preferred_element_type=F32)
        shared, values = projected[:, :lanes], projected[:, lanes:]
        out[2 * pair, piece] = jnp.where(low, shared, values).astype(BF16)
        out[2 * pair + 1, piece] = jnp.where(low, values, shared).astype(BF16)


def project_kernel(head_dim, rows, shared_proj, value_proj, after, out):
    both = joined_weights(shared_proj, value_proj, 2 * head_dim)
    pack(head_dim, rows[...], both, out, slice(None))


def open_kernel(head_dim, per_dev, source, shared_hbm, value_hbm, rounded_hbm, out_hbm, rows, shared_proj,
                value_proj, packed, came, went, rounded):
    heads, flat_rows, lanes = packed.shape
    row_count = flat_rows // per_dev
    arrivals = [
        pltpu.make_async_copy(shared_hbm, shared_proj, came.at[per_dev]),
        pltpu.make_async_copy(value_hbm, value_proj, came.at[per_dev + 1]),
    ]
    pieces = [slice(image * row_count, (image + 1) * row_count) for image in range(per_dev)]
    loads = [
        pltpu.make_async_copy(source.at[piece], rows.at[piece], came.at[image])
        for image, piece in enumerate(pieces)
    ]
    for copy in arrivals + loads:
        copy.start()
    for copy in arrivals:
        copy.wait()
    both = joined_weights(shared_proj, value_proj, lanes)
    leaving = []
    for image, piece in enumerate(pieces):
        loads[image].wait()
        value = rows[piece].astype(BF16)
        rounded[piece] = value
        leaving.append(pltpu.make_async_copy(rounded.at[piece], rounded_hbm.at[piece], went.at[1, image]))
        leaving[-1].start()
        pack(head_dim, value, both, packed, piece)
        leaving.append(pltpu.make_async_copy(packed.at[:, piece], out_hbm.at[:, piece], went.at[0, image]))
        leaving[-1].start()
    for copy in leaving:
        copy.wait()


def spread(packed, row_devices):
    if row_devices > HEADS:
        packed = jnp.repeat(packed, row_devices // HEADS, axis=0)
    return exchange(packed)


def project_cost(rows, width, weigh):
    return pl.CostEstimate(
        flops=weigh * 4 * rows * width * width, bytes_accessed=6 * rows * width, transcendentals=0
    )


def begin(features, shared_proj, value_proj):
    per_dev, row_count, width = features.shape
    rows = per_dev * row_count
    head_dim = width // HEADS
    packed_shape = (HEADS, rows, 2 * head_dim)
    rounded, packed = pl.pallas_call(
        functools.partial(open_kernel, head_dim, per_dev),
        out_shape=(jax.ShapeDtypeStruct((rows, width), BF16), jax.ShapeDtypeStruct(packed_shape, BF16)),
        in_specs=[whole(pl.ANY)] * 3,
        out_specs=(whole(pl.ANY),) * 2,
        scratch_shapes=[
            pltpu.VMEM((rows, width), F32),
            pltpu.VMEM(shared_proj.shape, BF16),
            pltpu.VMEM(value_proj.shape, BF16),
            pltpu.VMEM(packed_shape, BF16),
            pltpu.SemaphoreType.DMA((per_dev + 2,)),
            pltpu.SemaphoreType.DMA((2, per_dev)),
            pltpu.VMEM((rows, width), BF16),
        ],
        compiler_params=pltpu.CompilerParams(vmem_limit_bytes=VMEM),
        cost_estimate=project_cost(rows, width, 1),
        name="begin",
    )(features.reshape(rows, width), shared_proj, value_proj)
    return rounded.reshape(features.shape), packed


def project(value, shared_proj, value_proj, after):
    per_dev, row_count, width = value.shape
    rows = per_dev * row_count
    head_dim = width // HEADS
    waits = pltpu.SMEM if after.dtype == jnp.int32 else pl.ANY
    return pl.pallas_call(
        functools.partial(project_kernel, head_dim),
        out_shape=jax.ShapeDtypeStruct((HEADS, rows, 2 * head_dim), BF16),
        in_specs=[whole()] * 3 + [whole(waits)],
        out_specs=whole(),
        compiler_params=pltpu.CompilerParams(vmem_limit_bytes=VMEM // 4),
        cost_estimate=project_cost(rows, width, 50),
        name="project",
    )(value.reshape(rows, width), shared_proj, value_proj, after)


def make_plan(counts, partners, per_dev):
    length = 4 * len(CALLS) * plan_slots(per_dev) + len(CALLS)
    return pl.pallas_call(
        plan,
        out_shape=jax.ShapeDtypeStruct((length,), jnp.int32),
        in_specs=[whole(pltpu.SMEM)] * 2,
        out_specs=whole(pltpu.SMEM),
        name="plan",
    )(counts, partners)


def tie(value, after):
    def kernel(value_ref, after_ref, out_ref):
        pass

    return pl.pallas_call(
        kernel,
        out_shape=jax.ShapeDtypeStruct(value.shape, value.dtype),
        in_specs=[whole(pltpu.HBM)] * 2,
        out_specs=whole(pltpu.HBM),
        input_output_aliases={0: 0},
        name="tie",
    )(value, after)


def attend_kernel(call, first, last, head_dim, todo, own_hbm, *refs):
    kinds = CALLS[call]
    blocks_hbm, refs = refs[:len(kinds)], refs[len(kinds):]
    if not first:
        carried_hbm, refs = refs[0], refs[1:]
    outs = HEADS if last else 2 if first else 1
    outs_hbm, refs = refs[:outs], refs[outs:]
    own, blocks, total, limits, seen, arrived, left, *out = refs
    out = out[0] if last else None
    devices, flat_rows, lanes = own.shape
    halved, keypoints, _ = total.shape
    per_dev = 2 * halved
    row_count = flat_rows // per_dev
    slots = plan_slots(per_dev)
    once = max(min(512, keypoints), row_count)
    sources = once // row_count
    factor = head_dim ** (-0.5) * math.log2(math.e)

    def image_rows(image):
        return pl.ds(pl.multiple_of(image * row_count, row_count), row_count)

    def start_totals():
        if first:
            total[...] = jnp.zeros_like(total)
            return []
        copy = pltpu.make_async_copy(carried_hbm, total, left.at[halved * HEADS])
        copy.start()
        return [copy]

    def block_copy(source, place, other, spot):
        rows = image_rows(other)
        return pltpu.make_async_copy(source.at[:, rows], blocks.at[place, :, rows], arrived.at[devices + spot])

    copies = []
    for device in range(devices):
        copies.append(pltpu.make_async_copy(own_hbm.at[device], own.at[device], arrived.at[device]))
        copies[-1].start()
    for place, source in enumerate(blocks_hbm):
        for other in range(per_dev):
            block_copy(source, place, other, place * per_dev + other).start()
            if place + other == 0:
                copies += start_totals()
    seen[0] = 0

    def need(spots):
        def one(spot, carry):
            block_copy(blocks_hbm[0], 0, 0, spot).wait()
            return carry

        lax.fori_loop(seen[0], spots, one, 0)
        seen[0] = jnp.maximum(seen[0], spots)

    key_side = lax.rem(lax.div(lax.axis_index("row"), devices // HEADS), 2)
    lane_side = lax.broadcasted_iota(jnp.int32, (1, lanes), 1) // head_dim
    key_row = lax.broadcasted_iota(jnp.int32, (keypoints, 1), 0)
    key_lane = lax.broadcasted_iota(jnp.int32, (1, keypoints), 1)
    one, zero = jnp.ones((), BF16), jnp.zeros((), BF16)
    limits[...] = jnp.ones_like(limits)
    pairs = todo[4 * len(CALLS) * slots + call]
    for copy in copies:
        copy.wait()
    kept = []
    if first:
        for device in range(devices):
            scaled = own[device].astype(F32) * factor
            head = scaled.astype(BF16)
            rest = pltpu.roll(scaled - head.astype(F32), head_dim, 1).astype(BF16)
            own[device] = jnp.where(lane_side == key_side, head, rest)
            kept.append(pltpu.make_async_copy(own.at[device], outs_hbm[1].at[device], arrived.at[device]))
            kept[-1].start()

    def operands(number):
        spot, image, times, limit = [todo[(4 * call + field) * slots + number] for field in range(4)]
        place, other = lax.div(spot, per_dev), lax.rem(spot, per_dev)
        tile = blocks[place, :, image_rows(other), :].reshape(keypoints, lanes)
        is_key, present = lane_side == key_side, key_row < limit
        keys = jnp.where(present, jnp.where(is_key, tile, pltpu.roll(tile, head_dim, 1)), zero)
        values = jnp.where(present, jnp.where(is_key, one, tile), zero)
        return image, keys, values, limit, times.astype(F32)

    def score(image, start, keys):
        queries = own[start:start + sources, image_rows(image), :].reshape(once, lanes)
        return lax.dot_general(queries, keys, NT, preferred_element_type=F32)

    def add(image, start, got, times):
        rows = slice(start * row_count, start * row_count + once)
        side = lax.rem(image, 2)
        turned = pltpu.roll(got, head_dim, 1)
        stays = side != key_side
        above, below = jnp.where(stays, got, turned), jnp.where(stays, turned, got)
        share = pl.reciprocal(below, approx=True)
        share = share * (2.0 - below * share)
        total[lax.div(image, 2), rows] += jnp.where(lane_side == side, above * (share * times), 0.0)

    def fast(numbers):
        need(todo[4 * call * slots + numbers[-1]] + 1)
        work = [operands(number) for number in numbers]
        least, most = limits[0], limits[1]
        for start in range(0, devices, sources):
            results = []
            for image, keys, values, _, times in work:
                raised = jnp.exp2(score(image, start, keys)).astype(BF16)
                got = jnp.dot(raised, values, preferred_element_type=F32)
                by_row = got.reshape(once // 8, 8, lanes)
                least = jnp.minimum(least, jnp.min(by_row, axis=0))
                most = jnp.maximum(most, jnp.max(by_row, axis=0))
                results.append(got)
            for (image, _, _, _, times), got in zip(work, results):
                add(image, start, got, times)
        limits[0] = least
        limits[1] = most

    def slow(number, carry):
        image, keys, values, limit, times = operands(number)
        present = key_lane < limit
        for start in range(0, devices, sources):
            scores = score(image, start, keys)
            peak = jnp.max(jnp.where(present, scores, NEGATIVE), axis=1, keepdims=True)
            raised = jnp.where(present, jnp.exp2(scores - peak), 0.0).astype(BF16)
            add(image, start, jnp.dot(raised, values, preferred_element_type=F32), times)
        return carry

    def two(number, carry):
        fast([2 * number, 2 * number + 1])
        return carry

    lax.fori_loop(0, pairs // 2, two, 0)

    @pl.when(pairs % 2 == 1)
    def _():
        fast([pairs - 1])

    need(len(kinds) * per_dev)
    outside = (limits[0] < LEAST) | (limits[1] > MOST)
    outside = jnp.where((lane_side == key_side) & outside, 1.0, 0.0)

    @pl.when(jnp.max(outside) > 0.5)
    def _():
        for copy in start_totals():
            copy.wait()
        lax.fori_loop(0, pairs, slow, 0)

    gone = kept
    if last:
        shift = devices // HEADS
        for number, target in enumerate(outs_hbm):
            rows = image_rows(lax.axis_index("row") ^ (number * shift))
            for pair in range(halved):
                out[number, pair] = total[pair, rows].astype(BF16)
            gone.append(pltpu.make_async_copy(out.at[number], target, left.at[number]))
            gone[-1].start()
    else:
        for pair in range(halved):
            for number in range(HEADS):
                rows = slice(number * keypoints // HEADS, (number + 1) * keypoints // HEADS)
                place = left.at[pair * HEADS + number]
                gone.append(pltpu.make_async_copy(total.at[pair, rows], outs_hbm[0].at[pair, rows], place))
                gone[-1].start()
    for copy in gone:
        copy.wait()


def attend(call, per_dev, head_dim, todo, own, blocks, carried):
    devices, flat_rows, lanes = own.shape
    first, last = call == 0, call == len(CALLS) - 1
    halved = per_dev // 2
    row_count = flat_rows // (2 * halved)
    packed = (halved, devices * row_count, lanes)
    arguments = [todo, own, *blocks] + ([] if first else [carried])
    if last:
        out_shape = (jax.ShapeDtypeStruct((halved, row_count, lanes), BF16),) * HEADS
    else:
        out_shape = (jax.ShapeDtypeStruct(packed, F32),)
        if first:
            out_shape += (jax.ShapeDtypeStruct(own.shape, BF16),)
    scratch = [
        pltpu.VMEM(own.shape, BF16),
        pltpu.VMEM((len(blocks), *own.shape), BF16),
        pltpu.VMEM(packed, F32),
        pltpu.VMEM((2, 8, lanes), F32),
        pltpu.SMEM((1,), jnp.int32),
        pltpu.SemaphoreType.DMA((devices + len(blocks) * per_dev,)),
        pltpu.SemaphoreType.DMA((halved * HEADS + 1,)),
    ]
    if last:
        scratch.append(pltpu.VMEM((HEADS, halved, row_count, lanes), BF16))
    area = (devices * row_count) ** 2
    return pl.pallas_call(
        functools.partial(attend_kernel, call, first, last, head_dim),
        out_shape=out_shape,
        in_specs=[whole(pltpu.SMEM)] + [whole(pltpu.HBM)] * (len(arguments) - 1),
        out_specs=(whole(pltpu.HBM),) * len(out_shape),
        scratch_shapes=scratch,
        compiler_params=pltpu.CompilerParams(vmem_limit_bytes=VMEM),
        cost_estimate=pl.CostEstimate(
            flops=0 if first else len(blocks) * 4 * 2 * 2 * area * 512,
            bytes_accessed=0 if first else 4 * devices * flat_rows * lanes,
            transcendentals=0 if first else len(blocks) * 4 * area,
        ),
        name=f"attend{call}",
    )(*arguments)


def refine_kernel(head_dim, shift, everyone, features, *refs):
    messages, refs = refs[:HEADS], refs[HEADS:]
    out_proj, ffn_in, ffn_in_bias, norm_gain, norm_bias, ffn_out, ffn_out_bias, out, by_head = refs
    together, row_count, width = features.shape
    lanes = 2 * head_dim
    pair = pl.program_id(0)
    first_image = (lax.axis_index("img") * pl.num_programs(0) + pair) * together
    lane_side = lax.broadcasted_iota(jnp.int32, (1, lanes), 1) // head_dim
    for number, message in enumerate(messages):
        by_head[lax.div(lax.axis_index("row"), shift) ^ number] = message[0].astype(F32)
    tiles = [by_head[head] for head in range(HEADS)]
    turned = [pltpu.roll(tile, head_dim, 1) for tile in tiles]
    averaged = []
    for image in range(together):
        low, high = (tiles, turned) if image == 0 else (turned, tiles)
        inbox = jnp.concatenate(
            [jnp.where(lane_side == 0, low[head], high[head + 1]) for head in range(0, HEADS, 2)], axis=1
        )
        asked = (everyone[...] == first_image + image).astype(F32)
        degree = jnp.sum(asked, axis=1, keepdims=True)
        averaged.append((inbox / (2.0 + degree)).astype(BF16))
    averaged = jnp.concatenate(averaged, axis=0)
    projected = jnp.dot(averaged, out_proj[...], preferred_element_type=F32).astype(BF16)
    source = features[...].reshape(together * row_count, width)
    hidden = (
        jnp.dot(source.astype(BF16), ffn_in[:width], preferred_element_type=F32)
        + jnp.dot(projected, ffn_in[width:], preferred_element_type=F32)
        + ffn_in_bias[...]
    )
    hidden = hidden - jnp.mean(hidden, axis=1, keepdims=True)
    spread = jnp.mean(hidden * hidden, axis=1, keepdims=True)
    normed = hidden * lax.rsqrt(spread + 1e-05) * norm_gain[...] + norm_bias[...]
    activated = (0.5 * normed * (1.0 + lax.erf(normed * (0.5**0.5)))).astype(BF16)
    refined = source + jnp.dot(activated, ffn_out[...], preferred_element_type=F32) + ffn_out_bias[...]
    out[...] = refined.reshape(together, row_count, width)


def per_device(features, partners, counts, shared_proj, value_proj, out_proj, ffn_in, ffn_in_bias,
               norm_gain, norm_bias, ffn_out, ffn_out_bias):
    img_count = lax.axis_size("img")
    row_devices = lax.axis_size("row")
    per_dev, row_count, width = features.shape
    head_dim = width // HEADS
    blocks = range(img_count)
    swap = [(s, s ^ 1) for s in blocks]
    thick_pairs = [(s, (s + (2 if s % 2 else -2)) % img_count) for s in blocks]
    thin_pairs = [(s, (s + (-2 if s % 2 else 2)) % img_count) for s in blocks]

    rounded, own = begin(features, shared_proj, value_proj)
    own = spread(own, row_devices)
    thick = lax.ppermute(rounded, "img", thick_pairs)
    thin = lax.ppermute(rounded, "img", thin_pairs)
    flat_partners = partners.reshape(-1)

    companion = lax.ppermute(own, "img", swap)
    todo = make_plan(counts, flat_partners, per_dev)
    thick = spread(project(thick, shared_proj, value_proj, todo), row_devices)
    sums, own = attend(0, per_dev, head_dim, todo, own, [companion], None)
    thick = tie(thick, sums)
    cross = lax.ppermute(thick, "img", swap)
    thin = spread(project(thin, shared_proj, value_proj, sums), row_devices)
    (sums,) = attend(1, per_dev, head_dim, todo, own, [thick, cross], sums)
    messages = attend(2, per_dev, head_dim, todo, own, [thin], sums)
    shift = row_devices // HEADS
    messages = [
        lax.ppermute(message, "row", [(s, s ^ (number * shift)) for s in range(row_devices)]) if number else message
        for number, message in enumerate(messages)
    ]

    pair = pl.BlockSpec((2, row_count, width), lambda i: (i, 0, 0))
    return pl.pallas_call(
        functools.partial(refine_kernel, head_dim, shift),
        grid=(per_dev // 2,),
        out_shape=jax.ShapeDtypeStruct(features.shape, F32),
        in_specs=[
            whole(), pair, *[pl.BlockSpec((1, row_count, 2 * head_dim), lambda i: (i, 0, 0))] * HEADS,
        ] + [whole()] * 7,
        out_specs=pair,
        scratch_shapes=[pltpu.VMEM((HEADS, row_count, 2 * head_dim), F32)],
        compiler_params=pltpu.CompilerParams(vmem_limit_bytes=VMEM // 3),
        cost_estimate=pl.CostEstimate(
            flops=10 * per_dev * row_count * width * width * 2, bytes_accessed=2**22, transcendentals=2**20
        ),
        name="refine",
    )(flat_partners[None], features, *messages, out_proj, ffn_in, ffn_in_bias[None], norm_gain[None],
      norm_bias[None], ffn_out, ffn_out_bias[None])


def solution(mesh):
    return jax.shard_map(
        per_device,
        mesh=mesh,
        in_specs=(P("img", "row", None), P(), P(), P(), P(), P(), P(), P(), P(), P(), P(), P()),
        out_specs=P("img", "row", None),
        check_vma=False,
    )
```

```python
import functools
import math

import jax
import jax.numpy as jnp
from jax import lax
from jax.experimental import pallas as pl
from jax.experimental.pallas import tpu as pltpu
from jax.sharding import PartitionSpec as P

HEADS = 4
LEAST, MOST = 1e-25, 1e25
NEGATIVE = -1e30
VMEM = 60 * 2**20
NT = (((1,), (1,)), ((), ()))
F32 = jnp.float32
BF16 = jnp.bfloat16

COMPANION, THICK, THIN, CROSS = range(4)


def block_of(kind, me, img_count):
    odd = lax.rem(me, 2)
    ahead = 1 - 2 * odd
    step = {COMPANION: ahead, THICK: 2 * ahead, THIN: -2 * ahead, CROSS: -ahead}[kind]
    return lax.rem(me + step + img_count, img_count)


def whole(memory=pltpu.VMEM):
    return pl.BlockSpec(memory_space=memory)


def exchange(value):
    return lax.all_to_all(value, "row", split_axis=0, concat_axis=0, tiled=True)


CALLS = ((COMPANION,), (THICK, CROSS), (THIN,))


def plan_slots(per_dev):
    return max(len(kinds) for kinds in CALLS) * per_dev * per_dev + 1


def plan(counts, partners, todo):
    img_count = lax.axis_size("img")
    me = lax.axis_index("img")
    per_dev = counts.shape[0] // img_count
    slots = plan_slots(per_dev)
    for call, kinds in enumerate(CALLS):
        pairs = jnp.zeros((), jnp.int32)
        start = 4 * call * slots
        for place, kind in enumerate(kinds):
            block_id = block_of(kind, me, img_count)
            for other in range(per_dev):
                for image in range(per_dev):
                    theirs, mine = block_id * per_dev + other, me * per_dev + image
                    times = jnp.zeros((), jnp.int32)
                    for side in range(2):
                        times += (partners[2 * mine + side] == theirs).astype(jnp.int32)
                        times += (partners[2 * theirs + side] == mine).astype(jnp.int32)
                    todo[start + pairs] = place * per_dev + other
                    todo[start + slots + pairs] = image
                    todo[start + 2 * slots + pairs] = times
                    todo[start + 3 * slots + pairs] = counts[theirs]
                    pairs = pairs + (times > 0).astype(jnp.int32)
        todo[4 * len(CALLS) * slots + call] = pairs


def joined_weights(shared_proj, value_proj, lanes):
    both = []
    for start in range(0, shared_proj.shape[1], lanes):
        columns = slice(start, start + lanes)
        turned = pltpu.roll(value_proj[:, columns].astype(F32), lanes // 2, 1).astype(BF16)
        both.append(jnp.concatenate([shared_proj[:, columns], turned], axis=1))
    return both


def pack(head_dim, value, both, out, piece):
    lanes = 2 * head_dim
    low = lax.broadcasted_iota(jnp.int32, (1, lanes), 1) < head_dim
    for pair, weight in enumerate(both):
        projected = jnp.dot(value, weight, preferred_element_type=F32)
        shared, values = projected[:, :lanes], projected[:, lanes:]
        out[2 * pair, piece] = jnp.where(low, shared, values).astype(BF16)
        out[2 * pair + 1, piece] = jnp.where(low, values, shared).astype(BF16)


def project_kernel(head_dim, rows, shared_proj, value_proj, after, out):
    both = joined_weights(shared_proj, value_proj, 2 * head_dim)
    pack(head_dim, rows[...], both, out, slice(None))


def open_kernel(head_dim, per_dev, source, shared_hbm, value_hbm, rounded_hbm, out_hbm, rows, shared_proj,
                value_proj, packed, came, went, rounded):
    heads, flat_rows, lanes = packed.shape
    row_count = flat_rows // per_dev
    arrivals = [
        pltpu.make_async_copy(shared_hbm, shared_proj, came.at[per_dev]),
        pltpu.make_async_copy(value_hbm, value_proj, came.at[per_dev + 1]),
    ]
    pieces = [slice(image * row_count, (image + 1) * row_count) for image in range(per_dev)]
    loads = [
        pltpu.make_async_copy(source.at[piece], rows.at[piece], came.at[image])
        for image, piece in enumerate(pieces)
    ]
    for copy in arrivals + loads:
        copy.start()
    for copy in arrivals:
        copy.wait()
    both = joined_weights(shared_proj, value_proj, lanes)
    leaving = []
    for image, piece in enumerate(pieces):
        loads[image].wait()
        value = rows[piece].astype(BF16)
        rounded[piece] = value
        leaving.append(pltpu.make_async_copy(rounded.at[piece], rounded_hbm.at[piece], went.at[1, image]))
        leaving[-1].start()
        pack(head_dim, value, both, packed, piece)
        leaving.append(pltpu.make_async_copy(packed.at[:, piece], out_hbm.at[:, piece], went.at[0, image]))
        leaving[-1].start()
    for copy in leaving:
        copy.wait()


def spread(packed, row_devices):
    if row_devices > HEADS:
        packed = jnp.repeat(packed, row_devices // HEADS, axis=0)
    return exchange(packed)


def project_cost(rows, width, weigh):
    return pl.CostEstimate(
        flops=weigh * 4 * rows * width * width, bytes_accessed=6 * rows * width, transcendentals=0
    )


def begin(features, shared_proj, value_proj):
    per_dev, row_count, width = features.shape
    rows = per_dev * row_count
    head_dim = width // HEADS
    packed_shape = (HEADS, rows, 2 * head_dim)
    rounded, packed = pl.pallas_call(
        functools.partial(open_kernel, head_dim, per_dev),
        out_shape=(jax.ShapeDtypeStruct((rows, width), BF16), jax.ShapeDtypeStruct(packed_shape, BF16)),
        in_specs=[whole(pl.ANY)] * 3,
        out_specs=(whole(pl.ANY),) * 2,
        scratch_shapes=[
            pltpu.VMEM((rows, width), F32),
            pltpu.VMEM(shared_proj.shape, BF16),
            pltpu.VMEM(value_proj.shape, BF16),
            pltpu.VMEM(packed_shape, BF16),
            pltpu.SemaphoreType.DMA((per_dev + 2,)),
            pltpu.SemaphoreType.DMA((2, per_dev)),
            pltpu.VMEM((rows, width), BF16),
        ],
        compiler_params=pltpu.CompilerParams(vmem_limit_bytes=VMEM),
        cost_estimate=project_cost(rows, width, 1),
        name="begin",
    )(features.reshape(rows, width), shared_proj, value_proj)
    return rounded.reshape(features.shape), packed


def project(value, shared_proj, value_proj, after):
    per_dev, row_count, width = value.shape
    rows = per_dev * row_count
    head_dim = width // HEADS
    waits = pltpu.SMEM if after.dtype == jnp.int32 else pl.ANY
    return pl.pallas_call(
        functools.partial(project_kernel, head_dim),
        out_shape=jax.ShapeDtypeStruct((HEADS, rows, 2 * head_dim), BF16),
        in_specs=[whole()] * 3 + [whole(waits)],
        out_specs=whole(),
        compiler_params=pltpu.CompilerParams(vmem_limit_bytes=VMEM // 4),
        cost_estimate=project_cost(rows, width, 50),
        name="project",
    )(value.reshape(rows, width), shared_proj, value_proj, after)


def make_plan(counts, partners, per_dev):
    length = 4 * len(CALLS) * plan_slots(per_dev) + len(CALLS)
    return pl.pallas_call(
        plan,
        out_shape=jax.ShapeDtypeStruct((length,), jnp.int32),
        in_specs=[whole(pltpu.SMEM)] * 2,
        out_specs=whole(pltpu.SMEM),
        name="plan",
    )(counts, partners)


def tie(value, after):
    def kernel(value_ref, after_ref, out_ref):
        pass

    return pl.pallas_call(
        kernel,
        out_shape=jax.ShapeDtypeStruct(value.shape, value.dtype),
        in_specs=[whole(pltpu.HBM)] * 2,
        out_specs=whole(pltpu.HBM),
        input_output_aliases={0: 0},
        name="tie",
    )(value, after)


def attend_kernel(call, first, last, head_dim, todo, own_hbm, *refs):
    kinds = CALLS[call]
    blocks_hbm, refs = refs[:len(kinds)], refs[len(kinds):]
    if not first:
        carried_hbm, refs = refs[0], refs[1:]
    outs_hbm, refs = refs[:HEADS if last else 1], refs[HEADS if last else 1:]
    own, blocks, total, limits, seen, arrived, left, *out = refs
    out = out[0] if last else None
    devices, flat_rows, lanes = own.shape
    halved, keypoints, _ = total.shape
    per_dev = 2 * halved
    row_count = flat_rows // per_dev
    slots = plan_slots(per_dev)
    once = max(min(1024, keypoints), row_count)
    sources = once // row_count
    factor = head_dim ** (-0.5) * math.log2(math.e)

    def image_rows(image):
        return pl.ds(pl.multiple_of(image * row_count, row_count), row_count)

    def start_totals():
        if first:
            total[...] = jnp.zeros_like(total)
            return []
        copy = pltpu.make_async_copy(carried_hbm, total, left.at[halved * HEADS])
        copy.start()
        return [copy]

    def block_copy(source, place, other, spot):
        rows = image_rows(other)
        return pltpu.make_async_copy(source.at[:, rows], blocks.at[place, :, rows], arrived.at[devices + spot])

    copies = []
    for device in range(devices):
        copies.append(pltpu.make_async_copy(own_hbm.at[device], own.at[device], arrived.at[device]))
        copies[-1].start()
    for place, source in enumerate(blocks_hbm):
        for other in range(per_dev):
            block_copy(source, place, other, place * per_dev + other).start()
            if place + other == 0:
                copies += start_totals()
    seen[0] = 0

    def need(spots):
        def one(spot, carry):
            block_copy(blocks_hbm[0], 0, 0, spot).wait()
            return carry

        lax.fori_loop(seen[0], spots, one, 0)
        seen[0] = jnp.maximum(seen[0], spots)

    key_side = lax.rem(lax.div(lax.axis_index("row"), devices // HEADS), 2)
    lane_side = lax.broadcasted_iota(jnp.int32, (1, lanes), 1) // head_dim
    key_row = lax.broadcasted_iota(jnp.int32, (keypoints, 1), 0)
    key_lane = lax.broadcasted_iota(jnp.int32, (1, keypoints), 1)
    one, zero = jnp.ones((), BF16), jnp.zeros((), BF16)
    limits[...] = jnp.ones_like(limits)
    pairs = todo[4 * len(CALLS) * slots + call]
    for copy in copies:
        copy.wait()

    def operands(number):
        spot, image, times, limit = [todo[(4 * call + field) * slots + number] for field in range(4)]
        place, other = lax.div(spot, per_dev), lax.rem(spot, per_dev)
        tile = blocks[place, :, image_rows(other), :].reshape(keypoints, lanes)
        is_key, present = lane_side == key_side, key_row < limit
        keys = jnp.where(present, jnp.where(is_key, tile, zero), zero)
        values = jnp.where(present, jnp.where(is_key, one, tile), zero)
        return image, keys, values, limit, times.astype(F32)

    def score(image, start, keys):
        queries = own[start:start + sources, image_rows(image), :].reshape(once, lanes)
        return lax.dot_general(queries, keys, NT, preferred_element_type=F32)

    def add(image, start, got, times):
        rows = slice(start * row_count, start * row_count + once)
        side = lax.rem(image, 2)
        turned = pltpu.roll(got, head_dim, 1)
        stays = side != key_side
        above, below = jnp.where(stays, got, turned), jnp.where(stays, turned, got)
        share = pl.reciprocal(below, approx=True)
        share = share * (2.0 - below * share)
        total[lax.div(image, 2), rows] += jnp.where(lane_side == side, above * (share * times), 0.0)

    def fast(numbers):
        need(todo[4 * call * slots + numbers[-1]] + 1)
        work = [operands(number) for number in numbers]
        least, most = limits[0], limits[1]
        for start in range(0, devices, sources):
            results = []
            for image, keys, values, _, times in work:
                raised = jnp.exp2(score(image, start, keys) * factor).astype(BF16)
                got = jnp.dot(raised, values, preferred_element_type=F32)
                by_row = got.reshape(once // 8, 8, lanes)
                least = jnp.minimum(least, jnp.min(by_row, axis=0))
                most = jnp.maximum(most, jnp.max(by_row, axis=0))
                results.append(got)
            for (image, _, _, _, times), got in zip(work, results):
                add(image, start, got, times)
        limits[0] = least
        limits[1] = most

    def slow(number, carry):
        image, keys, values, limit, times = operands(number)
        present = key_lane < limit
        for start in range(0, devices, sources):
            scores = score(image, start, keys)
            peak = jnp.max(jnp.where(present, scores, NEGATIVE), axis=1, keepdims=True)
            raised = jnp.where(present, jnp.exp2((scores - peak) * factor), 0.0).astype(BF16)
            add(image, start, jnp.dot(raised, values, preferred_element_type=F32), times)
        return carry

    def two(number, carry):
        fast([2 * number, 2 * number + 1])
        return carry

    lax.fori_loop(0, pairs // 2, two, 0)

    @pl.when(pairs % 2 == 1)
    def _():
        fast([pairs - 1])

    need(len(kinds) * per_dev)
    outside = (limits[0] < LEAST) | (limits[1] > MOST)
    outside = jnp.where((lane_side == key_side) & outside, 1.0, 0.0)

    @pl.when(jnp.max(outside) > 0.5)
    def _():
        for copy in start_totals():
            copy.wait()
        lax.fori_loop(0, pairs, slow, 0)

    gone = []
    if last:
        shift = devices // HEADS
        for number, target in enumerate(outs_hbm):
            rows = image_rows(lax.axis_index("row") ^ (number * shift))
            for pair in range(halved):
                out[number, pair] = total[pair, rows].astype(BF16)
            gone.append(pltpu.make_async_copy(out.at[number], target, left.at[number]))
            gone[-1].start()
    else:
        for pair in range(halved):
            for number in range(HEADS):
                rows = slice(number * keypoints // HEADS, (number + 1) * keypoints // HEADS)
                place = left.at[pair * HEADS + number]
                gone.append(pltpu.make_async_copy(total.at[pair, rows], outs_hbm[0].at[pair, rows], place))
                gone[-1].start()
    for copy in gone:
        copy.wait()


def attend(call, per_dev, head_dim, todo, own, blocks, carried):
    devices, flat_rows, lanes = own.shape
    first, last = call == 0, call == len(CALLS) - 1
    halved = per_dev // 2
    row_count = flat_rows // (2 * halved)
    packed = (halved, devices * row_count, lanes)
    arguments = [todo, own, *blocks] + ([] if first else [carried])
    if last:
        out_shape = (jax.ShapeDtypeStruct((halved, row_count, lanes), BF16),) * HEADS
    else:
        out_shape = (jax.ShapeDtypeStruct(packed, F32),)
    scratch = [
        pltpu.VMEM(own.shape, BF16),
        pltpu.VMEM((len(blocks), *own.shape), BF16),
        pltpu.VMEM(packed, F32),
        pltpu.VMEM((2, 8, lanes), F32),
        pltpu.SMEM((1,), jnp.int32),
        pltpu.SemaphoreType.DMA((devices + len(blocks) * per_dev,)),
        pltpu.SemaphoreType.DMA((halved * HEADS + 1,)),
    ]
    if last:
        scratch.append(pltpu.VMEM((HEADS, halved, row_count, lanes), BF16))
    area = (devices * row_count) ** 2
    return pl.pallas_call(
        functools.partial(attend_kernel, call, first, last, head_dim),
        out_shape=out_shape,
        in_specs=[whole(pltpu.SMEM)] + [whole(pltpu.HBM)] * (len(arguments) - 1),
        out_specs=(whole(pltpu.HBM),) * len(out_shape),
        scratch_shapes=scratch,
        compiler_params=pltpu.CompilerParams(vmem_limit_bytes=VMEM),
        cost_estimate=pl.CostEstimate(
            flops=0 if first else len(blocks) * 4 * 2 * 2 * area * 512,
            bytes_accessed=0 if first else 4 * devices * flat_rows * lanes,
            transcendentals=0 if first else len(blocks) * 4 * area,
        ),
        name=f"attend{call}",
    )(*arguments)


def refine_kernel(head_dim, shift, everyone, features, *refs):
    messages, refs = refs[:HEADS], refs[HEADS:]
    out_proj, ffn_in, ffn_in_bias, norm_gain, norm_bias, ffn_out, ffn_out_bias, out, by_head = refs
    together, row_count, width = features.shape
    lanes = 2 * head_dim
    pair = pl.program_id(0)
    first_image = (lax.axis_index("img") * pl.num_programs(0) + pair) * together
    lane_side = lax.broadcasted_iota(jnp.int32, (1, lanes), 1) // head_dim
    for number, message in enumerate(messages):
        by_head[lax.div(lax.axis_index("row"), shift) ^ number] = message[0].astype(F32)
    tiles = [by_head[head] for head in range(HEADS)]
    turned = [pltpu.roll(tile, head_dim, 1) for tile in tiles]
    averaged = []
    for image in range(together):
        low, high = (tiles, turned) if image == 0 else (turned, tiles)
        inbox = jnp.concatenate(
            [jnp.where(lane_side == 0, low[head], high[head + 1]) for head in range(0, HEADS, 2)], axis=1
        )
        asked = (everyone[...] == first_image + image).astype(F32)
        degree = jnp.sum(asked, axis=1, keepdims=True)
        averaged.append((inbox / (2.0 + degree)).astype(BF16))
    averaged = jnp.concatenate(averaged, axis=0)
    projected = jnp.dot(averaged, out_proj[...], preferred_element_type=F32).astype(BF16)
    source = features[...].reshape(together * row_count, width)
    hidden = (
        jnp.dot(source.astype(BF16), ffn_in[:width], preferred_element_type=F32)
        + jnp.dot(projected, ffn_in[width:], preferred_element_type=F32)
        + ffn_in_bias[...]
    )
    hidden = hidden - jnp.mean(hidden, axis=1, keepdims=True)
    spread = jnp.mean(hidden * hidden, axis=1, keepdims=True)
    normed = hidden * lax.rsqrt(spread + 1e-05) * norm_gain[...] + norm_bias[...]
    activated = (0.5 * normed * (1.0 + lax.erf(normed * (0.5**0.5)))).astype(BF16)
    refined = source + jnp.dot(activated, ffn_out[...], preferred_element_type=F32) + ffn_out_bias[...]
    out[...] = refined.reshape(together, row_count, width)


def per_device(features, partners, counts, shared_proj, value_proj, out_proj, ffn_in, ffn_in_bias,
               norm_gain, norm_bias, ffn_out, ffn_out_bias):
    img_count = lax.axis_size("img")
    row_devices = lax.axis_size("row")
    per_dev, row_count, width = features.shape
    head_dim = width // HEADS
    blocks = range(img_count)
    swap = [(s, s ^ 1) for s in blocks]
    thick_pairs = [(s, (s + (2 if s % 2 else -2)) % img_count) for s in blocks]
    thin_pairs = [(s, (s + (-2 if s % 2 else 2)) % img_count) for s in blocks]

    rounded, own = begin(features, shared_proj, value_proj)
    own = spread(own, row_devices)
    thick = lax.ppermute(rounded, "img", thick_pairs)
    thin = lax.ppermute(rounded, "img", thin_pairs)
    flat_partners = partners.reshape(-1)

    companion = lax.ppermute(own, "img", swap)
    todo = make_plan(counts, flat_partners, per_dev)
    thick = spread(project(thick, shared_proj, value_proj, todo), row_devices)
    (sums,) = attend(0, per_dev, head_dim, todo, own, [companion], None)
    thick = tie(thick, sums)
    cross = lax.ppermute(thick, "img", swap)
    thin = spread(project(thin, shared_proj, value_proj, sums), row_devices)
    (sums,) = attend(1, per_dev, head_dim, todo, own, [thick, cross], sums)
    messages = attend(2, per_dev, head_dim, todo, own, [thin], sums)
    shift = row_devices // HEADS
    messages = [
        lax.ppermute(message, "row", [(s, s ^ (number * shift)) for s in range(row_devices)]) if number else message
        for number, message in enumerate(messages)
    ]

    pair = pl.BlockSpec((2, row_count, width), lambda i: (i, 0, 0))
    return pl.pallas_call(
        functools.partial(refine_kernel, head_dim, shift),
        grid=(per_dev // 2,),
        out_shape=jax.ShapeDtypeStruct(features.shape, F32),
        in_specs=[
            whole(), pair, *[pl.BlockSpec((1, row_count, 2 * head_dim), lambda i: (i, 0, 0))] * HEADS,
        ] + [whole()] * 7,
        out_specs=pair,
        scratch_shapes=[pltpu.VMEM((HEADS, row_count, 2 * head_dim), F32)],
        compiler_params=pltpu.CompilerParams(vmem_limit_bytes=VMEM // 3),
        cost_estimate=pl.CostEstimate(
            flops=10 * per_dev * row_count * width * width * 2, bytes_accessed=2**22, transcendentals=2**20
        ),
        name="refine",
    )(flat_partners[None], features, *messages, out_proj, ffn_in, ffn_in_bias[None], norm_gain[None],
      norm_bias[None], ffn_out, ffn_out_bias[None])


def solution(mesh):
    return jax.shard_map(
        per_device,
        mesh=mesh,
        in_specs=(P("img", "row", None), P(), P(), P(), P(), P(), P(), P(), P(), P(), P(), P()),
        out_specs=P("img", "row", None),
        check_vma=False,
    )
```
